32 devices in a mesh: groups: 1, dp: 2 (over core), expert: 16 (over z, y, x).
Axes of the slice: x: 2, y: 2, z: 4, core: 2. Of those that a mesh axis runs over, the one named last changes fastest.
Arguments:
- tokens: bfloat16 [512, 2048], P(('groups', 'dp', 'expert')), may hold values from -6 to 6
- cotangent: bfloat16 [512, 2048], P(('groups', 'dp', 'expert')), may hold values from -12 to 12
- gate_values: bfloat16 [512, 8], P(('groups', 'dp', 'expert')), may hold values from 0.049804688 to 0.29882812
- expert_ids: int32 [512, 8], P(('groups', 'dp', 'expert')), may hold values from 0 to 15, all different within a row; in each aligned block of 16 rows (0 to 15, 16 to 31, ...) at most 9 rows name the same one
- packing: int32 [512], P(('groups', 'dp', 'expert')), may hold values from -1 to 31, as said below
- w_gate: bfloat16 [16, 384, 2048], P('expert', 'dp'), may hold values from -0.125 to 0.125
- w_up: bfloat16 [16, 384, 2048], P('expert', 'dp'), may hold values from -0.125 to 0.125
- w_down: bfloat16 [16, 384, 2048], P('expert', 'dp'), may hold values from -0.3125 to 0.3125
Outputs:
- input_grad: bfloat16 [512, 2048], P(('groups', 'dp', 'expert'))
- grad_gate: bfloat16 [16, 384, 2048], P(('groups', 'expert'), 'dp')
- grad_up: bfloat16 [16, 384, 2048], P(('groups', 'expert'), 'dp')
- grad_down: bfloat16 [16, 384, 2048], P(('groups', 'expert'), 'dp')
The draws below stay inside these ranges and needn't reach their ends.
Inputs may be any that keep to these rules, and one draw needn't show every extreme that they name: `packing`: slot value q names home row q % 16 of the dp device q // 16 with the same expert index; -1 marks an empty slot. Home rows come in groups of 8 completions that are kept or filtered together; over the devices sharing an expert index, every kept row is named exactly once and filtered rows never; the i-th kept row, in home order, goes to slot i // 2 of dp device i % 2, so empty slots come last on each device. `expert_ids`: in the 16 rows of one device, no expert is named by more than 9 rows, a bound that some block reaches.
All inputs are finite; a program needn't handle non-finite values.
Results may differ from the reference program's by a relative error of at most 0.0072.
Values may be sent and summed in bfloat16 or wider, within the bound.
No kernel may reach another device: no remote copies, remote signals or barrier semaphores. Data moves between devices by JAX's collectives and lax.ppermute only.
A program may use at most 64 MiB of HBM per device.

```python
import math
import jax
import jax.numpy as jnp
import numpy as np
from jax import lax

D = 2048
TOP = 8
FF = 384
ROWS_DEV = 16
GROUP_ROWS = 8
EXPERTS = 16
CAP = 9
PAIR_ROWS = 32
ROWS = 512
N_DP = 2
N_EXPERT = 16


def draw_packing(key, part):
    key = jax.random.fold_in(key, 7)
    members = PAIR_ROWS // ROWS_DEV
    groups = PAIR_ROWS // GROUP_ROWS
    retained = jax.random.randint(key, (EXPERTS, groups), 0, 8) > 0
    group_index = jnp.arange(groups)
    retained = jnp.where(group_index[None, :] == 0, False, retained)
    retained = jnp.where(group_index[None, :] == groups - 1, True, retained)
    row_kept = jnp.repeat(retained, GROUP_ROWS, axis=1)
    kept_count = row_kept.astype(jnp.int32)
    kept_rank = jnp.cumsum(kept_count, axis=1) - 1
    target = kept_rank % members * ROWS_DEV + kept_rank // members
    places = jnp.arange(PAIR_ROWS, dtype=jnp.int32)
    matched = row_kept[:, None, :] & (target[:, None, :] == places[None, :, None])
    source = jnp.sum(jnp.where(matched, places[None, None, :] + 1, 0), axis=2) - 1
    layout = source.reshape(EXPERTS, members, ROWS_DEV).transpose(1, 0, 2)
    return layout.reshape(-1).astype(jnp.int32)


def shard_levels(rng, dims, cuts, least, high):
    def one(dim, parts):
        heights = jax.random.uniform(jax.random.fold_in(jax.random.fold_in(rng, 6), dim), (parts,), jnp.float32, least / len(cuts), high / len(cuts))
        return jnp.repeat(jnp.exp(heights), dims[dim] // parts).reshape((-1,) + (1,) * (len(dims) - dim - 1))

    factor_of = one(*cuts[0])
    for cut in cuts[1:]:
        factor_of = factor_of * one(*cut)
    return factor_of


def assign_block(key, own, number, rows, count, top, reach, slope):
    ranking = jax.random.permutation(key, count)
    packed, common = shares(count, rows * top, reach, slope, True), shares(count, rows * top, reach, slope, False)
    places = jnp.arange(count)

    def named(tallies, turn):
        used = int((tallies > 0).sum())
        fixed = max(1, used // 4)
        passed = fixed + (places - fixed + turn * (used - fixed)) % max(1, count - fixed)
        return jnp.zeros((count,), jnp.int32).at[ranking[jnp.where(places < fixed, places, passed)]].set(jnp.asarray(tallies, jnp.int32))

    tallies = jnp.where(number % 4 == 0, named(packed, number // 4), named(common, number - number // 4 - 1))
    mixed = jax.random.permutation(jax.random.fold_in(own, 3), count)
    source_of, sink = mixed[0:count // 2 * 2:2], mixed[1:count // 2 * 2:2]
    slack = jnp.minimum(tallies[source_of] - 1, reach - tallies[sink]) // 2
    slack = jnp.where((source_of == ranking[0]) | (sink == ranking[0]) | (tallies[sink] == 0), 0, jnp.maximum(slack, 0))
    passed = jax.random.randint(jax.random.fold_in(own, 4), (count // 2,), 0, 1 << 20) % (slack + 1)
    tallies = tallies.at[source_of].add(-passed).at[sink].add(passed)
    items = jnp.searchsorted(jnp.cumsum(tallies), jnp.arange(rows * top), side="right").astype(jnp.int32)
    table = items.reshape(top, rows).T
    table = table[jax.random.permutation(jax.random.fold_in(own, 1), rows)]
    turn = jax.random.randint(jax.random.fold_in(own, 2), (rows, 1), 0, top)
    return jnp.take_along_axis(table, (jnp.arange(top)[None, :] + turn) % top, axis=1)


def shares(count, total, bound, skew, full):
    weights = [(1 << 20) // math.isqrt(grade ** skew) + 1 for grade in range(1, count + 1)]
    largest = bound if full else min(bound, max(-(-total // count), total * weights[0] // sum(weights)))
    least = 1 if total - largest >= count - 1 else 0
    counts, rest = [largest] + [least] * (count - 1), total - largest - least * (count - 1)
    while rest > 0:
        free = [i for i in range(1, count) if counts[i] < largest] or [i for i in range(1, count) if counts[i] < bound]
        whole, left = sum([weights[i] for i in free]), rest
        for i in free:
            extra = min(bound - counts[i], max(1, left * weights[i] // whole), rest)
            counts[i] = counts[i] + extra
            rest = rest - extra
    return np.array(counts)


def gaussian(own_key, shape, width, most, cuts=(), held_as=jnp.bfloat16):
    drawn = width * jax.random.normal(own_key, shape, jnp.float32)
    if cuts:
        drawn = drawn * shard_levels(own_key, shape, cuts, -0.22, 0.18)
    return jnp.clip(drawn, -most, most).astype(held_as)


def setup_inputs(seed: int = 0, part: int = 0) -> dict:
    streams_of = jax.random.split(jax.random.key(seed), 9)
    own_keys = jax.random.split(jax.random.fold_in(streams_of[8], part), 9)
    tokens = gaussian(own_keys[0], (ROWS, D), 1.0, 6.0, ((0, 32),))
    cotangent = gaussian(own_keys[1], (ROWS, D), 2.0, 12.0, ((0, 32),))
    gate_values = jnp.clip(0.049804688 + 0.24902344 * jax.random.uniform(own_keys[2], (ROWS, TOP), jnp.float32) ** shard_levels(own_keys[2], (ROWS, TOP), ((0, 32),), -0.2, 0.2), 0.049804688, 0.29882812).astype(jnp.bfloat16)
    expert_ids_keys = jax.random.split(jax.random.fold_in(own_keys[3], 1), ROWS // ROWS_DEV)
    expert_ids_turns = jax.random.permutation(jax.random.fold_in(own_keys[3], 3), ROWS // ROWS_DEV)
    expert_ids = jax.vmap(lambda own, number: assign_block(jax.random.fold_in(own_keys[3], 2), own, number, ROWS_DEV, EXPERTS, TOP, CAP, 1))(expert_ids_keys, expert_ids_turns).reshape((ROWS, TOP))
    packing = draw_packing(jax.random.fold_in(jax.random.fold_in(streams_of[8], part), 71), part)
    w_gate = gaussian(streams_of[5], (EXPERTS, FF, D), D ** -0.5, 0.125, ((0, 16), (1, 2)))
    w_up = gaussian(streams_of[6], (EXPERTS, FF, D), D ** -0.5, 0.125, ((0, 16), (1, 2)))
    w_down = gaussian(streams_of[7], (EXPERTS, FF, D), FF ** -0.5, 0.3125, ((0, 16), (1, 2)))
    return {"tokens": tokens, "cotangent": cotangent, "gate_values": gate_values, "expert_ids": expert_ids, "packing": packing, "w_gate": w_gate, "w_up": w_up, "w_down": w_down}


def expert_terms(inputs, upstream, gate_mat, up_mat, down_mat):
    gate_pre = jnp.dot(inputs, gate_mat.T, preferred_element_type=jnp.float32)
    up_pre = jnp.dot(inputs, up_mat.T, preferred_element_type=jnp.float32)
    sigmoid_val = jax.nn.sigmoid(gate_pre)
    activated = gate_pre * sigmoid_val
    hidden = (activated * up_pre).astype(jnp.bfloat16)
    hidden_grad = jnp.dot(upstream, down_mat.T, preferred_element_type=jnp.float32)
    silu_slope = sigmoid_val * (1.0 + gate_pre * (1.0 - sigmoid_val))
    gate_grad = (hidden_grad * up_pre * silu_slope).astype(jnp.bfloat16)
    up_grad = (hidden_grad * activated).astype(jnp.bfloat16)
    weight_grads = (
        jnp.dot(gate_grad.T, inputs, preferred_element_type=jnp.float32).astype(jnp.bfloat16),
        jnp.dot(up_grad.T, inputs, preferred_element_type=jnp.float32).astype(jnp.bfloat16),
        jnp.dot(hidden.T, upstream, preferred_element_type=jnp.float32).astype(jnp.bfloat16),
    )
    return weight_grads, gate_grad, up_grad


def reference(tokens, cotangent, gate_values, expert_ids, packing, w_gate, w_up, w_down):
    slot_index = jnp.arange(ROWS, dtype=jnp.int32)
    expert_col = (slot_index // ROWS_DEV) % N_EXPERT
    is_kept = packing >= 0
    home_row = jnp.where(is_kept, ((packing // ROWS_DEV) * N_EXPERT + expert_col) * ROWS_DEV + packing % ROWS_DEV, 0).astype(jnp.int32)
    rebal_rows = jnp.where(is_kept[:, None], tokens[home_row], jnp.zeros((), tokens.dtype))
    rebal_upstream = jnp.where(is_kept[:, None], cotangent[home_row], jnp.zeros((), cotangent.dtype))
    flat_ids = expert_ids.reshape(-1)
    flat_gates = gate_values.reshape(-1).astype(jnp.float32)
    bucket = N_DP * N_EXPERT * CAP
    assignments = ROWS * TOP
    block_width = FF // N_DP

    def one_expert(running, expert):
        picked = jnp.nonzero(flat_ids == expert, size=bucket, fill_value=assignments)[0].astype(jnp.int32)
        is_live = picked < assignments
        clipped = jnp.minimum(picked, assignments - 1)
        owner_row = clipped // TOP
        inputs = jnp.where(is_live[:, None], rebal_rows[owner_row], jnp.zeros((), rebal_rows.dtype))
        upstream = jnp.where(is_live[:, None], flat_gates[clipped][:, None] * rebal_upstream[owner_row].astype(jnp.float32), 0.0).astype(jnp.bfloat16)
        gate_mat = w_gate[expert]
        up_mat = w_up[expert]
        weight_grads, gate_grad, up_grad = expert_terms(inputs, upstream, gate_mat, up_mat, w_down[expert])
        slot_sum = jnp.zeros((bucket, D), jnp.float32)
        for block_index in range(N_DP):
            low = block_index * block_width
            term = jnp.dot(gate_grad[:, low:low + block_width], gate_mat[low:low + block_width], preferred_element_type=jnp.float32)
            term = term + jnp.dot(up_grad[:, low:low + block_width], up_mat[low:low + block_width], preferred_element_type=jnp.float32)
            rounded = lax.optimization_barrier(term.astype(jnp.bfloat16))
            slot_sum = slot_sum + rounded.astype(jnp.float32)
        slot_grad = slot_sum.astype(jnp.bfloat16)
        running = running.at[owner_row].add(jnp.where(is_live[:, None], slot_grad.astype(jnp.float32), 0.0))
        return running, weight_grads

    running, weight_grads = lax.scan(one_expert, jnp.zeros((ROWS, D), jnp.float32), jnp.arange(EXPERTS, dtype=jnp.int32))
    rebal_grad = running.astype(jnp.bfloat16)
    target = jnp.where(is_kept, home_row, ROWS).astype(jnp.int32)
    input_grad = jnp.zeros((ROWS, D), jnp.bfloat16).at[target].add(rebal_grad, mode="drop")
    return input_grad, weight_grads[0], weight_grads[1], weight_grads[2]
```

```python
import jax
import jax.numpy as jnp
from jax import lax
from jax.sharding import PartitionSpec as P


def slot_table(route_ids, route_gates, expert_count, capacity):
    row_count, top_count = route_ids.shape
    flat_ids = route_ids.reshape(-1)
    labels = jnp.arange(expert_count, dtype=jnp.int32)
    onehot = (flat_ids[:, None] == labels[None, :]).astype(jnp.int32)
    earlier = jnp.cumsum(onehot, axis=0) - onehot
    rank_in = jnp.sum(earlier * onehot, axis=1)
    position = flat_ids * capacity + rank_in
    places = jnp.arange(expert_count * capacity, dtype=jnp.int32)
    matched = places[:, None] == position[None, :]
    owner_row = jnp.arange(row_count * top_count, dtype=jnp.int32) // top_count
    occupied = jnp.any(matched, axis=1)
    slot_row = jnp.sum(jnp.where(matched, owner_row[None, :], 0), axis=1)
    flat_gates = route_gates.reshape(-1).astype(jnp.float32)
    slot_gate = jnp.sum(jnp.where(matched, flat_gates[None, :], 0.0), axis=1)
    return (position.reshape(row_count, top_count), occupied, slot_row, slot_gate)


def pick_rows(slot_lists, pooled):
    sources = jnp.arange(pooled.shape[0], dtype=jnp.int32)
    choose = (slot_lists[:, None] == sources[None, :]).astype(jnp.bfloat16)
    return jnp.dot(choose, pooled, preferred_element_type=jnp.float32).astype(jnp.bfloat16)


def fill_slots(rebal_rows, rebal_upstream, occupied, slot_row, slot_gate):
    send_rows = jnp.where(occupied[:, None], rebal_rows[slot_row], jnp.zeros((), jnp.bfloat16))
    scaled = slot_gate[:, None] * rebal_upstream[slot_row].astype(jnp.float32)
    send_upstream = jnp.where(occupied[:, None], scaled, 0.0).astype(jnp.bfloat16)
    return (send_rows, send_upstream)


def expert_terms(inputs, upstream, gate_mat, up_mat, down_mat):
    gate_pre = jnp.dot(inputs, gate_mat.T, preferred_element_type=jnp.float32)
    up_pre = jnp.dot(inputs, up_mat.T, preferred_element_type=jnp.float32)
    sigmoid_val = jax.nn.sigmoid(gate_pre)
    activated = gate_pre * sigmoid_val
    hidden = (activated * up_pre).astype(jnp.bfloat16)
    hidden_grad = jnp.dot(upstream, down_mat.T, preferred_element_type=jnp.float32)
    silu_slope = sigmoid_val * (1.0 + gate_pre * (1.0 - sigmoid_val))
    gate_grad = (hidden_grad * up_pre * silu_slope).astype(jnp.bfloat16)
    up_grad = (hidden_grad * activated).astype(jnp.bfloat16)
    weight_grads = (
        jnp.dot(gate_grad.T, inputs, preferred_element_type=jnp.float32).astype(jnp.bfloat16)[None],
        jnp.dot(up_grad.T, inputs, preferred_element_type=jnp.float32).astype(jnp.bfloat16)[None],
        jnp.dot(hidden.T, upstream, preferred_element_type=jnp.float32).astype(jnp.bfloat16)[None],
    )
    partial_grad = jnp.dot(gate_grad, gate_mat, preferred_element_type=jnp.float32)
    partial_grad = partial_grad + jnp.dot(up_grad, up_mat, preferred_element_type=jnp.float32)
    return (weight_grads, partial_grad)


def routed_local(tokens, cotangent, gate_values, expert_ids, packing, w_gate, w_up, w_down):
    row_count, top_count = expert_ids.shape
    model_width = tokens.shape[1]
    dp_size = lax.axis_size("dp")
    expert_count = lax.axis_size("expert") * w_gate.shape[0]
    capacity = min(row_count, max(2, row_count * top_count // expert_count + 1))
    gate_mat = w_gate[0]
    up_mat = w_up[0]
    down_mat = w_down[0]
    pooled_rows, pooled_upstream, pooled_gates = (
        lax.all_gather(tokens, "dp", axis=0, tiled=True),
        lax.all_gather(cotangent, "dp", axis=0, tiled=True),
        lax.all_gather(gate_values, "dp", axis=0, tiled=True),
    )
    lists_all, pooled_ids = (
        lax.all_gather(packing, "dp", axis=0, tiled=True),
        lax.all_gather(expert_ids, "dp", axis=0, tiled=True),
    )
    member_rows = []
    member_upstream = []
    member_positions = []
    for member in range(dp_size):
        low = member * row_count
        slot_lists = lists_all[low : low + row_count]
        position, occupied, slot_row, slot_gate = slot_table(
            pooled_ids[low : low + row_count],
            pooled_gates[low : low + row_count],
            expert_count,
            capacity,
        )
        send_rows, send_upstream = fill_slots(
            pick_rows(slot_lists, pooled_rows),
            pick_rows(slot_lists, pooled_upstream),
            occupied,
            slot_row,
            slot_gate,
        )
        member_rows.append(send_rows.reshape(expert_count, capacity * model_width))
        member_upstream.append(send_upstream.reshape(expert_count, capacity * model_width))
        member_positions.append(position)
    own_position = jnp.stack(member_positions)[lax.axis_index("dp")]
    send_rows = jnp.concatenate(member_rows, axis=1).reshape(
        expert_count * dp_size * capacity, model_width
    )
    send_upstream = jnp.concatenate(member_upstream, axis=1).reshape(
        expert_count * dp_size * capacity, model_width
    )
    recv_rows, recv_upstream = (
        lax.all_to_all(send_rows, "expert", split_axis=0, concat_axis=0, tiled=True),
        lax.all_to_all(send_upstream, "expert", split_axis=0, concat_axis=0, tiled=True),
    )
    weight_grads, partial_grad = expert_terms(recv_rows, recv_upstream, gate_mat, up_mat, down_mat)
    summed = lax.psum_scatter(
        partial_grad.reshape(expert_count, dp_size * capacity * model_width).astype(jnp.bfloat16),
        "dp",
        scatter_dimension=1,
        tiled=True,
    ).astype(jnp.float32)
    slot_grad = summed.reshape(expert_count * capacity, model_width).astype(jnp.bfloat16)
    returned = lax.all_to_all(slot_grad, "expert", split_axis=0, concat_axis=0, tiled=True)
    rebal_grad = jnp.sum(returned[own_position].astype(jnp.float32), axis=1).astype(jnp.bfloat16)
    pooled_grad = lax.all_gather(rebal_grad, "dp", axis=0, tiled=True)
    home_index = lax.axis_index("dp") * row_count + jnp.arange(row_count, dtype=jnp.int32)
    choose = (lists_all[None, :] == home_index[:, None]).astype(jnp.bfloat16)
    input_grad = jnp.dot(choose, pooled_grad, preferred_element_type=jnp.float32).astype(
        jnp.bfloat16
    )
    return (input_grad, weight_grads[0], weight_grads[1], weight_grads[2])


def home_gates(packing, expert_ids, gate_values, dp_size, expert_count):
    top = expert_ids.shape[1]
    here = lax.axis_index("expert")
    own = jnp.where(expert_ids == here, gate_values.astype(jnp.float32), 0.0)
    slot_gate = jnp.sum(own, axis=1)
    pair = lambda flat: flat.reshape(dp_size, expert_count, -1).transpose(1, 0, 2).reshape(expert_count, -1)
    lists = pair(packing)
    by_slot = pair(slot_gate)
    pair_rows = lists.shape[1]
    homes = jnp.arange(pair_rows, dtype=jnp.int32)
    matched = lists[:, None, :] == homes[None, :, None]
    by_home = jnp.sum(jnp.where(matched, by_slot[:, None, :], 0.0), axis=2)
    return by_home.reshape(expert_count, dp_size, -1).transpose(1, 0, 2).reshape(-1)


def dense_local(tokens, cotangent, gate_values, expert_ids, packing, w_gate, w_up, w_down):
    row_count, top = expert_ids.shape
    dp_size = lax.axis_size("dp")
    devices = lax.axis_size("expert")
    axes = ("dp", "expert")
    gate_mat, up_mat, down_mat = w_gate[0], w_up[0], w_down[0]
    routing = jnp.concatenate(
        [
            gate_values,
            expert_ids.astype(jnp.bfloat16),
            packing[:, None].astype(jnp.bfloat16),
        ],
        axis=1,
    )
    routing = lax.all_gather(routing, axes, axis=0, tiled=True)
    inputs = lax.all_gather(tokens, axes, axis=0, tiled=True)
    upstream = lax.all_gather(cotangent, axes, axis=0, tiled=True)
    gates = home_gates(
        routing[:, 2 * top].astype(jnp.int32),
        routing[:, top : 2 * top].astype(jnp.int32),
        routing[:, :top],
        dp_size,
        devices,
    )[:, None]
    gate_pre = jnp.dot(inputs, gate_mat.T, preferred_element_type=jnp.float32)
    up_pre = jnp.dot(inputs, up_mat.T, preferred_element_type=jnp.float32)
    hidden_grad = gates * jnp.dot(upstream, down_mat.T, preferred_element_type=jnp.float32)
    sigmoid_val = jax.nn.sigmoid(gate_pre)
    activated = gate_pre * sigmoid_val
    hidden = (gates * activated * up_pre).astype(jnp.bfloat16)
    silu_slope = sigmoid_val * (1.0 + gate_pre * (1.0 - sigmoid_val))
    gate_grad = (hidden_grad * up_pre * silu_slope).astype(jnp.bfloat16)
    up_grad = (hidden_grad * activated).astype(jnp.bfloat16)
    partial_grad = jnp.dot(gate_grad, gate_mat, preferred_element_type=jnp.float32)
    partial_grad = partial_grad + jnp.dot(up_grad, up_mat, preferred_element_type=jnp.float32)
    input_grad = lax.psum_scatter(
        partial_grad.astype(jnp.bfloat16), axes, scatter_dimension=0, tiled=True
    )
    weight_grads = [
        jnp.dot(grad.T, rows, preferred_element_type=jnp.float32).astype(jnp.bfloat16)[None]
        for grad, rows in ((gate_grad, inputs), (up_grad, inputs), (hidden, upstream))
    ]
    return (input_grad, *weight_grads)


def local(tokens, cotangent, gate_values, expert_ids, packing, w_gate, w_up, w_down):
    row_count, top = expert_ids.shape
    expert_count = lax.axis_size("expert") * w_gate.shape[0]
    capacity = min(row_count, max(2, row_count * top // expert_count + 1))
    few = capacity * 4 <= row_count
    chosen = routed_local if few else dense_local
    return chosen(
        tokens, cotangent, gate_values, expert_ids, packing, w_gate, w_up, w_down
    )


def solution(mesh):
    in_specs = (
        P(("groups", "dp", "expert"), None),
        P(("groups", "dp", "expert"), None),
        P(("groups", "dp", "expert"), None),
        P(("groups", "dp", "expert"), None),
        P(("groups", "dp", "expert")),
        P("expert", "dp", None),
        P("expert", "dp", None),
        P("expert", "dp", None),
    )
    out_specs = (
        P(("groups", "dp", "expert"), None),
        P(("groups", "expert"), "dp", None),
        P(("groups", "expert"), "dp", None),
        P(("groups", "expert"), "dp", None),
    )
    return jax.shard_map(local, mesh=mesh, in_specs=in_specs, out_specs=out_specs, check_vma=False)
```

```python
import math

import jax
import jax.numpy as jnp
from jax import lax
from jax.sharding import PartitionSpec as P


def slot_table(route_ids, route_gates, expert_count, capacity):
    row_count, top_count = route_ids.shape
    flat_ids = route_ids.reshape(-1)
    labels = jnp.arange(expert_count, dtype=jnp.int32)
    onehot = (flat_ids[:, None] == labels[None, :]).astype(jnp.int32)
    earlier = jnp.cumsum(onehot, axis=0) - onehot
    rank_in = jnp.sum(earlier * onehot, axis=1)
    position = flat_ids * capacity + rank_in
    places = jnp.arange(expert_count * capacity, dtype=jnp.int32)
    matched = places[:, None] == position[None, :]
    owner_row = jnp.arange(row_count * top_count, dtype=jnp.int32) // top_count
    occupied = jnp.any(matched, axis=1)
    slot_row = jnp.sum(jnp.where(matched, owner_row[None, :], 0), axis=1)
    flat_gates = route_gates.reshape(-1).astype(jnp.float32)
    slot_gate = jnp.sum(jnp.where(matched, flat_gates[None, :], 0.0), axis=1)
    return (position.reshape(row_count, top_count), occupied, slot_row, slot_gate)


def pick_rows(slot_lists, pooled):
    sources = jnp.arange(pooled.shape[0], dtype=jnp.int32)
    choose = (slot_lists[:, None] == sources[None, :]).astype(jnp.bfloat16)
    return jnp.dot(choose, pooled, preferred_element_type=jnp.float32).astype(jnp.bfloat16)


def fill_slots(rebal_rows, rebal_upstream, occupied, slot_row, slot_gate):
    send_rows = jnp.where(occupied[:, None], rebal_rows[slot_row], jnp.zeros((), jnp.bfloat16))
    scaled = slot_gate[:, None] * rebal_upstream[slot_row].astype(jnp.float32)
    send_upstream = jnp.where(occupied[:, None], scaled, 0.0).astype(jnp.bfloat16)
    return (send_rows, send_upstream)


def expert_terms(inputs, upstream, gate_mat, up_mat, down_mat):
    gate_pre = jnp.dot(inputs, gate_mat.T, preferred_element_type=jnp.float32)
    up_pre = jnp.dot(inputs, up_mat.T, preferred_element_type=jnp.float32)
    sigmoid_val = jax.nn.sigmoid(gate_pre)
    activated = gate_pre * sigmoid_val
    hidden = (activated * up_pre).astype(jnp.bfloat16)
    hidden_grad = jnp.dot(upstream, down_mat.T, preferred_element_type=jnp.float32)
    silu_slope = sigmoid_val * (1.0 + gate_pre * (1.0 - sigmoid_val))
    gate_grad = (hidden_grad * up_pre * silu_slope).astype(jnp.bfloat16)
    up_grad = (hidden_grad * activated).astype(jnp.bfloat16)
    weight_grads = (
        jnp.dot(gate_grad.T, inputs, preferred_element_type=jnp.float32).astype(jnp.bfloat16)[None],
        jnp.dot(up_grad.T, inputs, preferred_element_type=jnp.float32).astype(jnp.bfloat16)[None],
        jnp.dot(hidden.T, upstream, preferred_element_type=jnp.float32).astype(jnp.bfloat16)[None],
    )
    partial_grad = jnp.dot(gate_grad, gate_mat, preferred_element_type=jnp.float32)
    partial_grad = partial_grad + jnp.dot(up_grad, up_mat, preferred_element_type=jnp.float32)
    return (weight_grads, partial_grad)


def routed_local(tokens, cotangent, gate_values, expert_ids, packing, w_gate, w_up, w_down):
    row_count, top_count = expert_ids.shape
    model_width = tokens.shape[1]
    dp_size = lax.axis_size("dp")
    expert_count = lax.axis_size("expert") * w_gate.shape[0]
    capacity = min(row_count, max(2, row_count * top_count // expert_count + 1))
    gate_mat = w_gate[0]
    up_mat = w_up[0]
    down_mat = w_down[0]
    pooled_rows, pooled_upstream, pooled_gates = (
        lax.all_gather(tokens, "dp", axis=0, tiled=True),
        lax.all_gather(cotangent, "dp", axis=0, tiled=True),
        lax.all_gather(gate_values, "dp", axis=0, tiled=True),
    )
    lists_all, pooled_ids = (
        lax.all_gather(packing, "dp", axis=0, tiled=True),
        lax.all_gather(expert_ids, "dp", axis=0, tiled=True),
    )
    member_rows = []
    member_upstream = []
    member_positions = []
    for member in range(dp_size):
        low = member * row_count
        slot_lists = lists_all[low : low + row_count]
        position, occupied, slot_row, slot_gate = slot_table(
            pooled_ids[low : low + row_count],
            pooled_gates[low : low + row_count],
            expert_count,
            capacity,
        )
        send_rows, send_upstream = fill_slots(
            pick_rows(slot_lists, pooled_rows),
            pick_rows(slot_lists, pooled_upstream),
            occupied,
            slot_row,
            slot_gate,
        )
        member_rows.append(send_rows.reshape(expert_count, capacity * model_width))
        member_upstream.append(send_upstream.reshape(expert_count, capacity * model_width))
        member_positions.append(position)
    own_position = jnp.stack(member_positions)[lax.axis_index("dp")]
    send_rows = jnp.concatenate(member_rows, axis=1).reshape(
        expert_count * dp_size * capacity, model_width
    )
    send_upstream = jnp.concatenate(member_upstream, axis=1).reshape(
        expert_count * dp_size * capacity, model_width
    )
    recv_rows, recv_upstream = (
        lax.all_to_all(send_rows, "expert", split_axis=0, concat_axis=0, tiled=True),
        lax.all_to_all(send_upstream, "expert", split_axis=0, concat_axis=0, tiled=True),
    )
    weight_grads, partial_grad = expert_terms(recv_rows, recv_upstream, gate_mat, up_mat, down_mat)
    summed = lax.psum_scatter(
        partial_grad.reshape(expert_count, dp_size * capacity * model_width).astype(jnp.bfloat16),
        "dp",
        scatter_dimension=1,
        tiled=True,
    ).astype(jnp.float32)
    slot_grad = summed.reshape(expert_count * capacity, model_width).astype(jnp.bfloat16)
    returned = lax.all_to_all(slot_grad, "expert", split_axis=0, concat_axis=0, tiled=True)
    rebal_grad = jnp.sum(returned[own_position].astype(jnp.float32), axis=1).astype(jnp.bfloat16)
    pooled_grad = lax.all_gather(rebal_grad, "dp", axis=0, tiled=True)
    home_index = lax.axis_index("dp") * row_count + jnp.arange(row_count, dtype=jnp.int32)
    choose = (lists_all[None, :] == home_index[:, None]).astype(jnp.bfloat16)
    input_grad = jnp.dot(choose, pooled_grad, preferred_element_type=jnp.float32).astype(
        jnp.bfloat16
    )
    return (input_grad, weight_grads[0], weight_grads[1], weight_grads[2])


def swap(value):
    return lax.ppermute(value, "dp", [(0, 1), (1, 0)])


def shift_outer(value, count, inner, step):
    return lax.ppermute(
        value, "expert", [(place, (place + step * inner) % count) for place in range(count)]
    )


def swap_inner(value, count, partner):
    return lax.ppermute(value, "expert", [(place, place ^ partner) for place in range(count)])


def home_gates(packing, expert_ids, gate_values, count):
    row_count = packing.shape[0]
    labels = jnp.arange(count, dtype=jnp.int32)
    named = expert_ids[:, :, None] == labels[None, None, :]
    by_slot = jnp.sum(jnp.where(named, gate_values.astype(jnp.float32)[:, :, None], 0.0), axis=1)
    own_homes = lax.axis_index("dp") * row_count + jnp.arange(row_count, dtype=jnp.int32)
    routing = jnp.concatenate(
        [packing[:, None].astype(jnp.bfloat16), by_slot.astype(jnp.bfloat16)], axis=1
    )
    routing = jnp.concatenate([routing, swap(routing)], axis=0).astype(jnp.float32)
    matched = own_homes[:, None] == routing[:, 0].astype(jnp.int32)[None, :]
    return jnp.sum(jnp.where(matched[:, :, None], routing[None, :, 1:], 0.0), axis=1)


def spread(value, count, inner):
    column = jnp.concatenate(
        [value] + [shift_outer(value, count, inner, step) for step in range(1, count // inner)],
        axis=0,
    )
    return jnp.concatenate(
        [column] + [swap_inner(column, count, partner) for partner in range(1, inner)], axis=0
    )


def bring_back(value, count, inner):
    outer = count // inner
    blocks = value.reshape(inner, -1, value.shape[-1])
    total = blocks[0].astype(jnp.float32)
    for partner in range(1, inner):
        total = total + swap_inner(blocks[partner], count, partner).astype(jnp.float32)
    blocks = total.reshape(outer, -1, value.shape[-1])
    rounded = blocks.astype(jnp.bfloat16)
    total = blocks[0]
    for step in range(1, outer):
        total = total + shift_outer(rounded[step], count, inner, -step).astype(jnp.float32)
    return total.astype(jnp.bfloat16)


def dense_local(tokens, cotangent, gate_values, expert_ids, packing, w_gate, w_up, w_down):
    model_width = tokens.shape[1]
    half = w_gate.shape[1]
    count = lax.axis_size("expert")
    inner = math.gcd(count, 4)
    gate_up = jnp.concatenate([w_gate[0], swap(w_gate[0]), w_up[0], swap(w_up[0])], axis=0)
    down = jnp.concatenate([w_down[0], swap(w_down[0])], axis=0)
    gates = home_gates(packing, expert_ids, gate_values, count).astype(jnp.bfloat16)
    inputs = spread(tokens, count, inner)
    upstream = spread(jnp.concatenate([cotangent, gates], axis=1), count, inner)
    here = jnp.arange(count, dtype=jnp.int32) == lax.axis_index("expert")
    gate = jnp.sum(
        jnp.where(here[None, :], upstream[:, model_width:].astype(jnp.float32), 0.0),
        axis=1,
        keepdims=True,
    )
    upstream = upstream[:, :model_width]
    pre = jnp.dot(inputs, gate_up.T, preferred_element_type=jnp.float32)
    gate_pre, up_pre = pre[:, : 2 * half], pre[:, 2 * half :]
    hidden_grad = gate * jnp.dot(upstream, down.T, preferred_element_type=jnp.float32)
    sigmoid_val = jax.nn.sigmoid(gate_pre)
    activated = gate_pre * sigmoid_val
    hidden = (gate * activated * up_pre).astype(jnp.bfloat16)
    silu_slope = sigmoid_val * (1.0 + gate_pre * (1.0 - sigmoid_val))
    gate_grad = (hidden_grad * up_pre * silu_slope).astype(jnp.bfloat16)
    up_grad = (hidden_grad * activated).astype(jnp.bfloat16)
    both_grad = jnp.concatenate([gate_grad, up_grad], axis=1)
    partial_grad = jnp.dot(both_grad, gate_up, preferred_element_type=jnp.float32)
    input_grad = bring_back(partial_grad.astype(jnp.bfloat16), count, inner)
    weight_grads = []
    for grad, rows in ((gate_grad, inputs), (up_grad, inputs), (hidden, upstream)):
        whole = jnp.dot(grad.T, rows, preferred_element_type=jnp.float32)
        other = swap(whole[half:].astype(jnp.bfloat16)).astype(jnp.float32)
        weight_grads.append((whole[:half] + other).astype(jnp.bfloat16)[None])
    return (input_grad, *weight_grads)


def local(tokens, cotangent, gate_values, expert_ids, packing, w_gate, w_up, w_down):
    row_count, top = expert_ids.shape
    expert_count = lax.axis_size("expert") * w_gate.shape[0]
    capacity = min(row_count, max(2, row_count * top // expert_count + 1))
    few = capacity * 4 <= row_count
    chosen = routed_local if few else dense_local
    return chosen(
        tokens, cotangent, gate_values, expert_ids, packing, w_gate, w_up, w_down
    )


def solution(mesh):
    in_specs = (
        P(("groups", "dp", "expert"), None),
        P(("groups", "dp", "expert"), None),
        P(("groups", "dp", "expert"), None),
        P(("groups", "dp", "expert"), None),
        P(("groups", "dp", "expert")),
        P("expert", "dp", None),
        P("expert", "dp", None),
        P("expert", "dp", None),
    )
    out_specs = (
        P(("groups", "dp", "expert"), None),
        P(("groups", "expert"), "dp", None),
        P(("groups", "expert"), "dp", None),
        P(("groups", "expert"), "dp", None),
    )
    return jax.shard_map(local, mesh=mesh, in_specs=in_specs, out_specs=out_specs, check_vma=False)
```

```python
import math

import jax
import jax.numpy as jnp
from jax import lax
from jax.sharding import PartitionSpec as P


def slot_table(route_ids, route_gates, expert_count, capacity):
    row_count, top_count = route_ids.shape
    flat_ids = route_ids.reshape(-1)
    labels = jnp.arange(expert_count, dtype=jnp.int32)
    onehot = (flat_ids[:, None] == labels[None, :]).astype(jnp.int32)
    earlier = jnp.cumsum(onehot, axis=0) - onehot
    rank_in = jnp.sum(earlier * onehot, axis=1)
    position = flat_ids * capacity + rank_in
    places = jnp.arange(expert_count * capacity, dtype=jnp.int32)
    matched = places[:, None] == position[None, :]
    owner_row = jnp.arange(row_count * top_count, dtype=jnp.int32) // top_count
    occupied = jnp.any(matched, axis=1)
    slot_row = jnp.sum(jnp.where(matched, owner_row[None, :], 0), axis=1)
    flat_gates = route_gates.reshape(-1).astype(jnp.float32)
    slot_gate = jnp.sum(jnp.where(matched, flat_gates[None, :], 0.0), axis=1)
    return (position.reshape(row_count, top_count), occupied, slot_row, slot_gate)


def pick_rows(slot_lists, pooled):
    sources = jnp.arange(pooled.shape[0], dtype=jnp.int32)
    choose = (slot_lists[:, None] == sources[None, :]).astype(jnp.bfloat16)
    return jnp.dot(choose, pooled, preferred_element_type=jnp.float32).astype(jnp.bfloat16)


def fill_slots(rebal_rows, rebal_upstream, occupied, slot_row, slot_gate):
    send_rows = jnp.where(occupied[:, None], rebal_rows[slot_row], jnp.zeros((), jnp.bfloat16))
    scaled = slot_gate[:, None] * rebal_upstream[slot_row].astype(jnp.float32)
    send_upstream = jnp.where(occupied[:, None], scaled, 0.0).astype(jnp.bfloat16)
    return (send_rows, send_upstream)


def expert_terms(inputs, upstream, gate_mat, up_mat, down_mat):
    gate_pre = jnp.dot(inputs, gate_mat.T, preferred_element_type=jnp.float32)
    up_pre = jnp.dot(inputs, up_mat.T, preferred_element_type=jnp.float32)
    sigmoid_val = jax.nn.sigmoid(gate_pre)
    activated = gate_pre * sigmoid_val
    hidden = (activated * up_pre).astype(jnp.bfloat16)
    hidden_grad = jnp.dot(upstream, down_mat.T, preferred_element_type=jnp.float32)
    silu_slope = sigmoid_val * (1.0 + gate_pre * (1.0 - sigmoid_val))
    gate_grad = (hidden_grad * up_pre * silu_slope).astype(jnp.bfloat16)
    up_grad = (hidden_grad * activated).astype(jnp.bfloat16)
    weight_grads = (
        jnp.dot(gate_grad.T, inputs, preferred_element_type=jnp.float32).astype(jnp.bfloat16)[None],
        jnp.dot(up_grad.T, inputs, preferred_element_type=jnp.float32).astype(jnp.bfloat16)[None],
        jnp.dot(hidden.T, upstream, preferred_element_type=jnp.float32).astype(jnp.bfloat16)[None],
    )
    partial_grad = jnp.dot(gate_grad, gate_mat, preferred_element_type=jnp.float32)
    partial_grad = partial_grad + jnp.dot(up_grad, up_mat, preferred_element_type=jnp.float32)
    return (weight_grads, partial_grad)


def routed_local(tokens, cotangent, gate_values, expert_ids, packing, w_gate, w_up, w_down):
    row_count, top_count = expert_ids.shape
    model_width = tokens.shape[1]
    dp_size = lax.axis_size("dp")
    expert_count = lax.axis_size("expert") * w_gate.shape[0]
    capacity = min(row_count, max(2, row_count * top_count // expert_count + 1))
    gate_mat = w_gate[0]
    up_mat = w_up[0]
    down_mat = w_down[0]
    pooled_rows, pooled_upstream, pooled_gates = (
        lax.all_gather(tokens, "dp", axis=0, tiled=True),
        lax.all_gather(cotangent, "dp", axis=0, tiled=True),
        lax.all_gather(gate_values, "dp", axis=0, tiled=True),
    )
    lists_all, pooled_ids = (
        lax.all_gather(packing, "dp", axis=0, tiled=True),
        lax.all_gather(expert_ids, "dp", axis=0, tiled=True),
    )
    member_rows = []
    member_upstream = []
    member_positions = []
    for member in range(dp_size):
        low = member * row_count
        slot_lists = lists_all[low : low + row_count]
        position, occupied, slot_row, slot_gate = slot_table(
            pooled_ids[low : low + row_count],
            pooled_gates[low : low + row_count],
            expert_count,
            capacity,
        )
        send_rows, send_upstream = fill_slots(
            pick_rows(slot_lists, pooled_rows),
            pick_rows(slot_lists, pooled_upstream),
            occupied,
            slot_row,
            slot_gate,
        )
        member_rows.append(send_rows.reshape(expert_count, capacity * model_width))
        member_upstream.append(send_upstream.reshape(expert_count, capacity * model_width))
        member_positions.append(position)
    own_position = jnp.stack(member_positions)[lax.axis_index("dp")]
    send_rows = jnp.concatenate(member_rows, axis=1).reshape(
        expert_count * dp_size * capacity, model_width
    )
    send_upstream = jnp.concatenate(member_upstream, axis=1).reshape(
        expert_count * dp_size * capacity, model_width
    )
    recv_rows, recv_upstream = (
        lax.all_to_all(send_rows, "expert", split_axis=0, concat_axis=0, tiled=True),
        lax.all_to_all(send_upstream, "expert", split_axis=0, concat_axis=0, tiled=True),
    )
    weight_grads, partial_grad = expert_terms(recv_rows, recv_upstream, gate_mat, up_mat, down_mat)
    summed = lax.psum_scatter(
        partial_grad.reshape(expert_count, dp_size * capacity * model_width).astype(jnp.bfloat16),
        "dp",
        scatter_dimension=1,
        tiled=True,
    ).astype(jnp.float32)
    slot_grad = summed.reshape(expert_count * capacity, model_width).astype(jnp.bfloat16)
    returned = lax.all_to_all(slot_grad, "expert", split_axis=0, concat_axis=0, tiled=True)
    rebal_grad = jnp.sum(returned[own_position].astype(jnp.float32), axis=1).astype(jnp.bfloat16)
    pooled_grad = lax.all_gather(rebal_grad, "dp", axis=0, tiled=True)
    home_index = lax.axis_index("dp") * row_count + jnp.arange(row_count, dtype=jnp.int32)
    choose = (lists_all[None, :] == home_index[:, None]).astype(jnp.bfloat16)
    input_grad = jnp.dot(choose, pooled_grad, preferred_element_type=jnp.float32).astype(
        jnp.bfloat16
    )
    return (input_grad, weight_grads[0], weight_grads[1], weight_grads[2])


def swap(value):
    return lax.ppermute(value, "dp", [(0, 1), (1, 0)])


def shift_outer(value, count, inner, step):
    return lax.ppermute(
        value, "expert", [(place, (place + step * inner) % count) for place in range(count)]
    )


def swap_inner(value, count, partner):
    return lax.ppermute(value, "expert", [(place, place ^ partner) for place in range(count)])


def home_gates(packing, expert_ids, gate_values, count):
    row_count = packing.shape[0]
    labels = jnp.arange(count, dtype=jnp.int32)
    named = expert_ids[:, :, None] == labels[None, None, :]
    by_slot = jnp.sum(jnp.where(named, gate_values.astype(jnp.float32)[:, :, None], 0.0), axis=1)
    own_homes = lax.axis_index("dp") * row_count + jnp.arange(row_count, dtype=jnp.int32)
    routing = jnp.concatenate(
        [packing[:, None].astype(jnp.bfloat16), by_slot.astype(jnp.bfloat16)], axis=1
    )
    routing = jnp.concatenate([routing, swap(routing)], axis=0).astype(jnp.float32)
    matched = own_homes[:, None] == routing[:, 0].astype(jnp.int32)[None, :]
    return jnp.sum(jnp.where(matched[:, :, None], routing[None, :, 1:], 0.0), axis=1)


def along_outer(value, count, inner):
    return [value] + [shift_outer(value, count, inner, step) for step in range(1, count // inner)]


def across_inner(column, count, inner):
    if inner < 4:
        return [column] + [swap_inner(column, count, partner) for partner in range(1, inner)]
    cut = column.shape[0] // 2
    first = swap_inner(column, count, 1)
    second = swap_inner(column, count, 2)
    far_top = swap_inner(first[:cut], count, 2)
    far_bottom = swap_inner(second[cut:], count, 1)
    return [column, first, second, far_top, far_bottom]


def bring_back(value, count, inner):
    outer = count // inner
    blocks = value.reshape(inner, -1, value.shape[-1])
    total = blocks[0].astype(jnp.float32)
    for partner in range(1, inner):
        total = total + swap_inner(blocks[partner], count, partner).astype(jnp.float32)
    blocks = total.reshape(outer, -1, value.shape[-1])
    rounded = blocks.astype(jnp.bfloat16)
    total = blocks[0]
    for step in range(1, outer):
        total = total + shift_outer(rounded[step], count, inner, -step).astype(jnp.float32)
    return total.astype(jnp.bfloat16)


def dense_local(tokens, cotangent, gate_values, expert_ids, packing, w_gate, w_up, w_down):
    model_width = tokens.shape[1]
    half = w_gate.shape[1]
    count = lax.axis_size("expert")
    inner = math.gcd(count, 4)
    token_column = jnp.concatenate(along_outer(tokens, count, inner), axis=0)
    other = swap(jnp.concatenate([w_gate[0], w_up[0], w_down[0]], axis=0))
    gates = home_gates(packing, expert_ids, gate_values, count).astype(jnp.bfloat16)
    payload = jnp.concatenate([cotangent, gates], axis=1)
    payload, token_column, other = lax.optimization_barrier((payload, token_column, other))
    upstream_column = jnp.concatenate(along_outer(payload, count, inner), axis=0)
    inputs = jnp.concatenate(across_inner(token_column, count, inner), axis=0)
    other_inputs = swap(inputs)
    upstream = jnp.concatenate(across_inner(upstream_column, count, inner), axis=0)
    here = jnp.arange(count, dtype=jnp.int32) == lax.axis_index("expert")
    gate = jnp.sum(
        jnp.where(here[None, :], upstream[:, model_width:].astype(jnp.float32), 0.0),
        axis=1,
        keepdims=True,
    )
    upstream = upstream[:, :model_width]
    gate_up = jnp.concatenate([w_gate[0], other[:half], w_up[0], other[half : 2 * half]], axis=0)
    down = jnp.concatenate([w_down[0], other[2 * half :]], axis=0)
    pre = jnp.dot(inputs, gate_up.T, preferred_element_type=jnp.float32)
    gate_pre, up_pre = pre[:, : 2 * half], pre[:, 2 * half :]
    hidden_grad = gate * jnp.dot(upstream, down.T, preferred_element_type=jnp.float32)
    sigmoid_val = jax.nn.sigmoid(gate_pre)
    activated = gate_pre * sigmoid_val
    hidden = (gate * activated * up_pre).astype(jnp.bfloat16)
    silu_slope = sigmoid_val * (1.0 + gate_pre * (1.0 - sigmoid_val))
    gate_grad = (hidden_grad * up_pre * silu_slope).astype(jnp.bfloat16)
    up_grad = (hidden_grad * activated).astype(jnp.bfloat16)
    both_grad = jnp.concatenate([gate_grad, up_grad], axis=1)
    partial_grad = jnp.dot(both_grad, gate_up, preferred_element_type=jnp.float32)
    partial_grad = partial_grad.astype(jnp.bfloat16)
    input_grad = bring_back(partial_grad, count, inner)
    grads = (gate_grad, up_grad, hidden)
    own_grads = jnp.concatenate([grad[:, :half] for grad in grads], axis=1)
    sent_grads = jnp.concatenate([grad[:, half:] for grad in grads], axis=1)
    sent_grads, upstream, _ = lax.optimization_barrier((sent_grads, upstream, partial_grad))
    other_grads = swap(sent_grads)
    other_upstream = swap(upstream)
    weight_grads = []
    for index, (rows, other_rows) in enumerate(
        ((inputs, other_inputs), (inputs, other_inputs), (upstream, other_upstream))
    ):
        low = index * half
        total = jnp.dot(
            own_grads[:, low : low + half].T, rows, preferred_element_type=jnp.float32
        ) + jnp.dot(
            other_grads[:, low : low + half].T, other_rows, preferred_element_type=jnp.float32
        )
        weight_grads.append(total.astype(jnp.bfloat16)[None])
    return (input_grad, *weight_grads)


def local(tokens, cotangent, gate_values, expert_ids, packing, w_gate, w_up, w_down):
    row_count, top = expert_ids.shape
    expert_count = lax.axis_size("expert") * w_gate.shape[0]
    capacity = min(row_count, max(2, row_count * top // expert_count + 1))
    few = capacity * 4 <= row_count
    chosen = routed_local if few else dense_local
    return chosen(
        tokens, cotangent, gate_values, expert_ids, packing, w_gate, w_up, w_down
    )


def solution(mesh):
    in_specs = (
        P(("groups", "dp", "expert"), None),
        P(("groups", "dp", "expert"), None),
        P(("groups", "dp", "expert"), None),
        P(("groups", "dp", "expert"), None),
        P(("groups", "dp", "expert")),
        P("expert", "dp", None),
        P("expert", "dp", None),
        P("expert", "dp", None),
    )
    out_specs = (
        P(("groups", "dp", "expert"), None),
        P(("groups", "expert"), "dp", None),
        P(("groups", "expert"), "dp", None),
        P(("groups", "expert"), "dp", None),
    )
    return jax.shard_map(local, mesh=mesh, in_specs=in_specs, out_specs=out_specs, check_vma=False)
```

```python
import math

import jax
import jax.numpy as jnp
from jax import lax
from jax.sharding import PartitionSpec as P


def slot_table(route_ids, route_gates, expert_count, capacity):
    row_count, top_count = route_ids.shape
    flat_ids = route_ids.reshape(-1)
    labels = jnp.arange(expert_count, dtype=jnp.int32)
    onehot = (flat_ids[:, None] == labels[None, :]).astype(jnp.int32)
    earlier = jnp.cumsum(onehot, axis=0) - onehot
    rank_in = jnp.sum(earlier * onehot, axis=1)
    position = flat_ids * capacity + rank_in
    places = jnp.arange(expert_count * capacity, dtype=jnp.int32)
    matched = places[:, None] == position[None, :]
    owner_row = jnp.arange(row_count * top_count, dtype=jnp.int32) // top_count
    occupied = jnp.any(matched, axis=1)
    slot_row = jnp.sum(jnp.where(matched, owner_row[None, :], 0), axis=1)
    flat_gates = route_gates.reshape(-1).astype(jnp.float32)
    slot_gate = jnp.sum(jnp.where(matched, flat_gates[None, :], 0.0), axis=1)
    return (position.reshape(row_count, top_count), occupied, slot_row, slot_gate)


def pick_rows(slot_lists, pooled):
    sources = jnp.arange(pooled.shape[0], dtype=jnp.int32)
    choose = (slot_lists[:, None] == sources[None, :]).astype(jnp.bfloat16)
    return jnp.dot(choose, pooled, preferred_element_type=jnp.float32).astype(jnp.bfloat16)


def fill_slots(rebal_rows, rebal_upstream, occupied, slot_row, slot_gate):
    send_rows = jnp.where(occupied[:, None], rebal_rows[slot_row], jnp.zeros((), jnp.bfloat16))
    scaled = slot_gate[:, None] * rebal_upstream[slot_row].astype(jnp.float32)
    send_upstream = jnp.where(occupied[:, None], scaled, 0.0).astype(jnp.bfloat16)
    return (send_rows, send_upstream)


def expert_terms(inputs, upstream, gate_mat, up_mat, down_mat):
    gate_pre = jnp.dot(inputs, gate_mat.T, preferred_element_type=jnp.float32)
    up_pre = jnp.dot(inputs, up_mat.T, preferred_element_type=jnp.float32)
    sigmoid_val = jax.nn.sigmoid(gate_pre)
    activated = gate_pre * sigmoid_val
    hidden = (activated * up_pre).astype(jnp.bfloat16)
    hidden_grad = jnp.dot(upstream, down_mat.T, preferred_element_type=jnp.float32)
    silu_slope = sigmoid_val * (1.0 + gate_pre * (1.0 - sigmoid_val))
    gate_grad = (hidden_grad * up_pre * silu_slope).astype(jnp.bfloat16)
    up_grad = (hidden_grad * activated).astype(jnp.bfloat16)
    weight_grads = (
        jnp.dot(gate_grad.T, inputs, preferred_element_type=jnp.float32).astype(jnp.bfloat16)[None],
        jnp.dot(up_grad.T, inputs, preferred_element_type=jnp.float32).astype(jnp.bfloat16)[None],
        jnp.dot(hidden.T, upstream, preferred_element_type=jnp.float32).astype(jnp.bfloat16)[None],
    )
    partial_grad = jnp.dot(gate_grad, gate_mat, preferred_element_type=jnp.float32)
    partial_grad = partial_grad + jnp.dot(up_grad, up_mat, preferred_element_type=jnp.float32)
    return (weight_grads, partial_grad)


def routed_local(tokens, cotangent, gate_values, expert_ids, packing, w_gate, w_up, w_down):
    row_count, top_count = expert_ids.shape
    model_width = tokens.shape[1]
    dp_size = lax.axis_size("dp")
    expert_count = lax.axis_size("expert") * w_gate.shape[0]
    capacity = min(row_count, max(2, row_count * top_count // expert_count + 1))
    gate_mat = w_gate[0]
    up_mat = w_up[0]
    down_mat = w_down[0]
    pooled_rows, pooled_upstream, pooled_gates = (
        lax.all_gather(tokens, "dp", axis=0, tiled=True),
        lax.all_gather(cotangent, "dp", axis=0, tiled=True),
        lax.all_gather(gate_values, "dp", axis=0, tiled=True),
    )
    lists_all, pooled_ids = (
        lax.all_gather(packing, "dp", axis=0, tiled=True),
        lax.all_gather(expert_ids, "dp", axis=0, tiled=True),
    )
    member_rows = []
    member_upstream = []
    member_positions = []
    for member in range(dp_size):
        low = member * row_count
        slot_lists = lists_all[low : low + row_count]
        position, occupied, slot_row, slot_gate = slot_table(
            pooled_ids[low : low + row_count],
            pooled_gates[low : low + row_count],
            expert_count,
            capacity,
        )
        send_rows, send_upstream = fill_slots(
            pick_rows(slot_lists, pooled_rows),
            pick_rows(slot_lists, pooled_upstream),
            occupied,
            slot_row,
            slot_gate,
        )
        member_rows.append(send_rows.reshape(expert_count, capacity * model_width))
        member_upstream.append(send_upstream.reshape(expert_count, capacity * model_width))
        member_positions.append(position)
    own_position = jnp.stack(member_positions)[lax.axis_index("dp")]
    send_rows = jnp.concatenate(member_rows, axis=1).reshape(
        expert_count * dp_size * capacity, model_width
    )
    send_upstream = jnp.concatenate(member_upstream, axis=1).reshape(
        expert_count * dp_size * capacity, model_width
    )
    recv_rows, recv_upstream = (
        lax.all_to_all(send_rows, "expert", split_axis=0, concat_axis=0, tiled=True),
        lax.all_to_all(send_upstream, "expert", split_axis=0, concat_axis=0, tiled=True),
    )
    weight_grads, partial_grad = expert_terms(recv_rows, recv_upstream, gate_mat, up_mat, down_mat)
    summed = lax.psum_scatter(
        partial_grad.reshape(expert_count, dp_size * capacity * model_width).astype(jnp.bfloat16),
        "dp",
        scatter_dimension=1,
        tiled=True,
    ).astype(jnp.float32)
    slot_grad = summed.reshape(expert_count * capacity, model_width).astype(jnp.bfloat16)
    returned = lax.all_to_all(slot_grad, "expert", split_axis=0, concat_axis=0, tiled=True)
    rebal_grad = jnp.sum(returned[own_position].astype(jnp.float32), axis=1).astype(jnp.bfloat16)
    pooled_grad = lax.all_gather(rebal_grad, "dp", axis=0, tiled=True)
    home_index = lax.axis_index("dp") * row_count + jnp.arange(row_count, dtype=jnp.int32)
    choose = (lists_all[None, :] == home_index[:, None]).astype(jnp.bfloat16)
    input_grad = jnp.dot(choose, pooled_grad, preferred_element_type=jnp.float32).astype(
        jnp.bfloat16
    )
    return (input_grad, weight_grads[0], weight_grads[1], weight_grads[2])


def swap(value):
    return lax.ppermute(value, "dp", [(0, 1), (1, 0)])


def shift_outer(value, count, inner, step):
    return lax.ppermute(
        value, "expert", [(place, (place + step * inner) % count) for place in range(count)]
    )


def swap_inner(value, count, partner):
    return lax.ppermute(value, "expert", [(place, place ^ partner) for place in range(count)])


def home_gates(packing, expert_ids, gate_values, count):
    row_count = packing.shape[0]
    labels = jnp.arange(count, dtype=jnp.int32)
    named = expert_ids[:, :, None] == labels[None, None, :]
    by_slot = jnp.sum(jnp.where(named, gate_values.astype(jnp.float32)[:, :, None], 0.0), axis=1)
    own_homes = lax.axis_index("dp") * row_count + jnp.arange(row_count, dtype=jnp.int32)
    routing = jnp.concatenate(
        [packing[:, None].astype(jnp.bfloat16), by_slot.astype(jnp.bfloat16)], axis=1
    )
    routing = jnp.concatenate([routing, swap(routing)], axis=0).astype(jnp.float32)
    matched = own_homes[:, None] == routing[:, 0].astype(jnp.int32)[None, :]
    return jnp.sum(jnp.where(matched[:, :, None], routing[None, :, 1:], 0.0), axis=1)


def along_outer(value, count, inner):
    return [value] + [shift_outer(value, count, inner, step) for step in range(1, count // inner)]


def across_inner(column, count, inner):
    if inner < 4:
        return [column] + [swap_inner(column, count, partner) for partner in range(1, inner)]
    cut = column.shape[0] // 2
    first = swap_inner(column, count, 1)
    second = swap_inner(column, count, 2)
    far_top = swap_inner(first[:cut], count, 2)
    far_bottom = swap_inner(second[cut:], count, 1)
    return [column, first, second, far_top, far_bottom]


def return_outer(total, count, inner):
    outer = count // inner
    blocks = total.reshape(outer, -1, total.shape[-1])
    rounded = blocks.astype(jnp.bfloat16)
    total = blocks[0]
    for step in range(1, outer):
        total = total + shift_outer(rounded[step], count, inner, -step).astype(jnp.float32)
    return total.astype(jnp.bfloat16)


def return_inner(blocks, count):
    if len(blocks) < 4:
        total = blocks[0]
        for partner in range(1, len(blocks)):
            block = blocks[partner].astype(jnp.bfloat16)
            total = total + swap_inner(block, count, partner).astype(jnp.float32)
        return total
    cut = blocks[3].shape[0] // 2
    far = blocks[3].astype(jnp.bfloat16)
    top = swap_inner(far[:cut], count, 2).astype(jnp.float32)
    bottom = swap_inner(far[cut:], count, 1).astype(jnp.float32)
    first = jnp.concatenate([blocks[1][:cut] + top, blocks[1][cut:]], axis=0)
    second = jnp.concatenate([blocks[2][:cut], blocks[2][cut:] + bottom], axis=0)
    first = swap_inner(first.astype(jnp.bfloat16), count, 1)
    second = swap_inner(second.astype(jnp.bfloat16), count, 2)
    return blocks[0] + first.astype(jnp.float32) + second.astype(jnp.float32)


def dense_local(tokens, cotangent, gate_values, expert_ids, packing, w_gate, w_up, w_down):
    model_width = tokens.shape[1]
    half = w_gate.shape[1]
    count = lax.axis_size("expert")
    inner = math.gcd(count, 4)
    token_blocks = along_outer(tokens, count, inner)
    own_weights = jnp.concatenate([w_gate[0], w_up[0], w_down[0]], axis=0)
    gates = home_gates(packing, expert_ids, gate_values, count).astype(jnp.bfloat16)
    payload = jnp.concatenate([cotangent, gates], axis=1)
    payload, token_blocks[1] = lax.optimization_barrier((payload, token_blocks[1]))
    token_column = jnp.concatenate(token_blocks, axis=0)
    upstream_column = jnp.concatenate(along_outer(payload, count, inner), axis=0)
    token_columns = across_inner(token_column, count, inner)
    own_weights, token_columns[1] = lax.optimization_barrier((own_weights, token_columns[1]))
    other = swap(own_weights)
    inputs = jnp.concatenate(token_columns, axis=0)
    other_inputs = swap(inputs)
    upstream = jnp.concatenate(across_inner(upstream_column, count, inner), axis=0)
    upstream, other_inputs = lax.optimization_barrier((upstream, other_inputs))
    here = jnp.arange(count, dtype=jnp.int32) == lax.axis_index("expert")
    gate = jnp.sum(
        jnp.where(here[None, :], upstream[:, model_width:].astype(jnp.float32), 0.0),
        axis=1,
        keepdims=True,
    )
    upstream = upstream[:, :model_width]
    gate_up = jnp.concatenate([w_gate[0], other[:half], w_up[0], other[half : 2 * half]], axis=0)
    down = jnp.concatenate([w_down[0], other[2 * half :]], axis=0)
    pre = jnp.dot(inputs, gate_up.T, preferred_element_type=jnp.float32)
    gate_pre, up_pre = pre[:, : 2 * half], pre[:, 2 * half :]
    hidden_grad = gate * jnp.dot(upstream, down.T, preferred_element_type=jnp.float32)
    sigmoid_val = jax.nn.sigmoid(gate_pre)
    activated = gate_pre * sigmoid_val
    hidden = (gate * activated * up_pre).astype(jnp.bfloat16)
    silu_slope = sigmoid_val * (1.0 + gate_pre * (1.0 - sigmoid_val))
    gate_grad = (hidden_grad * up_pre * silu_slope).astype(jnp.bfloat16)
    up_grad = (hidden_grad * activated).astype(jnp.bfloat16)
    both_grad = jnp.concatenate([gate_grad, up_grad], axis=1)
    depth = both_grad.shape[0] // inner
    blocks = [
        jnp.dot(both_grad[low : low + depth], gate_up, preferred_element_type=jnp.float32)
        for low in range(0, both_grad.shape[0], depth)
    ]
    input_grad = return_outer(return_inner(blocks, count), count, inner)
    grads = (gate_grad, up_grad, hidden)
    own_grads = jnp.concatenate([grad[:, :half] for grad in grads], axis=1)
    sent_grads = jnp.concatenate([grad[:, half:] for grad in grads], axis=1)
    sent_grads, upstream, _ = lax.optimization_barrier((sent_grads, upstream, blocks[-1]))
    other_grads = swap(sent_grads)
    other_upstream = swap(upstream)
    weight_grads = []
    for index, (rows, other_rows) in enumerate(
        ((inputs, other_inputs), (inputs, other_inputs), (upstream, other_upstream))
    ):
        low = index * half
        total = jnp.dot(
            own_grads[:, low : low + half].T, rows, preferred_element_type=jnp.float32
        ) + jnp.dot(
            other_grads[:, low : low + half].T, other_rows, preferred_element_type=jnp.float32
        )
        weight_grads.append(total.astype(jnp.bfloat16)[None])
    return (input_grad, *weight_grads)


def local(tokens, cotangent, gate_values, expert_ids, packing, w_gate, w_up, w_down):
    row_count, top = expert_ids.shape
    expert_count = lax.axis_size("expert") * w_gate.shape[0]
    capacity = min(row_count, max(2, row_count * top // expert_count + 1))
    few = capacity * 4 <= row_count
    chosen = routed_local if few else dense_local
    return chosen(
        tokens, cotangent, gate_values, expert_ids, packing, w_gate, w_up, w_down
    )


def solution(mesh):
    in_specs = (
        P(("groups", "dp", "expert"), None),
        P(("groups", "dp", "expert"), None),
        P(("groups", "dp", "expert"), None),
        P(("groups", "dp", "expert"), None),
        P(("groups", "dp", "expert")),
        P("expert", "dp", None),
        P("expert", "dp", None),
        P("expert", "dp", None),
    )
    out_specs = (
        P(("groups", "dp", "expert"), None),
        P(("groups", "expert"), "dp", None),
        P(("groups", "expert"), "dp", None),
        P(("groups", "expert"), "dp", None),
    )
    return jax.shard_map(local, mesh=mesh, in_specs=in_specs, out_specs=out_specs, check_vma=False)
```

```python
import math

import jax
import jax.numpy as jnp
from jax import lax
from jax.experimental import pallas as pl
from jax.experimental.pallas import tpu as pltpu
from jax.sharding import PartitionSpec as P


def slot_table(route_ids, route_gates, expert_count, capacity):
    row_count, top_count = route_ids.shape
    flat_ids = route_ids.reshape(-1)
    labels = jnp.arange(expert_count, dtype=jnp.int32)
    onehot = (flat_ids[:, None] == labels[None, :]).astype(jnp.int32)
    earlier = jnp.cumsum(onehot, axis=0) - onehot
    rank_in = jnp.sum(earlier * onehot, axis=1)
    position = flat_ids * capacity + rank_in
    places = jnp.arange(expert_count * capacity, dtype=jnp.int32)
    matched = places[:, None] == position[None, :]
    owner_row = jnp.arange(row_count * top_count, dtype=jnp.int32) // top_count
    occupied = jnp.any(matched, axis=1)
    slot_row = jnp.sum(jnp.where(matched, owner_row[None, :], 0), axis=1)
    flat_gates = route_gates.reshape(-1).astype(jnp.float32)
    slot_gate = jnp.sum(jnp.where(matched, flat_gates[None, :], 0.0), axis=1)
    return (position.reshape(row_count, top_count), occupied, slot_row, slot_gate)


def pick_rows(slot_lists, pooled):
    sources = jnp.arange(pooled.shape[0], dtype=jnp.int32)
    choose = (slot_lists[:, None] == sources[None, :]).astype(jnp.bfloat16)
    return jnp.dot(choose, pooled, preferred_element_type=jnp.float32).astype(jnp.bfloat16)


def fill_slots(rebal_rows, rebal_upstream, occupied, slot_row, slot_gate):
    send_rows = jnp.where(occupied[:, None], rebal_rows[slot_row], jnp.zeros((), jnp.bfloat16))
    scaled = slot_gate[:, None] * rebal_upstream[slot_row].astype(jnp.float32)
    send_upstream = jnp.where(occupied[:, None], scaled, 0.0).astype(jnp.bfloat16)
    return (send_rows, send_upstream)


def expert_terms(inputs, upstream, gate_mat, up_mat, down_mat):
    gate_pre = jnp.dot(inputs, gate_mat.T, preferred_element_type=jnp.float32)
    up_pre = jnp.dot(inputs, up_mat.T, preferred_element_type=jnp.float32)
    sigmoid_val = jax.nn.sigmoid(gate_pre)
    activated = gate_pre * sigmoid_val
    hidden = (activated * up_pre).astype(jnp.bfloat16)
    hidden_grad = jnp.dot(upstream, down_mat.T, preferred_element_type=jnp.float32)
    silu_slope = sigmoid_val * (1.0 + gate_pre * (1.0 - sigmoid_val))
    gate_grad = (hidden_grad * up_pre * silu_slope).astype(jnp.bfloat16)
    up_grad = (hidden_grad * activated).astype(jnp.bfloat16)
    weight_grads = (
        jnp.dot(gate_grad.T, inputs, preferred_element_type=jnp.float32).astype(jnp.bfloat16)[None],
        jnp.dot(up_grad.T, inputs, preferred_element_type=jnp.float32).astype(jnp.bfloat16)[None],
        jnp.dot(hidden.T, upstream, preferred_element_type=jnp.float32).astype(jnp.bfloat16)[None],
    )
    partial_grad = jnp.dot(gate_grad, gate_mat, preferred_element_type=jnp.float32)
    partial_grad = partial_grad + jnp.dot(up_grad, up_mat, preferred_element_type=jnp.float32)
    return (weight_grads, partial_grad)


def routed_local(tokens, cotangent, gate_values, expert_ids, packing, w_gate, w_up, w_down):
    row_count, top_count = expert_ids.shape
    model_width = tokens.shape[1]
    dp_size = lax.axis_size("dp")
    expert_count = lax.axis_size("expert") * w_gate.shape[0]
    capacity = min(row_count, max(2, row_count * top_count // expert_count + 1))
    gate_mat = w_gate[0]
    up_mat = w_up[0]
    down_mat = w_down[0]
    pooled_rows, pooled_upstream, pooled_gates = (
        lax.all_gather(tokens, "dp", axis=0, tiled=True),
        lax.all_gather(cotangent, "dp", axis=0, tiled=True),
        lax.all_gather(gate_values, "dp", axis=0, tiled=True),
    )
    lists_all, pooled_ids = (
        lax.all_gather(packing, "dp", axis=0, tiled=True),
        lax.all_gather(expert_ids, "dp", axis=0, tiled=True),
    )
    member_rows = []
    member_upstream = []
    member_positions = []
    for member in range(dp_size):
        low = member * row_count
        slot_lists = lists_all[low : low + row_count]
        position, occupied, slot_row, slot_gate = slot_table(
            pooled_ids[low : low + row_count],
            pooled_gates[low : low + row_count],
            expert_count,
            capacity,
        )
        send_rows, send_upstream = fill_slots(
            pick_rows(slot_lists, pooled_rows),
            pick_rows(slot_lists, pooled_upstream),
            occupied,
            slot_row,
            slot_gate,
        )
        member_rows.append(send_rows.reshape(expert_count, capacity * model_width))
        member_upstream.append(send_upstream.reshape(expert_count, capacity * model_width))
        member_positions.append(position)
    own_position = jnp.stack(member_positions)[lax.axis_index("dp")]
    send_rows = jnp.concatenate(member_rows, axis=1).reshape(
        expert_count * dp_size * capacity, model_width
    )
    send_upstream = jnp.concatenate(member_upstream, axis=1).reshape(
        expert_count * dp_size * capacity, model_width
    )
    recv_rows, recv_upstream = (
        lax.all_to_all(send_rows, "expert", split_axis=0, concat_axis=0, tiled=True),
        lax.all_to_all(send_upstream, "expert", split_axis=0, concat_axis=0, tiled=True),
    )
    weight_grads, partial_grad = expert_terms(recv_rows, recv_upstream, gate_mat, up_mat, down_mat)
    summed = lax.psum_scatter(
        partial_grad.reshape(expert_count, dp_size * capacity * model_width).astype(jnp.bfloat16),
        "dp",
        scatter_dimension=1,
        tiled=True,
    ).astype(jnp.float32)
    slot_grad = summed.reshape(expert_count * capacity, model_width).astype(jnp.bfloat16)
    returned = lax.all_to_all(slot_grad, "expert", split_axis=0, concat_axis=0, tiled=True)
    rebal_grad = jnp.sum(returned[own_position].astype(jnp.float32), axis=1).astype(jnp.bfloat16)
    pooled_grad = lax.all_gather(rebal_grad, "dp", axis=0, tiled=True)
    home_index = lax.axis_index("dp") * row_count + jnp.arange(row_count, dtype=jnp.int32)
    choose = (lists_all[None, :] == home_index[:, None]).astype(jnp.bfloat16)
    input_grad = jnp.dot(choose, pooled_grad, preferred_element_type=jnp.float32).astype(
        jnp.bfloat16
    )
    return (input_grad, weight_grads[0], weight_grads[1], weight_grads[2])


def swap(value):
    return lax.ppermute(value, "dp", [(0, 1), (1, 0)])


def shift_outer(value, count, inner, step):
    return lax.ppermute(
        value, "expert", [(place, (place + step * inner) % count) for place in range(count)]
    )


def swap_inner(value, count, partner):
    return lax.ppermute(value, "expert", [(place, place ^ partner) for place in range(count)])


VMEM = pl.BlockSpec(memory_space=pltpu.VMEM)
SMEM = pl.BlockSpec(memory_space=pltpu.SMEM)
NT = (((1,), (1,)), ((), ()))
TN = (((0,), (0,)), ((), ()))


def on_chip(body, outs, *args, scalars=0, flops=0):
    moved = sum(arg.size * arg.dtype.itemsize for arg in args)
    moved += sum(math.prod(shape) * jnp.dtype(dtype).itemsize for shape, dtype in outs)
    return pl.pallas_call(
        body,
        out_shape=[jax.ShapeDtypeStruct(shape, dtype) for shape, dtype in outs],
        in_specs=[SMEM] * scalars + [VMEM] * (len(args) - scalars),
        out_specs=[VMEM] * len(outs),
        compiler_params=pltpu.CompilerParams(vmem_limit_bytes=2 * moved + (8 << 20)),
        cost_estimate=pl.CostEstimate(flops=flops, bytes_accessed=moved, transcendentals=0),
    )(*args)


def stack_kernel(*refs):
    low = 0
    for ref in refs[:-1]:
        refs[-1][low : low + ref.shape[0], :] = ref[...]
        low += ref.shape[0]


def stack(blocks):
    rows = sum(block.shape[0] for block in blocks)
    return on_chip(stack_kernel, [((rows, blocks[0].shape[1]), blocks[0].dtype)], *blocks)[0]


def table_kernel(ids_ref, gates_ref, packing_ref, table_ref):
    slots = packing_ref.shape[1]
    count = table_ref.shape[0] - 16
    labels = lax.broadcasted_iota(jnp.int32, (count, slots), 0)
    total = jnp.zeros((count, slots), jnp.float32)
    for k in range(ids_ref.shape[0]):
        named = labels == ids_ref[k : k + 1, :]
        total = total + jnp.where(named, gates_ref[k : k + 1, :].astype(jnp.float32), 0.0)
    table_ref[:count, :] = total.astype(jnp.bfloat16)
    lists = jnp.broadcast_to(packing_ref[...], (16, slots)).astype(jnp.float32)
    table_ref[count:, :] = lists.astype(jnp.bfloat16)


def payload_kernel(place_ref, table_ref, other_ref, cotangent_ref, payload_ref):
    rows, width = cotangent_ref.shape
    count = table_ref.shape[0] - 16
    slots = table_ref.shape[1]
    homes = lax.broadcasted_iota(jnp.int32, (rows, slots), 0) + place_ref[0] * rows
    gates = jnp.zeros((rows, count), jnp.float32)
    for ref in (table_ref, other_ref):
        lists = ref[count:, :].astype(jnp.float32)[:1, :]
        matched = (lists == homes.astype(jnp.float32)).astype(jnp.float32).astype(jnp.bfloat16)
        gates = gates + lax.dot_general(
            matched, ref[:count, :], NT, preferred_element_type=jnp.float32
        )
    payload_ref[:, :width] = cotangent_ref[...]
    payload_ref[:, width:] = jnp.zeros((rows, payload_ref.shape[1] - width), jnp.bfloat16)
    payload_ref[:, width : width + count] = gates.astype(jnp.bfloat16)


def pre_kernel(own_ref, other_ref, *refs):
    pieces, rows_ref, outs = refs[:-5], refs[-5], refs[-4:]
    stack_kernel(*pieces, rows_ref)
    half = own_ref.shape[0] // 3
    rows = rows_ref[...]
    for index, weights in enumerate((own_ref, other_ref)):
        for kind in range(2):
            outs[2 * index + kind][...] = lax.dot_general(
                rows,
                weights[kind * half : (kind + 1) * half, :],
                NT,
                preferred_element_type=jnp.float32,
            )


def grad_kernel(place_ref, own_ref, other_ref, *refs):
    pre, pieces = refs[:4], refs[4:-7]
    rows_ref, own_grads_ref, sent_grads_ref, *blocks = refs[-7:]
    half = own_ref.shape[0] // 3
    height, width = rows_ref.shape
    gate = []
    low = 0
    for ref in pieces:
        rows_ref[low : low + ref.shape[0], :] = ref[:, :width]
        low += ref.shape[0]
        gates = ref[:, width:].astype(jnp.float32)
        lanes = lax.broadcasted_iota(jnp.int32, gates.shape, 1)
        gate.append(jnp.sum(jnp.where(lanes == place_ref[0], gates, 0.0), axis=1, keepdims=True))
    gate = jnp.concatenate(gate, axis=0)
    upstream = rows_ref[...]
    both = []
    for index, (weights, grads_ref) in enumerate(
        ((own_ref, own_grads_ref), (other_ref, sent_grads_ref))
    ):
        hidden_grad = gate * lax.dot_general(
            upstream, weights[2 * half :, :], NT, preferred_element_type=jnp.float32
        )
        gate_pre, up_pre = pre[2 * index][...], pre[2 * index + 1][...]
        sigmoid_val = 1.0 / (1.0 + jnp.exp(-gate_pre))
        activated = gate_pre * sigmoid_val
        silu_slope = sigmoid_val * (1.0 + gate_pre * (1.0 - sigmoid_val))
        gate_grad = (hidden_grad * up_pre * silu_slope).astype(jnp.bfloat16)
        up_grad = (hidden_grad * activated).astype(jnp.bfloat16)
        grads_ref[:height, :] = gate_grad
        grads_ref[height : 2 * height, :] = up_grad
        grads_ref[2 * height :, :] = (gate * activated * up_pre).astype(jnp.bfloat16)
        both.append(jnp.concatenate([gate_grad, up_grad], axis=1))
    depth = height // len(blocks)
    step = min(width, 512)
    for left in range(0, width, step):
        columns = slice(left, left + step)
        term = jnp.dot(
            both[0], own_ref[: 2 * half, columns], preferred_element_type=jnp.float32
        ) + jnp.dot(both[1], other_ref[: 2 * half, columns], preferred_element_type=jnp.float32)
        for index, block in enumerate(blocks):
            rows = term[index * depth : (index + 1) * depth]
            block[:, columns] = rows.astype(jnp.bfloat16)


def column_kernel(*refs):
    blocks, own_ref, sent = refs[:4], refs[4], refs[5:]
    total = blocks[0][...].astype(jnp.float32)
    for block in blocks[1:]:
        total = total + block[...].astype(jnp.float32)
    depth = own_ref.shape[0]
    own_ref[...] = total[:depth]
    for index, ref in enumerate(sent):
        ref[...] = total[(index + 1) * depth : (index + 2) * depth].astype(jnp.bfloat16)


def sum_kernel(own_ref, *refs):
    total = own_ref[...]
    for ref in refs[:-1]:
        total = total + ref[...].astype(jnp.float32)
    refs[-1][...] = total.astype(jnp.bfloat16)


def weight_kernel(own_grads, other_grads, rows, other_rows, upstream, other_upstream, *outs):
    height = rows.shape[0]
    for index, out in enumerate(outs):
        own, other = (upstream, other_upstream) if index == 2 else (rows, other_rows)
        span = slice(index * height, (index + 1) * height)
        step = min(out.shape[-1], 1024)
        for left in range(0, out.shape[-1], step):
            columns = slice(left, left + step)
            total = lax.dot_general(
                own_grads[span, :], own[:, columns], TN, preferred_element_type=jnp.float32
            ) + lax.dot_general(
                other_grads[span, :], other[:, columns], TN, preferred_element_type=jnp.float32
            )
            out[0, :, columns] = total.astype(jnp.bfloat16)


def along_outer(value, count, inner):
    return [value] + [shift_outer(value, count, inner, step) for step in range(1, count // inner)]


def across_inner(column, count):
    cut = column.shape[0] // 2
    first = swap_inner(column, count, 1)
    second = swap_inner(column, count, 2)
    far_top = swap_inner(first[:cut], count, 2)
    far_bottom = swap_inner(second[cut:], count, 1)
    return [column, first, second, far_top, far_bottom]


def dense_local(tokens, cotangent, gate_values, expert_ids, packing, w_gate, w_up, w_down):
    row_count, model_width = tokens.shape
    half = w_gate.shape[1]
    count = lax.axis_size("expert")
    inner = 4
    outer = count // inner
    height = row_count * count
    low, wide = jnp.bfloat16, jnp.float32
    dp_place = lax.axis_index("dp").reshape(1)
    place = lax.axis_index("expert").reshape(1)

    token_blocks = along_outer(tokens, count, inner)
    (table,) = on_chip(
        table_kernel,
        [((count + 16, row_count), low)],
        expert_ids.T,
        gate_values.T,
        packing.reshape(1, row_count),
    )
    other_table = swap(table)
    own_weights = jnp.concatenate([w_gate[0], w_up[0], w_down[0]], axis=0)
    own_weights, other_table = lax.optimization_barrier((own_weights, other_table))
    other_weights = swap(own_weights)
    (payload,) = on_chip(
        payload_kernel,
        [((row_count, model_width + 128), low)],
        dp_place,
        table,
        other_table,
        cotangent,
        scalars=1,
    )
    payload, token_blocks[1] = lax.optimization_barrier((payload, token_blocks[1]))
    token_columns = across_inner(stack(token_blocks), count)
    upstream_columns = across_inner(stack(along_outer(payload, count, inner)), count)

    inputs, *pre = on_chip(
        pre_kernel,
        [((height, model_width), low)] + [((height, half), wide)] * 4,
        own_weights,
        other_weights,
        *token_columns,
        flops=8 * height * half * model_width,
    )
    other_inputs = swap(inputs)
    upstream, own_grads, sent_grads, *blocks = on_chip(
        grad_kernel,
        [((height, model_width), low)]
        + [((3 * height, half), low)] * 2
        + [((height // inner, model_width), low)] * inner,
        place,
        own_weights,
        other_weights,
        *pre,
        *upstream_columns,
        scalars=1,
        flops=12 * height * half * model_width,
    )
    *blocks, other_inputs = lax.optimization_barrier((*blocks, other_inputs))
    returned = [swap_inner(blocks[partner], count, partner) for partner in range(1, inner)]
    other_grads = swap(sent_grads)
    other_upstream = swap(upstream)
    own, *sent = on_chip(
        column_kernel,
        [((row_count, model_width), wide)] + [((row_count, model_width), low)] * (outer - 1),
        blocks[0],
        *returned,
    )
    own, *sent, other_grads, other_upstream = lax.optimization_barrier(
        (own, *sent, other_grads, other_upstream)
    )
    back = [shift_outer(sent[step - 1], count, inner, -step) for step in range(1, outer)]
    weight_grads = on_chip(
        weight_kernel,
        [((1, half, model_width), low)] * 3,
        own_grads,
        other_grads,
        inputs,
        other_inputs,
        upstream,
        other_upstream,
        flops=12 * height * half * model_width,
    )
    (input_grad,) = on_chip(sum_kernel, [((row_count, model_width), low)], own, *back)
    return (input_grad, *weight_grads)


def local(tokens, cotangent, gate_values, expert_ids, packing, w_gate, w_up, w_down):
    row_count, top = expert_ids.shape
    count = lax.axis_size("expert")
    expert_count = count * w_gate.shape[0]
    capacity = min(row_count, max(2, row_count * top // expert_count + 1))
    few = capacity * 4 <= row_count
    regular = lax.axis_size("dp") == 2 and count % 4 == 0 and w_gate.shape[0] == 1
    chosen = dense_local if regular and not few else routed_local
    return chosen(
        tokens, cotangent, gate_values, expert_ids, packing, w_gate, w_up, w_down
    )


def solution(mesh):
    in_specs = (
        P(("groups", "dp", "expert"), None),
        P(("groups", "dp", "expert"), None),
        P(("groups", "dp", "expert"), None),
        P(("groups", "dp", "expert"), None),
        P(("groups", "dp", "expert")),
        P("expert", "dp", None),
        P("expert", "dp", None),
        P("expert", "dp", None),
    )
    out_specs = (
        P(("groups", "dp", "expert"), None),
        P(("groups", "expert"), "dp", None),
        P(("groups", "expert"), "dp", None),
        P(("groups", "expert"), "dp", None),
    )
    return jax.shard_map(local, mesh=mesh, in_specs=in_specs, out_specs=out_specs, check_vma=False)
```

```python
import math

import jax
import jax.numpy as jnp
from jax import lax
from jax.experimental import pallas as pl
from jax.experimental.pallas import tpu as pltpu
from jax.sharding import PartitionSpec as P


def slot_table(route_ids, route_gates, expert_count, capacity):
    row_count, top_count = route_ids.shape
    flat_ids = route_ids.reshape(-1)
    labels = jnp.arange(expert_count, dtype=jnp.int32)
    onehot = (flat_ids[:, None] == labels[None, :]).astype(jnp.int32)
    earlier = jnp.cumsum(onehot, axis=0) - onehot
    rank_in = jnp.sum(earlier * onehot, axis=1)
    position = flat_ids * capacity + rank_in
    places = jnp.arange(expert_count * capacity, dtype=jnp.int32)
    matched = places[:, None] == position[None, :]
    owner_row = jnp.arange(row_count * top_count, dtype=jnp.int32) // top_count
    occupied = jnp.any(matched, axis=1)
    slot_row = jnp.sum(jnp.where(matched, owner_row[None, :], 0), axis=1)
    flat_gates = route_gates.reshape(-1).astype(jnp.float32)
    slot_gate = jnp.sum(jnp.where(matched, flat_gates[None, :], 0.0), axis=1)
    return (position.reshape(row_count, top_count), occupied, slot_row, slot_gate)


def pick_rows(slot_lists, pooled):
    sources = jnp.arange(pooled.shape[0], dtype=jnp.int32)
    choose = (slot_lists[:, None] == sources[None, :]).astype(jnp.bfloat16)
    return jnp.dot(choose, pooled, preferred_element_type=jnp.float32).astype(jnp.bfloat16)


def fill_slots(rebal_rows, rebal_upstream, occupied, slot_row, slot_gate):
    send_rows = jnp.where(occupied[:, None], rebal_rows[slot_row], jnp.zeros((), jnp.bfloat16))
    scaled = slot_gate[:, None] * rebal_upstream[slot_row].astype(jnp.float32)
    send_upstream = jnp.where(occupied[:, None], scaled, 0.0).astype(jnp.bfloat16)
    return (send_rows, send_upstream)


def expert_terms(inputs, upstream, gate_mat, up_mat, down_mat):
    gate_pre = jnp.dot(inputs, gate_mat.T, preferred_element_type=jnp.float32)
    up_pre = jnp.dot(inputs, up_mat.T, preferred_element_type=jnp.float32)
    sigmoid_val = jax.nn.sigmoid(gate_pre)
    activated = gate_pre * sigmoid_val
    hidden = (activated * up_pre).astype(jnp.bfloat16)
    hidden_grad = jnp.dot(upstream, down_mat.T, preferred_element_type=jnp.float32)
    silu_slope = sigmoid_val * (1.0 + gate_pre * (1.0 - sigmoid_val))
    gate_grad = (hidden_grad * up_pre * silu_slope).astype(jnp.bfloat16)
    up_grad = (hidden_grad * activated).astype(jnp.bfloat16)
    weight_grads = (
        jnp.dot(gate_grad.T, inputs, preferred_element_type=jnp.float32).astype(jnp.bfloat16)[None],
        jnp.dot(up_grad.T, inputs, preferred_element_type=jnp.float32).astype(jnp.bfloat16)[None],
        jnp.dot(hidden.T, upstream, preferred_element_type=jnp.float32).astype(jnp.bfloat16)[None],
    )
    partial_grad = jnp.dot(gate_grad, gate_mat, preferred_element_type=jnp.float32)
    partial_grad = partial_grad + jnp.dot(up_grad, up_mat, preferred_element_type=jnp.float32)
    return (weight_grads, partial_grad)


def routed_local(tokens, cotangent, gate_values, expert_ids, packing, w_gate, w_up, w_down):
    row_count, top_count = expert_ids.shape
    model_width = tokens.shape[1]
    dp_size = lax.axis_size("dp")
    expert_count = lax.axis_size("expert") * w_gate.shape[0]
    capacity = min(row_count, max(2, row_count * top_count // expert_count + 1))
    gate_mat = w_gate[0]
    up_mat = w_up[0]
    down_mat = w_down[0]
    pooled_rows, pooled_upstream, pooled_gates = (
        lax.all_gather(tokens, "dp", axis=0, tiled=True),
        lax.all_gather(cotangent, "dp", axis=0, tiled=True),
        lax.all_gather(gate_values, "dp", axis=0, tiled=True),
    )
    lists_all, pooled_ids = (
        lax.all_gather(packing, "dp", axis=0, tiled=True),
        lax.all_gather(expert_ids, "dp", axis=0, tiled=True),
    )
    member_rows = []
    member_upstream = []
    member_positions = []
    for member in range(dp_size):
        low = member * row_count
        slot_lists = lists_all[low : low + row_count]
        position, occupied, slot_row, slot_gate = slot_table(
            pooled_ids[low : low + row_count],
            pooled_gates[low : low + row_count],
            expert_count,
            capacity,
        )
        send_rows, send_upstream = fill_slots(
            pick_rows(slot_lists, pooled_rows),
            pick_rows(slot_lists, pooled_upstream),
            occupied,
            slot_row,
            slot_gate,
        )
        member_rows.append(send_rows.reshape(expert_count, capacity * model_width))
        member_upstream.append(send_upstream.reshape(expert_count, capacity * model_width))
        member_positions.append(position)
    own_position = jnp.stack(member_positions)[lax.axis_index("dp")]
    send_rows = jnp.concatenate(member_rows, axis=1).reshape(
        expert_count * dp_size * capacity, model_width
    )
    send_upstream = jnp.concatenate(member_upstream, axis=1).reshape(
        expert_count * dp_size * capacity, model_width
    )
    recv_rows, recv_upstream = (
        lax.all_to_all(send_rows, "expert", split_axis=0, concat_axis=0, tiled=True),
        lax.all_to_all(send_upstream, "expert", split_axis=0, concat_axis=0, tiled=True),
    )
    weight_grads, partial_grad = expert_terms(recv_rows, recv_upstream, gate_mat, up_mat, down_mat)
    summed = lax.psum_scatter(
        partial_grad.reshape(expert_count, dp_size * capacity * model_width).astype(jnp.bfloat16),
        "dp",
        scatter_dimension=1,
        tiled=True,
    ).astype(jnp.float32)
    slot_grad = summed.reshape(expert_count * capacity, model_width).astype(jnp.bfloat16)
    returned = lax.all_to_all(slot_grad, "expert", split_axis=0, concat_axis=0, tiled=True)
    rebal_grad = jnp.sum(returned[own_position].astype(jnp.float32), axis=1).astype(jnp.bfloat16)
    pooled_grad = lax.all_gather(rebal_grad, "dp", axis=0, tiled=True)
    home_index = lax.axis_index("dp") * row_count + jnp.arange(row_count, dtype=jnp.int32)
    choose = (lists_all[None, :] == home_index[:, None]).astype(jnp.bfloat16)
    input_grad = jnp.dot(choose, pooled_grad, preferred_element_type=jnp.float32).astype(
        jnp.bfloat16
    )
    return (input_grad, weight_grads[0], weight_grads[1], weight_grads[2])


def swap(value):
    return lax.ppermute(value, "dp", [(0, 1), (1, 0)])


def shift_outer(value, count, inner, step):
    return lax.ppermute(
        value, "expert", [(place, (place + step * inner) % count) for place in range(count)]
    )


def swap_inner(value, count, partner):
    return lax.ppermute(value, "expert", [(place, place ^ partner) for place in range(count)])


VMEM = pl.BlockSpec(memory_space=pltpu.VMEM)
SMEM = pl.BlockSpec(memory_space=pltpu.SMEM)
NT = (((1,), (1,)), ((), ()))
LANES = 128


def on_chip(body, outs, *args, scalars=0):
    moved = sum(arg.size * arg.dtype.itemsize for arg in args)
    moved += sum(math.prod(shape) * jnp.dtype(dtype).itemsize for shape, dtype in outs)
    return pl.pallas_call(
        body,
        out_shape=[jax.ShapeDtypeStruct(shape, dtype) for shape, dtype in outs],
        in_specs=[SMEM] * scalars + [VMEM] * (len(args) - scalars),
        out_specs=[VMEM] * len(outs),
        compiler_params=pltpu.CompilerParams(vmem_limit_bytes=moved + (4 << 20)),
        cost_estimate=pl.CostEstimate(flops=0, bytes_accessed=moved, transcendentals=0),
    )(*args)


def stack_kernel(*refs):
    low = 0
    for ref in refs[:-1]:
        refs[-1][low : low + ref.shape[0], :] = ref[...]
        low += ref.shape[0]


def stack(blocks):
    rows = sum(block.shape[0] for block in blocks)
    return on_chip(stack_kernel, [((rows, blocks[0].shape[1]), blocks[0].dtype)], *blocks)[0]


def table_kernel(ids_ref, gates_ref, packing_ref, table_ref):
    slots = packing_ref.shape[1]
    count = table_ref.shape[0] - 16
    labels = lax.broadcasted_iota(jnp.int32, (count, slots), 0)
    total = jnp.zeros((count, slots), jnp.float32)
    for k in range(ids_ref.shape[0]):
        named = labels == ids_ref[k : k + 1, :]
        total = total + jnp.where(named, gates_ref[k : k + 1, :].astype(jnp.float32), 0.0)
    table_ref[:count, :] = total.astype(jnp.bfloat16)
    lists = jnp.broadcast_to(packing_ref[...], (16, slots)).astype(jnp.float32)
    table_ref[count:, :] = lists.astype(jnp.bfloat16)


def first_kernel(tokens_ref, cotangent_ref, out_ref):
    width = tokens_ref.shape[1]
    out_ref[:, :width] = tokens_ref[...]
    out_ref[:, width:] = cotangent_ref[:, : out_ref.shape[1] - width]


def second_kernel(place_ref, table_ref, other_ref, cotangent_ref, out_ref):
    rows, slots = cotangent_ref.shape[0], table_ref.shape[1]
    count = table_ref.shape[0] - 16
    width = out_ref.shape[1] - LANES
    homes = lax.broadcasted_iota(jnp.int32, (rows, slots), 0) + place_ref[0] * rows
    gates = jnp.zeros((rows, count), jnp.float32)
    for ref in (table_ref, other_ref):
        lists = ref[count:, :].astype(jnp.float32)[:1, :]
        matched = (lists == homes.astype(jnp.float32)).astype(jnp.float32).astype(jnp.bfloat16)
        gates = gates + lax.dot_general(
            matched, ref[:count, :], NT, preferred_element_type=jnp.float32
        )
    out_ref[:, :width] = cotangent_ref[:, cotangent_ref.shape[1] - width :]
    out_ref[:, width:] = jnp.zeros((rows, LANES), jnp.bfloat16)
    out_ref[:, width : width + count] = gates.astype(jnp.bfloat16)


def gather_kernel(place_ref, *refs):
    first, second, rows_ref, gate_ref = refs[:5], refs[5:-2], refs[-2], refs[-1]
    low = 0
    left = first[0].shape[1]
    for ref in first:
        rows_ref[low : low + ref.shape[0], :left] = ref[...]
        low += ref.shape[0]
    width = second[0].shape[1] - LANES
    column = first[0].shape[0]
    depth = column // len(second)
    for step, ref in enumerate(second):
        gates = ref[:, width:].astype(jnp.float32)
        lanes = lax.broadcasted_iota(jnp.int32, gates.shape, 1)
        gate = jnp.sum(jnp.where(lanes == place_ref[0], gates, 0.0), axis=1, keepdims=True)
        for partner in range(ref.shape[0] // depth):
            block = slice(partner * depth, (partner + 1) * depth)
            low = partner * column + step * depth
            rows_ref[low : low + depth, left:] = ref[block, :width]
            gate_ref[low : low + depth, :] = gate[block]


def split_kernel(first_ref, second_ref, *outs):
    first, second = outs[:3], outs[3:]
    column = first[0].shape[0]
    depth = column // len(second)
    for partner, out in enumerate(first):
        out[...] = first_ref[(partner + 1) * column : (partner + 2) * column, :]
    for step, out in enumerate(second):
        for partner in range(out.shape[0] // depth):
            low = partner * column + step * depth
            out[partner * depth : (partner + 1) * depth, :] = second_ref[low : low + depth, :]


def column_kernel(*refs):
    own_ref, sent = refs[4], refs[5:]
    depth = own_ref.shape[0]
    total = refs[0][: depth * (len(sent) + 1), :].astype(jnp.float32)
    for block in refs[1:4]:
        total = total + block[...].astype(jnp.float32)
    own_ref[...] = total[:depth]
    for index, ref in enumerate(sent):
        ref[...] = total[(index + 1) * depth : (index + 2) * depth].astype(jnp.bfloat16)


def sum_kernel(*refs):
    inputs, out_ref = refs[:-1], refs[-1]
    half = len(inputs) // 2
    low = 0
    for part in (inputs[:half], inputs[half:]):
        total = part[0][...]
        for ref in part[1:]:
            total = total + ref[...].astype(jnp.float32)
        out_ref[:, low : low + total.shape[1]] = total.astype(jnp.bfloat16)
        low += total.shape[1]


def along_outer(value, count, inner):
    return [value] + [shift_outer(value, count, inner, step) for step in range(1, count // inner)]


def across_inner(column, count):
    cut = column.shape[0] // 2
    first = swap_inner(column, count, 1)
    second = swap_inner(column, count, 2)
    far_top = swap_inner(first[:cut], count, 2)
    far_bottom = swap_inner(second[cut:], count, 1)
    return [column, first, second, far_top, far_bottom]


def dense_local(tokens, cotangent, gate_values, expert_ids, packing, w_gate, w_up, w_down):
    row_count, model_width = tokens.shape
    half = w_gate.shape[1]
    count = lax.axis_size("expert")
    inner = outer = 4
    height = row_count * count
    column = row_count * outer
    low, wide = jnp.bfloat16, jnp.float32
    dp_place = lax.axis_index("dp").reshape(1)
    place = lax.axis_index("expert").reshape(1)
    sent_late = model_width // 2
    back_late = model_width // 4
    early = 2 * model_width - sent_late
    back_early = model_width - back_late

    (first,) = on_chip(first_kernel, [((row_count, early), low)], tokens, cotangent)
    first_blocks = along_outer(first, count, inner)
    (table,) = on_chip(
        table_kernel,
        [((count + 16, row_count), low)],
        expert_ids.T,
        gate_values.T,
        packing.reshape(1, row_count),
    )
    other_table = swap(table)
    (second,) = on_chip(
        second_kernel,
        [((row_count, sent_late + LANES), low)],
        dp_place,
        table,
        other_table,
        cotangent,
        scalars=1,
    )
    second_plane = stack(
        [second] + [swap_inner(second, count, partner) for partner in range(1, inner)]
    )
    own_weights = jnp.concatenate([w_gate[0], w_up[0], w_down[0]], axis=0)
    first_column = stack(first_blocks)
    own_weights, first_column = lax.optimization_barrier((own_weights, first_column))
    other = swap(own_weights)
    first_pieces = across_inner(first_column, count)
    second_pieces = along_outer(second_plane, count, inner)
    rows, gate = on_chip(
        gather_kernel,
        [((height, 2 * model_width), low), ((height, 1), wide)],
        place,
        *first_pieces,
        *second_pieces,
        scalars=1,
    )
    other_rows = swap(rows)
    inputs, upstream = rows[:, :model_width], rows[:, model_width:]

    gate_up = jnp.concatenate([w_gate[0], other[:half], w_up[0], other[half : 2 * half]], axis=0)
    down = jnp.concatenate([w_down[0], other[2 * half :]], axis=0)
    pre = jnp.dot(inputs, gate_up.T, preferred_element_type=wide)
    gate_pre, up_pre = pre[:, : 2 * half], pre[:, 2 * half :]
    hidden_grad = gate * jnp.dot(upstream, down.T, preferred_element_type=wide)
    sigmoid_val = jax.nn.sigmoid(gate_pre)
    activated = gate_pre * sigmoid_val
    hidden = (gate * activated * up_pre).astype(low)
    silu_slope = sigmoid_val * (1.0 + gate_pre * (1.0 - sigmoid_val))
    gate_grad = (hidden_grad * up_pre * silu_slope).astype(low)
    up_grad = (hidden_grad * activated).astype(low)
    both_grad = jnp.concatenate([gate_grad, up_grad], axis=1)
    terms = [
        jnp.dot(both_grad, gate_up[:, columns], preferred_element_type=wide).astype(low)
        for columns in (slice(0, back_early), slice(back_early, None))
    ]
    blocks = on_chip(
        split_kernel,
        [((column, back_early), low)] * (inner - 1) + [((column, back_late), low)] * outer,
        *terms,
    )
    early_back = [
        swap_inner(block, count, partner + 1) for partner, block in enumerate(blocks[: inner - 1])
    ]
    late_blocks = blocks[inner - 1 :]
    late_back = [
        shift_outer(late_blocks[step], count, inner, -step) for step in range(1, outer)
    ]
    grads = (gate_grad, up_grad, hidden)
    own_grads = jnp.concatenate([grad[:, :half] for grad in grads], axis=1)
    sent_grads = jnp.concatenate([grad[:, half:] for grad in grads], axis=1)
    sent_grads, *blocks = lax.optimization_barrier((sent_grads, *blocks))
    other_grads = swap(sent_grads)
    early_own, *early_sent = on_chip(
        column_kernel,
        [((row_count, back_early), wide)] + [((row_count, back_early), low)] * (outer - 1),
        terms[0],
        *early_back,
    )
    late_own, *late_sent = on_chip(
        column_kernel,
        [((row_count, back_late), wide)] + [((row_count, back_late), low)] * (inner - 1),
        late_blocks[0],
        *late_back,
    )
    early_sent[0], other_grads, other_rows = lax.optimization_barrier(
        (early_sent[0], other_grads, other_rows)
    )
    early_parts = [
        shift_outer(block, count, inner, -step - 1) for step, block in enumerate(early_sent)
    ]
    late_parts = [
        swap_inner(block, count, partner + 1) for partner, block in enumerate(late_sent)
    ]
    weight_grads = []
    for index, span in enumerate((slice(0, model_width),) * 2 + (slice(model_width, None),)):
        part = slice(index * half, (index + 1) * half)
        total = jnp.dot(own_grads[:, part].T, rows[:, span], preferred_element_type=wide)
        total = total + jnp.dot(
            other_grads[:, part].T, other_rows[:, span], preferred_element_type=wide
        )
        weight_grads.append(total.astype(low)[None])
    (input_grad,) = on_chip(
        sum_kernel,
        [((row_count, model_width), low)],
        early_own,
        *early_parts,
        late_own,
        *late_parts,
    )
    return (input_grad, *weight_grads)


def local(tokens, cotangent, gate_values, expert_ids, packing, w_gate, w_up, w_down):
    row_count, top = expert_ids.shape
    count = lax.axis_size("expert")
    expert_count = count * w_gate.shape[0]
    capacity = min(row_count, max(2, row_count * top // expert_count + 1))
    few = capacity * 4 <= row_count
    regular = lax.axis_size("dp") == 2 and count == 16 and w_gate.shape[0] == 1
    chosen = dense_local if regular and not few else routed_local
    return chosen(
        tokens, cotangent, gate_values, expert_ids, packing, w_gate, w_up, w_down
    )


def solution(mesh):
    in_specs = (
        P(("groups", "dp", "expert"), None),
        P(("groups", "dp", "expert"), None),
        P(("groups", "dp", "expert"), None),
        P(("groups", "dp", "expert"), None),
        P(("groups", "dp", "expert")),
        P("expert", "dp", None),
        P("expert", "dp", None),
        P("expert", "dp", None),
    )
    out_specs = (
        P(("groups", "dp", "expert"), None),
        P(("groups", "expert"), "dp", None),
        P(("groups", "expert"), "dp", None),
        P(("groups", "expert"), "dp", None),
    )
    return jax.shard_map(local, mesh=mesh, in_specs=in_specs, out_specs=out_specs, check_vma=False)
```

```python
import math

import jax
import jax.numpy as jnp
from jax import lax
from jax.experimental import pallas as pl
from jax.experimental.pallas import tpu as pltpu
from jax.sharding import PartitionSpec as P


def slot_table(route_ids, route_gates, expert_count, capacity):
    row_count, top_count = route_ids.shape
    flat_ids = route_ids.reshape(-1)
    labels = jnp.arange(expert_count, dtype=jnp.int32)
    onehot = (flat_ids[:, None] == labels[None, :]).astype(jnp.int32)
    earlier = jnp.cumsum(onehot, axis=0) - onehot
    rank_in = jnp.sum(earlier * onehot, axis=1)
    position = flat_ids * capacity + rank_in
    places = jnp.arange(expert_count * capacity, dtype=jnp.int32)
    matched = places[:, None] == position[None, :]
    owner_row = jnp.arange(row_count * top_count, dtype=jnp.int32) // top_count
    occupied = jnp.any(matched, axis=1)
    slot_row = jnp.sum(jnp.where(matched, owner_row[None, :], 0), axis=1)
    flat_gates = route_gates.reshape(-1).astype(jnp.float32)
    slot_gate = jnp.sum(jnp.where(matched, flat_gates[None, :], 0.0), axis=1)
    return (position.reshape(row_count, top_count), occupied, slot_row, slot_gate)


def pick_rows(slot_lists, pooled):
    sources = jnp.arange(pooled.shape[0], dtype=jnp.int32)
    choose = (slot_lists[:, None] == sources[None, :]).astype(jnp.bfloat16)
    return jnp.dot(choose, pooled, preferred_element_type=jnp.float32).astype(jnp.bfloat16)


def fill_slots(rebal_rows, rebal_upstream, occupied, slot_row, slot_gate):
    send_rows = jnp.where(occupied[:, None], rebal_rows[slot_row], jnp.zeros((), jnp.bfloat16))
    scaled = slot_gate[:, None] * rebal_upstream[slot_row].astype(jnp.float32)
    send_upstream = jnp.where(occupied[:, None], scaled, 0.0).astype(jnp.bfloat16)
    return (send_rows, send_upstream)


def expert_terms(inputs, upstream, gate_mat, up_mat, down_mat):
    gate_pre = jnp.dot(inputs, gate_mat.T, preferred_element_type=jnp.float32)
    up_pre = jnp.dot(inputs, up_mat.T, preferred_element_type=jnp.float32)
    sigmoid_val = jax.nn.sigmoid(gate_pre)
    activated = gate_pre * sigmoid_val
    hidden = (activated * up_pre).astype(jnp.bfloat16)
    hidden_grad = jnp.dot(upstream, down_mat.T, preferred_element_type=jnp.float32)
    silu_slope = sigmoid_val * (1.0 + gate_pre * (1.0 - sigmoid_val))
    gate_grad = (hidden_grad * up_pre * silu_slope).astype(jnp.bfloat16)
    up_grad = (hidden_grad * activated).astype(jnp.bfloat16)
    weight_grads = (
        jnp.dot(gate_grad.T, inputs, preferred_element_type=jnp.float32).astype(jnp.bfloat16)[None],
        jnp.dot(up_grad.T, inputs, preferred_element_type=jnp.float32).astype(jnp.bfloat16)[None],
        jnp.dot(hidden.T, upstream, preferred_element_type=jnp.float32).astype(jnp.bfloat16)[None],
    )
    partial_grad = jnp.dot(gate_grad, gate_mat, preferred_element_type=jnp.float32)
    partial_grad = partial_grad + jnp.dot(up_grad, up_mat, preferred_element_type=jnp.float32)
    return (weight_grads, partial_grad)


def routed_local(tokens, cotangent, gate_values, expert_ids, packing, w_gate, w_up, w_down):
    row_count, top_count = expert_ids.shape
    model_width = tokens.shape[1]
    dp_size = lax.axis_size("dp")
    expert_count = lax.axis_size("expert") * w_gate.shape[0]
    capacity = min(row_count, max(2, row_count * top_count // expert_count + 1))
    gate_mat = w_gate[0]
    up_mat = w_up[0]
    down_mat = w_down[0]
    pooled_rows, pooled_upstream, pooled_gates = (
        lax.all_gather(tokens, "dp", axis=0, tiled=True),
        lax.all_gather(cotangent, "dp", axis=0, tiled=True),
        lax.all_gather(gate_values, "dp", axis=0, tiled=True),
    )
    lists_all, pooled_ids = (
        lax.all_gather(packing, "dp", axis=0, tiled=True),
        lax.all_gather(expert_ids, "dp", axis=0, tiled=True),
    )
    member_rows = []
    member_upstream = []
    member_positions = []
    for member in range(dp_size):
        low = member * row_count
        slot_lists = lists_all[low : low + row_count]
        position, occupied, slot_row, slot_gate = slot_table(
            pooled_ids[low : low + row_count],
            pooled_gates[low : low + row_count],
            expert_count,
            capacity,
        )
        send_rows, send_upstream = fill_slots(
            pick_rows(slot_lists, pooled_rows),
            pick_rows(slot_lists, pooled_upstream),
            occupied,
            slot_row,
            slot_gate,
        )
        member_rows.append(send_rows.reshape(expert_count, capacity * model_width))
        member_upstream.append(send_upstream.reshape(expert_count, capacity * model_width))
        member_positions.append(position)
    own_position = jnp.stack(member_positions)[lax.axis_index("dp")]
    send_rows = jnp.concatenate(member_rows, axis=1).reshape(
        expert_count * dp_size * capacity, model_width
    )
    send_upstream = jnp.concatenate(member_upstream, axis=1).reshape(
        expert_count * dp_size * capacity, model_width
    )
    recv_rows, recv_upstream = (
        lax.all_to_all(send_rows, "expert", split_axis=0, concat_axis=0, tiled=True),
        lax.all_to_all(send_upstream, "expert", split_axis=0, concat_axis=0, tiled=True),
    )
    weight_grads, partial_grad = expert_terms(recv_rows, recv_upstream, gate_mat, up_mat, down_mat)
    summed = lax.psum_scatter(
        partial_grad.reshape(expert_count, dp_size * capacity * model_width).astype(jnp.bfloat16),
        "dp",
        scatter_dimension=1,
        tiled=True,
    ).astype(jnp.float32)
    slot_grad = summed.reshape(expert_count * capacity, model_width).astype(jnp.bfloat16)
    returned = lax.all_to_all(slot_grad, "expert", split_axis=0, concat_axis=0, tiled=True)
    rebal_grad = jnp.sum(returned[own_position].astype(jnp.float32), axis=1).astype(jnp.bfloat16)
    pooled_grad = lax.all_gather(rebal_grad, "dp", axis=0, tiled=True)
    home_index = lax.axis_index("dp") * row_count + jnp.arange(row_count, dtype=jnp.int32)
    choose = (lists_all[None, :] == home_index[:, None]).astype(jnp.bfloat16)
    input_grad = jnp.dot(choose, pooled_grad, preferred_element_type=jnp.float32).astype(
        jnp.bfloat16
    )
    return (input_grad, weight_grads[0], weight_grads[1], weight_grads[2])


def swap(value):
    return lax.ppermute(value, "dp", [(0, 1), (1, 0)])


def shift_outer(value, count, inner, step):
    return lax.ppermute(
        value, "expert", [(place, (place + step * inner) % count) for place in range(count)]
    )


def swap_inner(value, count, partner):
    return lax.ppermute(value, "expert", [(place, place ^ partner) for place in range(count)])


VMEM = pl.BlockSpec(memory_space=pltpu.VMEM)
LANES = 128
NT = (((1,), (1,)), ((), ()))


def on_chip(body, outs, *args):
    moved = sum(arg.size * arg.dtype.itemsize for arg in args)
    moved += sum(math.prod(shape) * jnp.dtype(dtype).itemsize for shape, dtype in outs)
    return pl.pallas_call(
        body,
        out_shape=[jax.ShapeDtypeStruct(shape, dtype) for shape, dtype in outs],
        in_specs=[VMEM] * len(args),
        out_specs=[VMEM] * len(outs),
        compiler_params=pltpu.CompilerParams(vmem_limit_bytes=moved + (4 << 20)),
        cost_estimate=pl.CostEstimate(flops=0, bytes_accessed=moved, transcendentals=0),
    )(*args)


def stack_kernel(*refs):
    low = 0
    for ref in refs[:-1]:
        refs[-1][low : low + ref.shape[0], :] = ref[...]
        low += ref.shape[0]


def stack(blocks):
    rows = sum(block.shape[0] for block in blocks)
    return on_chip(stack_kernel, [((rows, blocks[0].shape[1]), blocks[0].dtype)], *blocks)[0]


def table_kernel(ids_ref, gates_ref, packing_ref, table_ref):
    slots = packing_ref.shape[1]
    count = table_ref.shape[0] - 16
    labels = lax.broadcasted_iota(jnp.int32, (count, slots), 0)
    total = jnp.zeros((count, slots), jnp.float32)
    for k in range(ids_ref.shape[0]):
        named = labels == ids_ref[k : k + 1, :]
        total = total + jnp.where(named, gates_ref[k : k + 1, :].astype(jnp.float32), 0.0)
    table_ref[:count, :] = total.astype(jnp.bfloat16)
    lists = jnp.broadcast_to(packing_ref[...], (16, slots)).astype(jnp.float32)
    table_ref[count:, :] = lists.astype(jnp.bfloat16)


def payload_kernel(table_ref, other_ref, cotangent_ref, payload_ref):
    rows, width = cotangent_ref.shape
    count = table_ref.shape[0] - 16
    slots = table_ref.shape[1]
    homes = lax.broadcasted_iota(jnp.int32, (rows, slots), 0) + lax.axis_index("dp") * rows
    gates = jnp.zeros((rows, count), jnp.float32)
    for ref in (table_ref, other_ref):
        lists = ref[count:, :].astype(jnp.float32)[:1, :]
        matched = (lists == homes.astype(jnp.float32)).astype(jnp.float32).astype(jnp.bfloat16)
        gates = gates + lax.dot_general(
            matched, ref[:count, :], NT, preferred_element_type=jnp.float32
        )
    payload_ref[:, :width] = cotangent_ref[...]
    payload_ref[:, width:] = jnp.zeros((rows, LANES), jnp.bfloat16)
    payload_ref[:, width : width + count] = gates.astype(jnp.bfloat16)


def rows_kernel(tokens_ref, *refs):
    pieces, rows_ref, gate_ref = refs[:-2], refs[-2], refs[-1]
    width = tokens_ref.shape[1]
    rows_ref[:, :width] = tokens_ref[...]
    low = 0
    for ref in pieces:
        span = slice(low, low + ref.shape[0])
        rows_ref[span, width:] = ref[:, :width]
        gates = ref[:, width:].astype(jnp.float32)
        lanes = lax.broadcasted_iota(jnp.int32, gates.shape, 1)
        here = jnp.where(lanes == lax.axis_index("expert"), gates, 0.0)
        gate = jnp.sum(here, axis=1, keepdims=True)
        gate_ref[span, :] = jnp.broadcast_to(gate, (ref.shape[0], gate_ref.shape[1]))
        low += ref.shape[0]


def column_kernel(*refs):
    blocks, own_ref, sent = refs[:4], refs[4], refs[5:]
    total = blocks[0][...].astype(jnp.float32)
    for block in blocks[1:]:
        total = total + block[...].astype(jnp.float32)
    depth = own_ref.shape[0]
    own_ref[...] = total[:depth]
    for index, ref in enumerate(sent):
        ref[...] = total[(index + 1) * depth : (index + 2) * depth].astype(jnp.bfloat16)


def sum_kernel(own_ref, *refs):
    total = own_ref[...]
    for ref in refs[:-1]:
        total = total + ref[...].astype(jnp.float32)
    refs[-1][...] = total.astype(jnp.bfloat16)


def along_outer(value, count, inner):
    return [value] + [shift_outer(value, count, inner, step) for step in range(1, count // inner)]


def dense_local(tokens, cotangent, gate_values, expert_ids, packing, w_gate, w_up, w_down):
    row_count, model_width = tokens.shape
    half = w_gate.shape[1]
    count = lax.axis_size("expert")
    inner = 4
    outer = count // inner
    low, wide = jnp.bfloat16, jnp.float32
    height = row_count * count

    token_blocks = along_outer(tokens, count, inner)
    (table,) = on_chip(
        table_kernel,
        [((count + 16, row_count), low)],
        expert_ids.T,
        gate_values.T,
        packing.reshape(1, row_count),
    )
    other_table = swap(table)
    (payload,) = on_chip(
        payload_kernel,
        [((row_count, model_width + LANES), low)],
        table,
        other_table,
        cotangent,
    )
    own_weights = jnp.concatenate([w_gate[0], w_up[0], w_down[0]], axis=0)
    column = row_count * outer
    top, bottom = slice(0, column // 2), slice(column // 2, None)

    token_column, payload = lax.optimization_barrier((stack(token_blocks), payload))
    token_near = [swap_inner(token_column, count, partner) for partner in (1, 2)]
    upstream_blocks = along_outer(payload, count, inner)

    token_near, upstream_column, own_weights = lax.optimization_barrier(
        (token_near, stack(upstream_blocks), own_weights)
    )
    token_far = [swap_inner(token_near[0][top], count, 2), swap_inner(token_near[1][bottom], count, 1)]
    upstream_near = [swap_inner(upstream_column, count, partner) for partner in (1, 2)]
    other = swap(own_weights)

    token_far, upstream_near = lax.optimization_barrier((token_far, upstream_near))
    inputs = stack([token_column, *token_near, *token_far])
    upstream_far = [
        swap_inner(upstream_near[0][top], count, 2),
        swap_inner(upstream_near[1][bottom], count, 1),
    ]
    rows, gate = on_chip(
        rows_kernel,
        [((height, 2 * model_width), low), ((height, 2 * half), wide)],
        inputs,
        upstream_column,
        *upstream_near,
        *upstream_far,
    )
    upstream = rows[:, model_width:]
    gate_up = jnp.concatenate([w_gate[0], other[:half], w_up[0], other[half : 2 * half]], axis=0)
    down = jnp.concatenate([w_down[0], other[2 * half :]], axis=0)
    pre = jnp.dot(inputs, gate_up.T, preferred_element_type=wide)
    gate_pre, up_pre = pre[:, : 2 * half], pre[:, 2 * half :]
    hidden_grad = gate * jnp.dot(upstream, down.T, preferred_element_type=wide)
    sigmoid_val = jax.nn.sigmoid(gate_pre)
    activated = gate_pre * sigmoid_val
    hidden = (gate * activated * up_pre).astype(low)
    silu_slope = sigmoid_val * (1.0 + gate_pre * (1.0 - sigmoid_val))
    gate_grad = (hidden_grad * up_pre * silu_slope).astype(low)
    up_grad = (hidden_grad * activated).astype(low)
    both_grad = jnp.concatenate([gate_grad, up_grad], axis=1)
    partial_grad = jnp.dot(both_grad, gate_up, preferred_element_type=wide).astype(low)
    blocks = jnp.split(partial_grad, inner, axis=0)
    grads = (gate_grad, up_grad, hidden)
    own_grads = jnp.concatenate([grad[:, :half] for grad in grads], axis=1)
    sent_grads = jnp.concatenate([grad[:, half:] for grad in grads], axis=1)

    blocks, sent_grads, rows = lax.optimization_barrier((blocks, sent_grads, rows))
    returned = [swap_inner(blocks[partner], count, partner) for partner in range(1, inner)]
    other_grads = swap(sent_grads)
    other_rows = swap(rows)
    own, *sent = on_chip(
        column_kernel,
        [((row_count, model_width), wide)] + [((row_count, model_width), low)] * (outer - 1),
        blocks[0],
        *returned,
    )

    sent, other_grads, other_rows = lax.optimization_barrier((sent, other_grads, other_rows))
    back = [shift_outer(sent[step - 1], count, inner, -step) for step in range(1, outer)]
    weight_grads = []
    for index, span in enumerate((slice(0, model_width),) * 2 + (slice(model_width, None),)):
        part = slice(index * half, (index + 1) * half)
        total = jnp.dot(own_grads[:, part].T, rows[:, span], preferred_element_type=wide)
        total = total + jnp.dot(
            other_grads[:, part].T, other_rows[:, span], preferred_element_type=wide
        )
        weight_grads.append(total.astype(low)[None])
    (input_grad,) = on_chip(sum_kernel, [((row_count, model_width), low)], own, *back)
    return (input_grad, *weight_grads)


def local(tokens, cotangent, gate_values, expert_ids, packing, w_gate, w_up, w_down):
    row_count, top = expert_ids.shape
    count = lax.axis_size("expert")
    expert_count = count * w_gate.shape[0]
    capacity = min(row_count, max(2, row_count * top // expert_count + 1))
    few = capacity * 4 <= row_count
    regular = lax.axis_size("dp") == 2 and count % 4 == 0 and w_gate.shape[0] == 1
    chosen = dense_local if regular and not few else routed_local
    return chosen(
        tokens, cotangent, gate_values, expert_ids, packing, w_gate, w_up, w_down
    )


def solution(mesh):
    in_specs = (
        P(("groups", "dp", "expert"), None),
        P(("groups", "dp", "expert"), None),
        P(("groups", "dp", "expert"), None),
        P(("groups", "dp", "expert"), None),
        P(("groups", "dp", "expert")),
        P("expert", "dp", None),
        P("expert", "dp", None),
        P("expert", "dp", None),
    )
    out_specs = (
        P(("groups", "dp", "expert"), None),
        P(("groups", "expert"), "dp", None),
        P(("groups", "expert"), "dp", None),
        P(("groups", "expert"), "dp", None),
    )
    return jax.shard_map(local, mesh=mesh, in_specs=in_specs, out_specs=out_specs, check_vma=False)
```

```python
import math

import jax
import jax.numpy as jnp
from jax import lax
from jax.experimental import pallas as pl
from jax.experimental.pallas import tpu as pltpu
from jax.sharding import PartitionSpec as P


def slot_table(route_ids, route_gates, expert_count, capacity):
    row_count, top_count = route_ids.shape
    flat_ids = route_ids.reshape(-1)
    labels = jnp.arange(expert_count, dtype=jnp.int32)
    onehot = (flat_ids[:, None] == labels[None, :]).astype(jnp.int32)
    earlier = jnp.cumsum(onehot, axis=0) - onehot
    rank_in = jnp.sum(earlier * onehot, axis=1)
    position = flat_ids * capacity + rank_in
    places = jnp.arange(expert_count * capacity, dtype=jnp.int32)
    matched = places[:, None] == position[None, :]
    owner_row = jnp.arange(row_count * top_count, dtype=jnp.int32) // top_count
    occupied = jnp.any(matched, axis=1)
    slot_row = jnp.sum(jnp.where(matched, owner_row[None, :], 0), axis=1)
    flat_gates = route_gates.reshape(-1).astype(jnp.float32)
    slot_gate = jnp.sum(jnp.where(matched, flat_gates[None, :], 0.0), axis=1)
    return (position.reshape(row_count, top_count), occupied, slot_row, slot_gate)


def pick_rows(slot_lists, pooled):
    sources = jnp.arange(pooled.shape[0], dtype=jnp.int32)
    choose = (slot_lists[:, None] == sources[None, :]).astype(jnp.bfloat16)
    return jnp.dot(choose, pooled, preferred_element_type=jnp.float32).astype(jnp.bfloat16)


def fill_slots(rebal_rows, rebal_upstream, occupied, slot_row, slot_gate):
    send_rows = jnp.where(occupied[:, None], rebal_rows[slot_row], jnp.zeros((), jnp.bfloat16))
    scaled = slot_gate[:, None] * rebal_upstream[slot_row].astype(jnp.float32)
    send_upstream = jnp.where(occupied[:, None], scaled, 0.0).astype(jnp.bfloat16)
    return (send_rows, send_upstream)


def expert_terms(inputs, upstream, gate_mat, up_mat, down_mat):
    gate_pre = jnp.dot(inputs, gate_mat.T, preferred_element_type=jnp.float32)
    up_pre = jnp.dot(inputs, up_mat.T, preferred_element_type=jnp.float32)
    sigmoid_val = jax.nn.sigmoid(gate_pre)
    activated = gate_pre * sigmoid_val
    hidden = (activated * up_pre).astype(jnp.bfloat16)
    hidden_grad = jnp.dot(upstream, down_mat.T, preferred_element_type=jnp.float32)
    silu_slope = sigmoid_val * (1.0 + gate_pre * (1.0 - sigmoid_val))
    gate_grad = (hidden_grad * up_pre * silu_slope).astype(jnp.bfloat16)
    up_grad = (hidden_grad * activated).astype(jnp.bfloat16)
    weight_grads = (
        jnp.dot(gate_grad.T, inputs, preferred_element_type=jnp.float32).astype(jnp.bfloat16)[None],
        jnp.dot(up_grad.T, inputs, preferred_element_type=jnp.float32).astype(jnp.bfloat16)[None],
        jnp.dot(hidden.T, upstream, preferred_element_type=jnp.float32).astype(jnp.bfloat16)[None],
    )
    partial_grad = jnp.dot(gate_grad, gate_mat, preferred_element_type=jnp.float32)
    partial_grad = partial_grad + jnp.dot(up_grad, up_mat, preferred_element_type=jnp.float32)
    return (weight_grads, partial_grad)


def routed_local(tokens, cotangent, gate_values, expert_ids, packing, w_gate, w_up, w_down):
    row_count, top_count = expert_ids.shape
    model_width = tokens.shape[1]
    dp_size = lax.axis_size("dp")
    expert_count = lax.axis_size("expert") * w_gate.shape[0]
    capacity = min(row_count, max(2, row_count * top_count // expert_count + 1))
    gate_mat = w_gate[0]
    up_mat = w_up[0]
    down_mat = w_down[0]
    pooled_rows, pooled_upstream, pooled_gates = (
        lax.all_gather(tokens, "dp", axis=0, tiled=True),
        lax.all_gather(cotangent, "dp", axis=0, tiled=True),
        lax.all_gather(gate_values, "dp", axis=0, tiled=True),
    )
    lists_all, pooled_ids = (
        lax.all_gather(packing, "dp", axis=0, tiled=True),
        lax.all_gather(expert_ids, "dp", axis=0, tiled=True),
    )
    member_rows = []
    member_upstream = []
    member_positions = []
    for member in range(dp_size):
        low = member * row_count
        slot_lists = lists_all[low : low + row_count]
        position, occupied, slot_row, slot_gate = slot_table(
            pooled_ids[low : low + row_count],
            pooled_gates[low : low + row_count],
            expert_count,
            capacity,
        )
        send_rows, send_upstream = fill_slots(
            pick_rows(slot_lists, pooled_rows),
            pick_rows(slot_lists, pooled_upstream),
            occupied,
            slot_row,
            slot_gate,
        )
        member_rows.append(send_rows.reshape(expert_count, capacity * model_width))
        member_upstream.append(send_upstream.reshape(expert_count, capacity * model_width))
        member_positions.append(position)
    own_position = jnp.stack(member_positions)[lax.axis_index("dp")]
    send_rows = jnp.concatenate(member_rows, axis=1).reshape(
        expert_count * dp_size * capacity, model_width
    )
    send_upstream = jnp.concatenate(member_upstream, axis=1).reshape(
        expert_count * dp_size * capacity, model_width
    )
    recv_rows, recv_upstream = (
        lax.all_to_all(send_rows, "expert", split_axis=0, concat_axis=0, tiled=True),
        lax.all_to_all(send_upstream, "expert", split_axis=0, concat_axis=0, tiled=True),
    )
    weight_grads, partial_grad = expert_terms(recv_rows, recv_upstream, gate_mat, up_mat, down_mat)
    summed = lax.psum_scatter(
        partial_grad.reshape(expert_count, dp_size * capacity * model_width).astype(jnp.bfloat16),
        "dp",
        scatter_dimension=1,
        tiled=True,
    ).astype(jnp.float32)
    slot_grad = summed.reshape(expert_count * capacity, model_width).astype(jnp.bfloat16)
    returned = lax.all_to_all(slot_grad, "expert", split_axis=0, concat_axis=0, tiled=True)
    rebal_grad = jnp.sum(returned[own_position].astype(jnp.float32), axis=1).astype(jnp.bfloat16)
    pooled_grad = lax.all_gather(rebal_grad, "dp", axis=0, tiled=True)
    home_index = lax.axis_index("dp") * row_count + jnp.arange(row_count, dtype=jnp.int32)
    choose = (lists_all[None, :] == home_index[:, None]).astype(jnp.bfloat16)
    input_grad = jnp.dot(choose, pooled_grad, preferred_element_type=jnp.float32).astype(
        jnp.bfloat16
    )
    return (input_grad, weight_grads[0], weight_grads[1], weight_grads[2])


def swap(value):
    return lax.ppermute(value, "dp", [(0, 1), (1, 0)])


def shift_outer(value, count, inner, step):
    return lax.ppermute(
        value, "expert", [(place, (place + step * inner) % count) for place in range(count)]
    )


def swap_inner(value, count, partner):
    return lax.ppermute(value, "expert", [(place, place ^ partner) for place in range(count)])


VMEM = pl.BlockSpec(memory_space=pltpu.VMEM)
ANY = pl.BlockSpec(memory_space=pl.ANY)
LANES = 128
NT = (((1,), (1,)), ((), ()))


def on_chip(body, outs, *args, scratch=(), spec=VMEM):
    moved = sum(arg.size * arg.dtype.itemsize for arg in args)
    moved += sum(math.prod(shape) * jnp.dtype(dtype).itemsize for shape, dtype in outs)
    return pl.pallas_call(
        body,
        out_shape=[jax.ShapeDtypeStruct(shape, dtype) for shape, dtype in outs],
        in_specs=[spec] * len(args),
        out_specs=[VMEM] * len(outs),
        scratch_shapes=list(scratch),
        compiler_params=pltpu.CompilerParams(vmem_limit_bytes=moved + (4 << 20)),
        cost_estimate=pl.CostEstimate(flops=0, bytes_accessed=moved, transcendentals=0),
    )(*args)


def stack_kernel(*refs):
    low = 0
    for ref in refs[:-1]:
        refs[-1][low : low + ref.shape[0], :] = ref[...]
        low += ref.shape[0]


def stack(blocks):
    rows = sum(block.shape[0] for block in blocks)
    return on_chip(stack_kernel, [((rows, blocks[0].shape[1]), blocks[0].dtype)], *blocks)[0]


def read_kernel(
    ids_hbm, gates_hbm, packing_hbm, tokens_hbm, cotangent_hbm,
    table_ref, tokens_ref, cotangent_ref,
    ids_ref, gates_ref, packing_ref, ready,
):
    copies = [
        pltpu.make_async_copy(source, target, ready.at[index])
        for index, (source, target) in enumerate(
            (
                (ids_hbm, ids_ref),
                (gates_hbm, gates_ref),
                (packing_hbm, packing_ref),
                (tokens_hbm, tokens_ref),
                (cotangent_hbm, cotangent_ref),
            )
        )
    ]
    for copy in copies:
        copy.start()
    for copy in copies:
        copy.wait()
    slots = packing_ref.shape[1]
    count = table_ref.shape[0] - 16
    labels = lax.broadcasted_iota(jnp.int32, (count, slots), 0)
    total = jnp.zeros((count, slots), jnp.float32)
    for k in range(ids_ref.shape[0]):
        named = labels == ids_ref[k : k + 1, :]
        total = total + jnp.where(named, gates_ref[k : k + 1, :].astype(jnp.float32), 0.0)
    table_ref[:count, :] = total.astype(jnp.bfloat16)
    lists = jnp.broadcast_to(packing_ref[...], (16, slots)).astype(jnp.float32)
    table_ref[count:, :] = lists.astype(jnp.bfloat16)


def payload_kernel(table_ref, other_ref, cotangent_ref, payload_ref):
    rows, width = cotangent_ref.shape
    count = table_ref.shape[0] - 16
    slots = table_ref.shape[1]
    homes = lax.broadcasted_iota(jnp.int32, (rows, slots), 0) + lax.axis_index("dp") * rows
    gates = jnp.zeros((rows, count), jnp.float32)
    for ref in (table_ref, other_ref):
        lists = ref[count:, :].astype(jnp.float32)[:1, :]
        matched = (lists == homes.astype(jnp.float32)).astype(jnp.float32).astype(jnp.bfloat16)
        gates = gates + lax.dot_general(
            matched, ref[:count, :], NT, preferred_element_type=jnp.float32
        )
    payload_ref[:, :width] = cotangent_ref[...]
    payload_ref[:, width:] = jnp.zeros((rows, LANES), jnp.bfloat16)
    payload_ref[:, width : width + count] = gates.astype(jnp.bfloat16)


def rows_kernel(tokens_ref, *refs):
    pieces, rows_ref, gate_ref = refs[:-2], refs[-2], refs[-1]
    width = tokens_ref.shape[1]
    rows_ref[:, :width] = tokens_ref[...]
    low = 0
    for ref in pieces:
        span = slice(low, low + ref.shape[0])
        rows_ref[span, width:] = ref[:, :width]
        gates = ref[:, width:].astype(jnp.float32)
        lanes = lax.broadcasted_iota(jnp.int32, gates.shape, 1)
        here = jnp.where(lanes == lax.axis_index("expert"), gates, 0.0)
        gate = jnp.sum(here, axis=1, keepdims=True)
        gate_ref[span, :] = jnp.broadcast_to(gate, (ref.shape[0], gate_ref.shape[1]))
        low += ref.shape[0]


def column_kernel(*refs):
    blocks, own_ref, sent = refs[:4], refs[4], refs[5:]
    total = blocks[0][...].astype(jnp.float32)
    for block in blocks[1:]:
        total = total + block[...].astype(jnp.float32)
    depth = own_ref.shape[0]
    own_ref[...] = total[:depth]
    for index, ref in enumerate(sent):
        ref[...] = total[(index + 1) * depth : (index + 2) * depth].astype(jnp.bfloat16)


def sum_kernel(own_ref, *refs):
    total = own_ref[...]
    for ref in refs[:-1]:
        total = total + ref[...].astype(jnp.float32)
    refs[-1][...] = total.astype(jnp.bfloat16)


def along_outer(value, count, inner):
    return [value] + [shift_outer(value, count, inner, step) for step in range(1, count // inner)]


def dense_local(tokens, cotangent, gate_values, expert_ids, packing, w_gate, w_up, w_down):
    row_count, model_width = tokens.shape
    half = w_gate.shape[1]
    count = lax.axis_size("expert")
    inner = 4
    outer = count // inner
    low, wide = jnp.bfloat16, jnp.float32
    height = row_count * count

    token_blocks = along_outer(tokens, count, inner)
    ids, gates, lists = expert_ids.T, gate_values.T, packing.reshape(1, row_count)
    table, own_tokens, own_cotangent = on_chip(
        read_kernel,
        [
            ((count + 16, row_count), low),
            ((row_count, model_width), low),
            ((row_count, model_width), low),
        ],
        ids,
        gates,
        lists,
        tokens,
        cotangent,
        spec=ANY,
        scratch=[
            pltpu.VMEM(ids.shape, ids.dtype),
            pltpu.VMEM(gates.shape, gates.dtype),
            pltpu.VMEM(lists.shape, lists.dtype),
            pltpu.SemaphoreType.DMA((5,)),
        ],
    )
    other_table = swap(table)
    other_table, own_gate, own_up = lax.optimization_barrier((other_table, w_gate[0], w_up[0]))
    other_gate, other_up = swap(own_gate), swap(own_up)
    (payload,) = on_chip(
        payload_kernel,
        [((row_count, model_width + LANES), low)],
        table,
        other_table,
        own_cotangent,
    )
    column = row_count * outer
    top, bottom = slice(0, column // 2), slice(column // 2, None)

    token_column = stack([own_tokens, *token_blocks[1:]])
    token_column, payload, other_gate, other_up = lax.optimization_barrier(
        (token_column, payload, other_gate, other_up)
    )
    gate_up = stack([w_gate[0], other_gate, w_up[0], other_up])
    token_near = [swap_inner(token_column, count, partner) for partner in (1, 2)]
    upstream_blocks = along_outer(payload, count, inner)

    token_near, upstream_column, gate_up, own_down = lax.optimization_barrier(
        (token_near, stack(upstream_blocks), gate_up, w_down[0])
    )
    token_far = [swap_inner(token_near[0][top], count, 2), swap_inner(token_near[1][bottom], count, 1)]
    upstream_near = [swap_inner(upstream_column, count, partner) for partner in (1, 2)]
    other_down = swap(own_down)

    token_far, upstream_near = lax.optimization_barrier((token_far, upstream_near))
    inputs = stack([token_column, *token_near, *token_far])
    upstream_far = [
        swap_inner(upstream_near[0][top], count, 2),
        swap_inner(upstream_near[1][bottom], count, 1),
    ]
    rows, gate = on_chip(
        rows_kernel,
        [((height, 2 * model_width), low), ((height, 2 * half), wide)],
        inputs,
        upstream_column,
        *upstream_near,
        *upstream_far,
    )
    upstream = rows[:, model_width:]
    down = jnp.concatenate([w_down[0], other_down], axis=0)
    pre = jnp.dot(inputs, gate_up.T, preferred_element_type=wide)
    gate_pre, up_pre = pre[:, : 2 * half], pre[:, 2 * half :]
    hidden_grad = gate * jnp.dot(upstream, down.T, preferred_element_type=wide)
    sigmoid_val = jax.nn.sigmoid(gate_pre)
    activated = gate_pre * sigmoid_val
    hidden = (gate * activated * up_pre).astype(low)
    silu_slope = sigmoid_val * (1.0 + gate_pre * (1.0 - sigmoid_val))
    gate_grad = (hidden_grad * up_pre * silu_slope).astype(low)
    up_grad = (hidden_grad * activated).astype(low)
    both_grad = jnp.concatenate([gate_grad, up_grad], axis=1)
    partial_grad = jnp.dot(both_grad, gate_up, preferred_element_type=wide).astype(low)
    blocks = jnp.split(partial_grad, inner, axis=0)
    grads = (gate_grad, up_grad, hidden)
    own_grads = jnp.concatenate([grad[:, :half] for grad in grads], axis=1)
    sent_grads = jnp.concatenate([grad[:, half:] for grad in grads], axis=1)

    blocks, sent_grads, rows = lax.optimization_barrier((blocks, sent_grads, rows))
    returned = [swap_inner(blocks[partner], count, partner) for partner in range(1, inner)]
    other_grads = swap(sent_grads)
    other_rows = swap(rows)
    own, *sent = on_chip(
        column_kernel,
        [((row_count, model_width), wide)] + [((row_count, model_width), low)] * (outer - 1),
        blocks[0],
        *returned,
    )

    sent, other_grads = lax.optimization_barrier((sent, other_grads))
    back = [shift_outer(sent[step - 1], count, inner, -step) for step in range(1, outer)]
    weight_grads = []
    for index, span in enumerate((slice(0, model_width),) * 2 + (slice(model_width, None),)):
        part = slice(index * half, (index + 1) * half)
        total = jnp.dot(own_grads[:, part].T, rows[:, span], preferred_element_type=wide)
        total = total + jnp.dot(
            other_grads[:, part].T, other_rows[:, span], preferred_element_type=wide
        )
        weight_grads.append(total.astype(low)[None])
    weight_grads, back = lax.optimization_barrier((weight_grads, back))
    (input_grad,) = on_chip(sum_kernel, [((row_count, model_width), low)], own, *back)
    return (input_grad, *weight_grads)


def local(tokens, cotangent, gate_values, expert_ids, packing, w_gate, w_up, w_down):
    row_count, top = expert_ids.shape
    count = lax.axis_size("expert")
    expert_count = count * w_gate.shape[0]
    capacity = min(row_count, max(2, row_count * top // expert_count + 1))
    few = capacity * 4 <= row_count
    regular = lax.axis_size("dp") == 2 and count % 4 == 0 and w_gate.shape[0] == 1
    chosen = dense_local if regular and not few else routed_local
    return chosen(
        tokens, cotangent, gate_values, expert_ids, packing, w_gate, w_up, w_down
    )


def solution(mesh):
    in_specs = (
        P(("groups", "dp", "expert"), None),
        P(("groups", "dp", "expert"), None),
        P(("groups", "dp", "expert"), None),
        P(("groups", "dp", "expert"), None),
        P(("groups", "dp", "expert")),
        P("expert", "dp", None),
        P("expert", "dp", None),
        P("expert", "dp", None),
    )
    out_specs = (
        P(("groups", "dp", "expert"), None),
        P(("groups", "expert"), "dp", None),
        P(("groups", "expert"), "dp", None),
        P(("groups", "expert"), "dp", None),
    )
    return jax.shard_map(local, mesh=mesh, in_specs=in_specs, out_specs=out_specs, check_vma=False)
```

```python
import math

import jax
import jax.numpy as jnp
from jax import lax
from jax.experimental import pallas as pl
from jax.experimental.pallas import tpu as pltpu
from jax.sharding import PartitionSpec as P


def slot_table(route_ids, route_gates, expert_count, capacity):
    row_count, top_count = route_ids.shape
    flat_ids = route_ids.reshape(-1)
    labels = jnp.arange(expert_count, dtype=jnp.int32)
    onehot = (flat_ids[:, None] == labels[None, :]).astype(jnp.int32)
    earlier = jnp.cumsum(onehot, axis=0) - onehot
    rank_in = jnp.sum(earlier * onehot, axis=1)
    position = flat_ids * capacity + rank_in
    places = jnp.arange(expert_count * capacity, dtype=jnp.int32)
    matched = places[:, None] == position[None, :]
    owner_row = jnp.arange(row_count * top_count, dtype=jnp.int32) // top_count
    occupied = jnp.any(matched, axis=1)
    slot_row = jnp.sum(jnp.where(matched, owner_row[None, :], 0), axis=1)
    flat_gates = route_gates.reshape(-1).astype(jnp.float32)
    slot_gate = jnp.sum(jnp.where(matched, flat_gates[None, :], 0.0), axis=1)
    return (position.reshape(row_count, top_count), occupied, slot_row, slot_gate)


def pick_rows(slot_lists, pooled):
    sources = jnp.arange(pooled.shape[0], dtype=jnp.int32)
    choose = (slot_lists[:, None] == sources[None, :]).astype(jnp.bfloat16)
    return jnp.dot(choose, pooled, preferred_element_type=jnp.float32).astype(jnp.bfloat16)


def fill_slots(rebal_rows, rebal_upstream, occupied, slot_row, slot_gate):
    send_rows = jnp.where(occupied[:, None], rebal_rows[slot_row], jnp.zeros((), jnp.bfloat16))
    scaled = slot_gate[:, None] * rebal_upstream[slot_row].astype(jnp.float32)
    send_upstream = jnp.where(occupied[:, None], scaled, 0.0).astype(jnp.bfloat16)
    return (send_rows, send_upstream)


def expert_terms(inputs, upstream, gate_mat, up_mat, down_mat):
    gate_pre = jnp.dot(inputs, gate_mat.T, preferred_element_type=jnp.float32)
    up_pre = jnp.dot(inputs, up_mat.T, preferred_element_type=jnp.float32)
    sigmoid_val = jax.nn.sigmoid(gate_pre)
    activated = gate_pre * sigmoid_val
    hidden = (activated * up_pre).astype(jnp.bfloat16)
    hidden_grad = jnp.dot(upstream, down_mat.T, preferred_element_type=jnp.float32)
    silu_slope = sigmoid_val * (1.0 + gate_pre * (1.0 - sigmoid_val))
    gate_grad = (hidden_grad * up_pre * silu_slope).astype(jnp.bfloat16)
    up_grad = (hidden_grad * activated).astype(jnp.bfloat16)
    weight_grads = (
        jnp.dot(gate_grad.T, inputs, preferred_element_type=jnp.float32).astype(jnp.bfloat16)[None],
        jnp.dot(up_grad.T, inputs, preferred_element_type=jnp.float32).astype(jnp.bfloat16)[None],
        jnp.dot(hidden.T, upstream, preferred_element_type=jnp.float32).astype(jnp.bfloat16)[None],
    )
    partial_grad = jnp.dot(gate_grad, gate_mat, preferred_element_type=jnp.float32)
    partial_grad = partial_grad + jnp.dot(up_grad, up_mat, preferred_element_type=jnp.float32)
    return (weight_grads, partial_grad)


def routed_local(tokens, cotangent, gate_values, expert_ids, packing, w_gate, w_up, w_down):
    row_count, top_count = expert_ids.shape
    model_width = tokens.shape[1]
    dp_size = lax.axis_size("dp")
    expert_count = lax.axis_size("expert") * w_gate.shape[0]
    capacity = min(row_count, max(2, row_count * top_count // expert_count + 1))
    gate_mat = w_gate[0]
    up_mat = w_up[0]
    down_mat = w_down[0]
    pooled_rows, pooled_upstream, pooled_gates = (
        lax.all_gather(tokens, "dp", axis=0, tiled=True),
        lax.all_gather(cotangent, "dp", axis=0, tiled=True),
        lax.all_gather(gate_values, "dp", axis=0, tiled=True),
    )
    lists_all, pooled_ids = (
        lax.all_gather(packing, "dp", axis=0, tiled=True),
        lax.all_gather(expert_ids, "dp", axis=0, tiled=True),
    )
    member_rows = []
    member_upstream = []
    member_positions = []
    for member in range(dp_size):
        low = member * row_count
        slot_lists = lists_all[low : low + row_count]
        position, occupied, slot_row, slot_gate = slot_table(
            pooled_ids[low : low + row_count],
            pooled_gates[low : low + row_count],
            expert_count,
            capacity,
        )
        send_rows, send_upstream = fill_slots(
            pick_rows(slot_lists, pooled_rows),
            pick_rows(slot_lists, pooled_upstream),
            occupied,
            slot_row,
            slot_gate,
        )
        member_rows.append(send_rows.reshape(expert_count, capacity * model_width))
        member_upstream.append(send_upstream.reshape(expert_count, capacity * model_width))
        member_positions.append(position)
    own_position = jnp.stack(member_positions)[lax.axis_index("dp")]
    send_rows = jnp.concatenate(member_rows, axis=1).reshape(
        expert_count * dp_size * capacity, model_width
    )
    send_upstream = jnp.concatenate(member_upstream, axis=1).reshape(
        expert_count * dp_size * capacity, model_width
    )
    recv_rows, recv_upstream = (
        lax.all_to_all(send_rows, "expert", split_axis=0, concat_axis=0, tiled=True),
        lax.all_to_all(send_upstream, "expert", split_axis=0, concat_axis=0, tiled=True),
    )
    weight_grads, partial_grad = expert_terms(recv_rows, recv_upstream, gate_mat, up_mat, down_mat)
    summed = lax.psum_scatter(
        partial_grad.reshape(expert_count, dp_size * capacity * model_width).astype(jnp.bfloat16),
        "dp",
        scatter_dimension=1,
        tiled=True,
    ).astype(jnp.float32)
    slot_grad = summed.reshape(expert_count * capacity, model_width).astype(jnp.bfloat16)
    returned = lax.all_to_all(slot_grad, "expert", split_axis=0, concat_axis=0, tiled=True)
    rebal_grad = jnp.sum(returned[own_position].astype(jnp.float32), axis=1).astype(jnp.bfloat16)
    pooled_grad = lax.all_gather(rebal_grad, "dp", axis=0, tiled=True)
    home_index = lax.axis_index("dp") * row_count + jnp.arange(row_count, dtype=jnp.int32)
    choose = (lists_all[None, :] == home_index[:, None]).astype(jnp.bfloat16)
    input_grad = jnp.dot(choose, pooled_grad, preferred_element_type=jnp.float32).astype(
        jnp.bfloat16
    )
    return (input_grad, weight_grads[0], weight_grads[1], weight_grads[2])


def swap(value):
    return lax.ppermute(value, "dp", [(0, 1), (1, 0)])


def swap_inner(value, count, partner):
    return lax.ppermute(value, "expert", [(place, place ^ partner) for place in range(count)])


VMEM = pl.BlockSpec(memory_space=pltpu.VMEM)
ANY = pl.BlockSpec(memory_space=pl.ANY)
LANES = 128
NT = (((1,), (1,)), ((), ()))


def on_chip(body, outs, *args, scratch=(), spec=VMEM, limit=None):
    moved = sum(arg.size * arg.dtype.itemsize for arg in args)
    moved += sum(math.prod(shape) * jnp.dtype(dtype).itemsize for shape, dtype in outs)
    return pl.pallas_call(
        body,
        out_shape=[jax.ShapeDtypeStruct(shape, dtype) for shape, dtype in outs],
        in_specs=[spec] * len(args),
        out_specs=[VMEM] * len(outs),
        scratch_shapes=list(scratch),
        compiler_params=pltpu.CompilerParams(vmem_limit_bytes=limit or moved + (4 << 20)),
        cost_estimate=pl.CostEstimate(flops=0, bytes_accessed=moved, transcendentals=0),
    )(*args)


def stack_kernel(*refs):
    low = 0
    for ref in refs[:-1]:
        refs[-1][low : low + ref.shape[0], :] = ref[...]
        low += ref.shape[0]


def stack(blocks):
    rows = sum(block.shape[0] for block in blocks)
    return on_chip(stack_kernel, [((rows, blocks[0].shape[1]), blocks[0].dtype)], *blocks)[0]


def read_kernel(
    ids_hbm, gates_hbm, packing_hbm, tokens_hbm, cotangent_hbm,
    table_ref, tokens_ref, cotangent_ref,
    ids_ref, gates_ref, packing_ref, ready,
):
    pairs = [(tokens_hbm, tokens_ref.at[index]) for index in range(tokens_ref.shape[0])]
    pairs += [
        (ids_hbm, ids_ref),
        (gates_hbm, gates_ref),
        (packing_hbm, packing_ref),
        (cotangent_hbm, cotangent_ref),
    ]
    copies = [
        pltpu.make_async_copy(source, target, ready.at[index])
        for index, (source, target) in enumerate(pairs)
    ]
    for copy in copies:
        copy.start()
    for copy in copies:
        copy.wait()
    slots = packing_ref.shape[1]
    count = table_ref.shape[0] - 16
    labels = lax.broadcasted_iota(jnp.int32, (count, slots), 0)
    total = jnp.zeros((count, slots), jnp.float32)
    for k in range(ids_ref.shape[0]):
        named = labels == ids_ref[k : k + 1, :]
        total = total + jnp.where(named, gates_ref[k : k + 1, :].astype(jnp.float32), 0.0)
    table_ref[:count, :] = total.astype(jnp.bfloat16)
    lists = jnp.broadcast_to(packing_ref[...], (16, slots)).astype(jnp.float32)
    table_ref[count:, :] = lists.astype(jnp.bfloat16)


def payload_kernel(table_ref, other_ref, cotangent_ref, payload_ref):
    rows, width = cotangent_ref.shape
    count = table_ref.shape[0] - 16
    slots = table_ref.shape[1]
    homes = lax.broadcasted_iota(jnp.int32, (rows, slots), 0) + lax.axis_index("dp") * rows
    gates = jnp.zeros((rows, count), jnp.float32)
    for ref in (table_ref, other_ref):
        lists = ref[count:, :].astype(jnp.float32)[:1, :]
        matched = (lists == homes.astype(jnp.float32)).astype(jnp.float32).astype(jnp.bfloat16)
        gates = gates + lax.dot_general(
            matched, ref[:count, :], NT, preferred_element_type=jnp.float32
        )
    for copy in range(payload_ref.shape[0]):
        payload_ref[copy, :, :width] = cotangent_ref[...]
        payload_ref[copy, :, width:] = jnp.zeros((rows, LANES), jnp.bfloat16)
        payload_ref[copy, :, width : width + count] = gates.astype(jnp.bfloat16)


def place_rows(target, pieces, columns, width):
    depth = pieces[0].shape[0]
    here = lax.rem(lax.axis_index("expert"), 4)
    for ref, partner, low in zip(pieces, (0, 1, 2, 3, 3), (0, 0, 0, 0, depth // 2)):
        start = pl.multiple_of((here ^ partner) * depth + low, 16)
        target[pl.ds(start, ref.shape[0]), columns] = ref[:, :width]


def tokens_kernel(*refs):
    place_rows(refs[-1], refs[:-1], slice(None), refs[-1].shape[1])


def rows_kernel(tokens_ref, *refs):
    pieces, rows_ref, gate_ref, beside_ref = refs[:-3], refs[-3], refs[-2], refs[-1]
    width = tokens_ref.shape[1]
    rows_ref[:, :width] = tokens_ref[...]
    place_rows(rows_ref, pieces, slice(width, None), width)
    place_rows(beside_ref, [ref.at[:, width:] for ref in pieces], slice(None), LANES)
    gates = beside_ref[...].astype(jnp.float32)
    lanes = lax.broadcasted_iota(jnp.int32, gates.shape, 1)
    here = jnp.where(lanes == lax.axis_index("expert"), gates, 0.0)
    gate = jnp.sum(here, axis=1, keepdims=True)
    gate_ref[...] = jnp.broadcast_to(gate, gate_ref.shape)


def column_kernel(blocks_ref, out_ref):
    total = blocks_ref[0].astype(jnp.float32)
    for index in range(1, blocks_ref.shape[0]):
        total = total + blocks_ref[index].astype(jnp.float32)
    depth = out_ref.shape[1]
    for index in range(out_ref.shape[0]):
        out_ref[index] = total[index * depth : (index + 1) * depth].astype(jnp.bfloat16)


def sum_kernel(blocks_ref, out_ref):
    total = blocks_ref[0].astype(jnp.float32)
    for index in range(1, blocks_ref.shape[0]):
        total = total + blocks_ref[index].astype(jnp.float32)
    out_ref[...] = total.astype(jnp.bfloat16)


def exchange(value, groups):
    return lax.all_to_all(value, "expert", 0, 0, axis_index_groups=groups)


def dense_local(tokens, cotangent, gate_values, expert_ids, packing, w_gate, w_up, w_down):
    row_count, model_width = tokens.shape
    half = w_gate.shape[1]
    count = lax.axis_size("expert")
    inner = 4
    outer = count // inner
    low, wide = jnp.bfloat16, jnp.float32
    height = row_count * count

    columns = [[place + step * inner for step in range(outer)] for place in range(inner)]
    planes = [[place * inner + step for step in range(inner)] for place in range(outer)]
    ids, gates, lists = expert_ids.T, gate_values.T, packing.reshape(1, row_count)
    table, sent_tokens, own_cotangent = on_chip(
        read_kernel,
        [
            ((count + 16, row_count), low),
            ((outer, row_count, model_width), low),
            ((row_count, model_width), low),
        ],
        ids,
        gates,
        lists,
        tokens,
        cotangent,
        spec=ANY,
        scratch=[
            pltpu.VMEM(ids.shape, ids.dtype),
            pltpu.VMEM(gates.shape, gates.dtype),
            pltpu.VMEM(lists.shape, lists.dtype),
            pltpu.SemaphoreType.DMA((4 + outer,)),
        ],
        limit=48 << 20,
    )
    column = row_count * outer
    token_column = exchange(sent_tokens, columns).reshape(column, model_width)
    other_table = swap(table)
    other_table, own_gate, own_up = lax.optimization_barrier((other_table, w_gate[0], w_up[0]))
    other_gate, other_up = swap(own_gate), swap(own_up)
    (payload,) = on_chip(
        payload_kernel,
        [((outer, row_count, model_width + LANES), low)],
        table,
        other_table,
        own_cotangent,
    )
    top, bottom = slice(0, column // 2), slice(column // 2, None)

    token_column, payload, other_gate, other_up = lax.optimization_barrier(
        (token_column, payload, other_gate, other_up)
    )
    gate_up = stack([w_gate[0], other_gate, w_up[0], other_up])
    token_near = [swap_inner(token_column, count, partner) for partner in (1, 2)]
    upstream_column = exchange(payload, columns).reshape(column, model_width + LANES)

    token_near, upstream_column, gate_up, own_down = lax.optimization_barrier(
        (token_near, upstream_column, gate_up, w_down[0])
    )
    token_far = [swap_inner(token_near[0][top], count, 2), swap_inner(token_near[1][bottom], count, 1)]
    upstream_near = [swap_inner(upstream_column, count, partner) for partner in (1, 2)]
    other_down = swap(own_down)

    token_far, upstream_near = lax.optimization_barrier((token_far, upstream_near))
    (inputs,) = on_chip(
        tokens_kernel, [((height, model_width), low)], token_column, *token_near, *token_far
    )
    upstream_far = [
        swap_inner(upstream_near[0][top], count, 2),
        swap_inner(upstream_near[1][bottom], count, 1),
    ]
    rows, gate = on_chip(
        rows_kernel,
        [((height, 2 * model_width), low), ((height, 2 * half), wide)],
        inputs,
        upstream_column,
        *upstream_near,
        *upstream_far,
        scratch=[pltpu.VMEM((height, LANES), low)],
    )
    upstream = rows[:, model_width:]
    down = jnp.concatenate([w_down[0], other_down], axis=0)
    pre = jnp.dot(inputs, gate_up.T, preferred_element_type=wide)
    gate_pre, up_pre = pre[:, : 2 * half], pre[:, 2 * half :]
    hidden_grad = gate * jnp.dot(upstream, down.T, preferred_element_type=wide)
    sigmoid_val = jax.nn.sigmoid(gate_pre)
    activated = gate_pre * sigmoid_val
    hidden = (gate * activated * up_pre).astype(low)
    silu_slope = sigmoid_val * (1.0 + gate_pre * (1.0 - sigmoid_val))
    gate_grad = (hidden_grad * up_pre * silu_slope).astype(low)
    up_grad = (hidden_grad * activated).astype(low)
    both_grad = jnp.concatenate([gate_grad, up_grad], axis=1)
    partial_grad = jnp.dot(both_grad, gate_up, preferred_element_type=wide).astype(low)
    grads = (gate_grad, up_grad, hidden)
    own_grads = jnp.concatenate([grad[:, :half] for grad in grads], axis=1)
    sent_grads = jnp.concatenate([grad[:, half:] for grad in grads], axis=1)

    partial_grad, sent_grads, rows = lax.optimization_barrier((partial_grad, sent_grads, rows))
    blocks = exchange(partial_grad.reshape(inner, column, model_width), planes)
    other_grads = swap(sent_grads)
    other_rows = swap(rows)
    (sent,) = on_chip(column_kernel, [((outer, row_count, model_width), low)], blocks)

    sent, other_grads = lax.optimization_barrier((sent, other_grads))
    back = exchange(sent, columns)
    weight_grads = []
    for index, span in enumerate((slice(0, model_width),) * 2 + (slice(model_width, None),)):
        part = slice(index * half, (index + 1) * half)
        total = jnp.dot(own_grads[:, part].T, rows[:, span], preferred_element_type=wide)
        total = total + jnp.dot(
            other_grads[:, part].T, other_rows[:, span], preferred_element_type=wide
        )
        weight_grads.append(total.astype(low)[None])
    weight_grads, back = lax.optimization_barrier((weight_grads, back))
    (input_grad,) = on_chip(sum_kernel, [((row_count, model_width), low)], back)
    return (input_grad, *weight_grads)


def local(tokens, cotangent, gate_values, expert_ids, packing, w_gate, w_up, w_down):
    row_count, top = expert_ids.shape
    count = lax.axis_size("expert")
    expert_count = count * w_gate.shape[0]
    capacity = min(row_count, max(2, row_count * top // expert_count + 1))
    few = capacity * 4 <= row_count
    regular = lax.axis_size("dp") == 2 and count % 4 == 0 and w_gate.shape[0] == 1
    chosen = dense_local if regular and not few else routed_local
    return chosen(
        tokens, cotangent, gate_values, expert_ids, packing, w_gate, w_up, w_down
    )


def solution(mesh):
    in_specs = (
        P(("groups", "dp", "expert"), None),
        P(("groups", "dp", "expert"), None),
        P(("groups", "dp", "expert"), None),
        P(("groups", "dp", "expert"), None),
        P(("groups", "dp", "expert")),
        P("expert", "dp", None),
        P("expert", "dp", None),
        P("expert", "dp", None),
    )
    out_specs = (
        P(("groups", "dp", "expert"), None),
        P(("groups", "expert"), "dp", None),
        P(("groups", "expert"), "dp", None),
        P(("groups", "expert"), "dp", None),
    )
    return jax.shard_map(local, mesh=mesh, in_specs=in_specs, out_specs=out_specs, check_vma=False)
```

```python
import math

import jax
import jax.numpy as jnp
from jax import lax
from jax.experimental import pallas as pl
from jax.experimental.pallas import tpu as pltpu
from jax.sharding import PartitionSpec as P


def slot_table(route_ids, route_gates, expert_count, capacity):
    row_count, top_count = route_ids.shape
    flat_ids = route_ids.reshape(-1)
    labels = jnp.arange(expert_count, dtype=jnp.int32)
    onehot = (flat_ids[:, None] == labels[None, :]).astype(jnp.int32)
    earlier = jnp.cumsum(onehot, axis=0) - onehot
    rank_in = jnp.sum(earlier * onehot, axis=1)
    position = flat_ids * capacity + rank_in
    places = jnp.arange(expert_count * capacity, dtype=jnp.int32)
    matched = places[:, None] == position[None, :]
    owner_row = jnp.arange(row_count * top_count, dtype=jnp.int32) // top_count
    occupied = jnp.any(matched, axis=1)
    slot_row = jnp.sum(jnp.where(matched, owner_row[None, :], 0), axis=1)
    flat_gates = route_gates.reshape(-1).astype(jnp.float32)
    slot_gate = jnp.sum(jnp.where(matched, flat_gates[None, :], 0.0), axis=1)
    return (position.reshape(row_count, top_count), occupied, slot_row, slot_gate)


def pick_rows(slot_lists, pooled):
    sources = jnp.arange(pooled.shape[0], dtype=jnp.int32)
    choose = (slot_lists[:, None] == sources[None, :]).astype(jnp.bfloat16)
    return jnp.dot(choose, pooled, preferred_element_type=jnp.float32).astype(jnp.bfloat16)


def fill_slots(rebal_rows, rebal_upstream, occupied, slot_row, slot_gate):
    send_rows = jnp.where(occupied[:, None], rebal_rows[slot_row], jnp.zeros((), jnp.bfloat16))
    scaled = slot_gate[:, None] * rebal_upstream[slot_row].astype(jnp.float32)
    send_upstream = jnp.where(occupied[:, None], scaled, 0.0).astype(jnp.bfloat16)
    return (send_rows, send_upstream)


def expert_terms(inputs, upstream, gate_mat, up_mat, down_mat):
    gate_pre = jnp.dot(inputs, gate_mat.T, preferred_element_type=jnp.float32)
    up_pre = jnp.dot(inputs, up_mat.T, preferred_element_type=jnp.float32)
    sigmoid_val = jax.nn.sigmoid(gate_pre)
    activated = gate_pre * sigmoid_val
    hidden = (activated * up_pre).astype(jnp.bfloat16)
    hidden_grad = jnp.dot(upstream, down_mat.T, preferred_element_type=jnp.float32)
    silu_slope = sigmoid_val * (1.0 + gate_pre * (1.0 - sigmoid_val))
    gate_grad = (hidden_grad * up_pre * silu_slope).astype(jnp.bfloat16)
    up_grad = (hidden_grad * activated).astype(jnp.bfloat16)
    weight_grads = (
        jnp.dot(gate_grad.T, inputs, preferred_element_type=jnp.float32).astype(jnp.bfloat16)[None],
        jnp.dot(up_grad.T, inputs, preferred_element_type=jnp.float32).astype(jnp.bfloat16)[None],
        jnp.dot(hidden.T, upstream, preferred_element_type=jnp.float32).astype(jnp.bfloat16)[None],
    )
    partial_grad = jnp.dot(gate_grad, gate_mat, preferred_element_type=jnp.float32)
    partial_grad = partial_grad + jnp.dot(up_grad, up_mat, preferred_element_type=jnp.float32)
    return (weight_grads, partial_grad)


def routed_local(tokens, cotangent, gate_values, expert_ids, packing, w_gate, w_up, w_down):
    row_count, top_count = expert_ids.shape
    model_width = tokens.shape[1]
    dp_size = lax.axis_size("dp")
    expert_count = lax.axis_size("expert") * w_gate.shape[0]
    capacity = min(row_count, max(2, row_count * top_count // expert_count + 1))
    gate_mat = w_gate[0]
    up_mat = w_up[0]
    down_mat = w_down[0]
    pooled_rows, pooled_upstream, pooled_gates = (
        lax.all_gather(tokens, "dp", axis=0, tiled=True),
        lax.all_gather(cotangent, "dp", axis=0, tiled=True),
        lax.all_gather(gate_values, "dp", axis=0, tiled=True),
    )
    lists_all, pooled_ids = (
        lax.all_gather(packing, "dp", axis=0, tiled=True),
        lax.all_gather(expert_ids, "dp", axis=0, tiled=True),
    )
    member_rows = []
    member_upstream = []
    member_positions = []
    for member in range(dp_size):
        low = member * row_count
        slot_lists = lists_all[low : low + row_count]
        position, occupied, slot_row, slot_gate = slot_table(
            pooled_ids[low : low + row_count],
            pooled_gates[low : low + row_count],
            expert_count,
            capacity,
        )
        send_rows, send_upstream = fill_slots(
            pick_rows(slot_lists, pooled_rows),
            pick_rows(slot_lists, pooled_upstream),
            occupied,
            slot_row,
            slot_gate,
        )
        member_rows.append(send_rows.reshape(expert_count, capacity * model_width))
        member_upstream.append(send_upstream.reshape(expert_count, capacity * model_width))
        member_positions.append(position)
    own_position = jnp.stack(member_positions)[lax.axis_index("dp")]
    send_rows = jnp.concatenate(member_rows, axis=1).reshape(
        expert_count * dp_size * capacity, model_width
    )
    send_upstream = jnp.concatenate(member_upstream, axis=1).reshape(
        expert_count * dp_size * capacity, model_width
    )
    recv_rows, recv_upstream = (
        lax.all_to_all(send_rows, "expert", split_axis=0, concat_axis=0, tiled=True),
        lax.all_to_all(send_upstream, "expert", split_axis=0, concat_axis=0, tiled=True),
    )
    weight_grads, partial_grad = expert_terms(recv_rows, recv_upstream, gate_mat, up_mat, down_mat)
    summed = lax.psum_scatter(
        partial_grad.reshape(expert_count, dp_size * capacity * model_width).astype(jnp.bfloat16),
        "dp",
        scatter_dimension=1,
        tiled=True,
    ).astype(jnp.float32)
    slot_grad = summed.reshape(expert_count * capacity, model_width).astype(jnp.bfloat16)
    returned = lax.all_to_all(slot_grad, "expert", split_axis=0, concat_axis=0, tiled=True)
    rebal_grad = jnp.sum(returned[own_position].astype(jnp.float32), axis=1).astype(jnp.bfloat16)
    pooled_grad = lax.all_gather(rebal_grad, "dp", axis=0, tiled=True)
    home_index = lax.axis_index("dp") * row_count + jnp.arange(row_count, dtype=jnp.int32)
    choose = (lists_all[None, :] == home_index[:, None]).astype(jnp.bfloat16)
    input_grad = jnp.dot(choose, pooled_grad, preferred_element_type=jnp.float32).astype(
        jnp.bfloat16
    )
    return (input_grad, weight_grads[0], weight_grads[1], weight_grads[2])


def swap(value):
    return lax.ppermute(value, "dp", [(0, 1), (1, 0)])


def shift_outer(value, count, inner, step):
    return lax.ppermute(
        value, "expert", [(place, (place + step * inner) % count) for place in range(count)]
    )


def swap_inner(value, count, partner):
    return lax.ppermute(value, "expert", [(place, place ^ partner) for place in range(count)])


VMEM = pl.BlockSpec(memory_space=pltpu.VMEM)
ANY = pl.BlockSpec(memory_space=pl.ANY)
NT = (((1,), (1,)), ((), ()))


def on_chip(body, outs, *args, scratch=(), spec=VMEM, limit=True):
    moved = sum(arg.size * arg.dtype.itemsize for arg in args)
    moved += sum(math.prod(shape) * jnp.dtype(dtype).itemsize for shape, dtype in outs)
    granted = {"vmem_limit_bytes": moved + (4 << 20)} if limit else {}
    return pl.pallas_call(
        body,
        out_shape=[jax.ShapeDtypeStruct(shape, dtype) for shape, dtype in outs],
        in_specs=[spec] * len(args),
        out_specs=[VMEM] * len(outs),
        scratch_shapes=list(scratch),
        compiler_params=pltpu.CompilerParams(**granted),
        cost_estimate=pl.CostEstimate(flops=0, bytes_accessed=moved, transcendentals=0),
    )(*args)


def read_kernel(
    ids_hbm, gates_hbm, packing_hbm, tokens_hbm, cotangent_hbm, gate_hbm, up_hbm, down_hbm,
    table_ref, tokens_ref, cotangent_ref, weights_ref,
    ids_ref, gates_ref, packing_ref, ready,
):
    half = gate_hbm.shape[1]
    pairs = [
        (ids_hbm, ids_ref),
        (gates_hbm, gates_ref),
        (packing_hbm, packing_ref),
        (tokens_hbm, tokens_ref),
        (cotangent_hbm, cotangent_ref),
    ]
    for index, source in enumerate((gate_hbm, up_hbm, down_hbm)):
        pairs.append((source.at[0], weights_ref.at[index * half : (index + 1) * half]))
    copies = [
        pltpu.make_async_copy(source, target, ready.at[index])
        for index, (source, target) in enumerate(pairs)
    ]
    for copy in copies:
        copy.start()
    for copy in copies:
        copy.wait()
    slots = packing_ref.shape[1]
    count = table_ref.shape[0] - 16
    labels = lax.broadcasted_iota(jnp.int32, (count, slots), 0)
    total = jnp.zeros((count, slots), jnp.float32)
    for k in range(ids_ref.shape[0]):
        named = labels == ids_ref[k : k + 1, :]
        total = total + jnp.where(named, gates_ref[k : k + 1, :].astype(jnp.float32), 0.0)
    table_ref[:count, :] = total.astype(jnp.bfloat16)
    lists = jnp.broadcast_to(packing_ref[...], (16, slots)).astype(jnp.float32)
    table_ref[count:, :] = lists.astype(jnp.bfloat16)


def payload_kernel(table_ref, other_ref, cotangent_ref, payload_ref, here_ref):
    rows, width = cotangent_ref.shape
    count = table_ref.shape[0] - 16
    slots = table_ref.shape[1]
    homes = lax.broadcasted_iota(jnp.int32, (rows, slots), 0) + lax.axis_index("dp") * rows
    gates = jnp.zeros((rows, count), jnp.float32)
    for ref in (table_ref, other_ref):
        lists = ref[count:, :].astype(jnp.float32)[:1, :]
        matched = (lists == homes.astype(jnp.float32)).astype(jnp.float32).astype(jnp.bfloat16)
        gates = gates + lax.dot_general(
            matched, ref[:count, :], NT, preferred_element_type=jnp.float32
        )
    payload_ref[:, :width] = cotangent_ref[...]
    payload_ref[:, width:] = gates.astype(jnp.bfloat16)
    lanes = lax.broadcasted_iota(jnp.int32, here_ref.shape, 1)
    here_ref[...] = (lanes == lax.axis_index("expert")).astype(jnp.float32)


def along_outer(value, count, inner):
    return [value] + [shift_outer(value, count, inner, step) for step in range(1, count // inner)]


def across_inner(column, count, inner):
    if inner < 4:
        return [column] + [swap_inner(column, count, partner) for partner in range(1, inner)]
    cut = column.shape[0] // 2
    first = swap_inner(column, count, 1)
    second = swap_inner(column, count, 2)
    far_top = swap_inner(first[:cut], count, 2)
    far_bottom = swap_inner(second[cut:], count, 1)
    return [column, first, second, far_top, far_bottom]


def return_inner(value, count, inner):
    blocks = value.reshape(inner, -1, value.shape[-1])
    total = blocks[0].astype(jnp.float32)
    for partner in range(1, inner):
        total = total + swap_inner(blocks[partner], count, partner).astype(jnp.float32)
    return total


def return_outer(value, count, inner):
    outer = count // inner
    blocks = value.reshape(outer, -1, value.shape[-1])
    rounded = blocks.astype(jnp.bfloat16)
    total = blocks[0]
    for step in range(1, outer):
        total = total + shift_outer(rounded[step], count, inner, -step).astype(jnp.float32)
    return total.astype(jnp.bfloat16)


def dense_local(tokens, cotangent, gate_values, expert_ids, packing, w_gate, w_up, w_down):
    model_width = tokens.shape[1]
    half = w_gate.shape[1]
    count = lax.axis_size("expert")
    inner = 4
    row_count = tokens.shape[0]
    low = jnp.bfloat16
    ids, gates, lists = expert_ids.T, gate_values.T, packing.reshape(1, row_count)
    table, own_tokens, own_cotangent, own_weights = on_chip(
        read_kernel,
        [
            ((count + 16, row_count), low),
            (tokens.shape, low),
            (cotangent.shape, low),
            ((3 * half, model_width), low),
        ],
        ids,
        gates,
        lists,
        tokens,
        cotangent,
        w_gate,
        w_up,
        w_down,
        spec=ANY,
        limit=False,
        scratch=[
            pltpu.VMEM(ids.shape, ids.dtype),
            pltpu.VMEM(gates.shape, gates.dtype),
            pltpu.VMEM(lists.shape, lists.dtype),
            pltpu.SemaphoreType.DMA((8,)),
        ],
    )
    token_column = jnp.concatenate(along_outer(own_tokens, count, inner), axis=0)
    other = swap(own_weights)
    payload, here = on_chip(
        payload_kernel,
        [((row_count, model_width + count), low), ((8, count), jnp.float32)],
        table,
        swap(table),
        own_cotangent,
    )
    payload, token_column, other = lax.optimization_barrier((payload, token_column, other))
    upstream_column = jnp.concatenate(along_outer(payload, count, inner), axis=0)
    inputs = jnp.concatenate(across_inner(token_column, count, inner), axis=0)
    other_inputs = swap(inputs)
    upstream = jnp.concatenate(across_inner(upstream_column, count, inner), axis=0)
    gate = jnp.sum(
        upstream[:, model_width:].astype(jnp.float32) * here[:1], axis=1, keepdims=True
    )
    upstream = upstream[:, :model_width]
    gate_up = jnp.concatenate(
        [own_weights[:half], other[:half], own_weights[half : 2 * half], other[half : 2 * half]],
        axis=0,
    )
    down = jnp.concatenate([own_weights[2 * half :], other[2 * half :]], axis=0)
    pre = jnp.dot(inputs, gate_up.T, preferred_element_type=jnp.float32)
    gate_pre, up_pre = pre[:, : 2 * half], pre[:, 2 * half :]
    hidden_grad = gate * jnp.dot(upstream, down.T, preferred_element_type=jnp.float32)
    sigmoid_val = jax.nn.sigmoid(gate_pre)
    activated = gate_pre * sigmoid_val
    hidden = (gate * activated * up_pre).astype(jnp.bfloat16)
    silu_slope = sigmoid_val * (1.0 + gate_pre * (1.0 - sigmoid_val))
    gate_grad = (hidden_grad * up_pre * silu_slope).astype(jnp.bfloat16)
    up_grad = (hidden_grad * activated).astype(jnp.bfloat16)
    both_grad = jnp.concatenate([gate_grad, up_grad], axis=1)
    partial_grad = jnp.dot(both_grad, gate_up, preferred_element_type=jnp.float32)
    partial_grad = partial_grad.astype(jnp.bfloat16)
    column_sum = return_inner(partial_grad, count, inner)
    grads = (gate_grad, up_grad, hidden)
    own_grads = jnp.concatenate([grad[:, :half] for grad in grads], axis=1)
    sent_grads = jnp.concatenate([grad[:, half:] for grad in grads], axis=1)
    sent_grads, upstream, _ = lax.optimization_barrier((sent_grads, upstream, partial_grad))
    other_grads = swap(sent_grads)
    other_upstream = swap(upstream)
    column_sum, other_grads, other_inputs = lax.optimization_barrier(
        (column_sum, other_grads, other_inputs)
    )
    input_grad = return_outer(column_sum, count, inner)
    weight_grads = []
    for index, (rows, other_rows) in enumerate(
        ((inputs, other_inputs), (inputs, other_inputs), (upstream, other_upstream))
    ):
        low = index * half
        total = jnp.dot(
            own_grads[:, low : low + half].T, rows, preferred_element_type=jnp.float32
        ) + jnp.dot(
            other_grads[:, low : low + half].T, other_rows, preferred_element_type=jnp.float32
        )
        weight_grads.append(total.astype(jnp.bfloat16)[None])
    return (input_grad, *weight_grads)


def local(tokens, cotangent, gate_values, expert_ids, packing, w_gate, w_up, w_down):
    row_count, top = expert_ids.shape
    count = lax.axis_size("expert")
    expert_count = count * w_gate.shape[0]
    capacity = min(row_count, max(2, row_count * top // expert_count + 1))
    few = capacity * 4 <= row_count
    regular = lax.axis_size("dp") == 2 and count % 4 == 0 and w_gate.shape[0] == 1
    chosen = dense_local if regular and not few else routed_local
    return chosen(
        tokens, cotangent, gate_values, expert_ids, packing, w_gate, w_up, w_down
    )


def solution(mesh):
    in_specs = (
        P(("groups", "dp", "expert"), None),
        P(("groups", "dp", "expert"), None),
        P(("groups", "dp", "expert"), None),
        P(("groups", "dp", "expert"), None),
        P(("groups", "dp", "expert")),
        P("expert", "dp", None),
        P("expert", "dp", None),
        P("expert", "dp", None),
    )
    out_specs = (
        P(("groups", "dp", "expert"), None),
        P(("groups", "expert"), "dp", None),
        P(("groups", "expert"), "dp", None),
        P(("groups", "expert"), "dp", None),
    )
    return jax.shard_map(local, mesh=mesh, in_specs=in_specs, out_specs=out_specs, check_vma=False)
```

```python
import math

import jax
import jax.numpy as jnp
from jax import lax
from jax.experimental import pallas as pl
from jax.experimental.pallas import tpu as pltpu
from jax.sharding import PartitionSpec as P


def slot_table(route_ids, route_gates, expert_count, capacity):
    row_count, top_count = route_ids.shape
    flat_ids = route_ids.reshape(-1)
    labels = jnp.arange(expert_count, dtype=jnp.int32)
    onehot = (flat_ids[:, None] == labels[None, :]).astype(jnp.int32)
    earlier = jnp.cumsum(onehot, axis=0) - onehot
    rank_in = jnp.sum(earlier * onehot, axis=1)
    position = flat_ids * capacity + rank_in
    places = jnp.arange(expert_count * capacity, dtype=jnp.int32)
    matched = places[:, None] == position[None, :]
    owner_row = jnp.arange(row_count * top_count, dtype=jnp.int32) // top_count
    occupied = jnp.any(matched, axis=1)
    slot_row = jnp.sum(jnp.where(matched, owner_row[None, :], 0), axis=1)
    flat_gates = route_gates.reshape(-1).astype(jnp.float32)
    slot_gate = jnp.sum(jnp.where(matched, flat_gates[None, :], 0.0), axis=1)
    return (position.reshape(row_count, top_count), occupied, slot_row, slot_gate)


def pick_rows(slot_lists, pooled):
    sources = jnp.arange(pooled.shape[0], dtype=jnp.int32)
    choose = (slot_lists[:, None] == sources[None, :]).astype(jnp.bfloat16)
    return jnp.dot(choose, pooled, preferred_element_type=jnp.float32).astype(jnp.bfloat16)


def fill_slots(rebal_rows, rebal_upstream, occupied, slot_row, slot_gate):
    send_rows = jnp.where(occupied[:, None], rebal_rows[slot_row], jnp.zeros((), jnp.bfloat16))
    scaled = slot_gate[:, None] * rebal_upstream[slot_row].astype(jnp.float32)
    send_upstream = jnp.where(occupied[:, None], scaled, 0.0).astype(jnp.bfloat16)
    return (send_rows, send_upstream)


def expert_terms(inputs, upstream, gate_mat, up_mat, down_mat):
    gate_pre = jnp.dot(inputs, gate_mat.T, preferred_element_type=jnp.float32)
    up_pre = jnp.dot(inputs, up_mat.T, preferred_element_type=jnp.float32)
    sigmoid_val = jax.nn.sigmoid(gate_pre)
    activated = gate_pre * sigmoid_val
    hidden = (activated * up_pre).astype(jnp.bfloat16)
    hidden_grad = jnp.dot(upstream, down_mat.T, preferred_element_type=jnp.float32)
    silu_slope = sigmoid_val * (1.0 + gate_pre * (1.0 - sigmoid_val))
    gate_grad = (hidden_grad * up_pre * silu_slope).astype(jnp.bfloat16)
    up_grad = (hidden_grad * activated).astype(jnp.bfloat16)
    weight_grads = (
        jnp.dot(gate_grad.T, inputs, preferred_element_type=jnp.float32).astype(jnp.bfloat16)[None],
        jnp.dot(up_grad.T, inputs, preferred_element_type=jnp.float32).astype(jnp.bfloat16)[None],
        jnp.dot(hidden.T, upstream, preferred_element_type=jnp.float32).astype(jnp.bfloat16)[None],
    )
    partial_grad = jnp.dot(gate_grad, gate_mat, preferred_element_type=jnp.float32)
    partial_grad = partial_grad + jnp.dot(up_grad, up_mat, preferred_element_type=jnp.float32)
    return (weight_grads, partial_grad)


def routed_local(tokens, cotangent, gate_values, expert_ids, packing, w_gate, w_up, w_down):
    row_count, top_count = expert_ids.shape
    model_width = tokens.shape[1]
    dp_size = lax.axis_size("dp")
    expert_count = lax.axis_size("expert") * w_gate.shape[0]
    capacity = min(row_count, max(2, row_count * top_count // expert_count + 1))
    gate_mat = w_gate[0]
    up_mat = w_up[0]
    down_mat = w_down[0]
    pooled_rows, pooled_upstream, pooled_gates = (
        lax.all_gather(tokens, "dp", axis=0, tiled=True),
        lax.all_gather(cotangent, "dp", axis=0, tiled=True),
        lax.all_gather(gate_values, "dp", axis=0, tiled=True),
    )
    lists_all, pooled_ids = (
        lax.all_gather(packing, "dp", axis=0, tiled=True),
        lax.all_gather(expert_ids, "dp", axis=0, tiled=True),
    )
    member_rows = []
    member_upstream = []
    member_positions = []
    for member in range(dp_size):
        low = member * row_count
        slot_lists = lists_all[low : low + row_count]
        position, occupied, slot_row, slot_gate = slot_table(
            pooled_ids[low : low + row_count],
            pooled_gates[low : low + row_count],
            expert_count,
            capacity,
        )
        send_rows, send_upstream = fill_slots(
            pick_rows(slot_lists, pooled_rows),
            pick_rows(slot_lists, pooled_upstream),
            occupied,
            slot_row,
            slot_gate,
        )
        member_rows.append(send_rows.reshape(expert_count, capacity * model_width))
        member_upstream.append(send_upstream.reshape(expert_count, capacity * model_width))
        member_positions.append(position)
    own_position = jnp.stack(member_positions)[lax.axis_index("dp")]
    send_rows = jnp.concatenate(member_rows, axis=1).reshape(
        expert_count * dp_size * capacity, model_width
    )
    send_upstream = jnp.concatenate(member_upstream, axis=1).reshape(
        expert_count * dp_size * capacity, model_width
    )
    recv_rows, recv_upstream = (
        lax.all_to_all(send_rows, "expert", split_axis=0, concat_axis=0, tiled=True),
        lax.all_to_all(send_upstream, "expert", split_axis=0, concat_axis=0, tiled=True),
    )
    weight_grads, partial_grad = expert_terms(recv_rows, recv_upstream, gate_mat, up_mat, down_mat)
    summed = lax.psum_scatter(
        partial_grad.reshape(expert_count, dp_size * capacity * model_width).astype(jnp.bfloat16),
        "dp",
        scatter_dimension=1,
        tiled=True,
    ).astype(jnp.float32)
    slot_grad = summed.reshape(expert_count * capacity, model_width).astype(jnp.bfloat16)
    returned = lax.all_to_all(slot_grad, "expert", split_axis=0, concat_axis=0, tiled=True)
    rebal_grad = jnp.sum(returned[own_position].astype(jnp.float32), axis=1).astype(jnp.bfloat16)
    pooled_grad = lax.all_gather(rebal_grad, "dp", axis=0, tiled=True)
    home_index = lax.axis_index("dp") * row_count + jnp.arange(row_count, dtype=jnp.int32)
    choose = (lists_all[None, :] == home_index[:, None]).astype(jnp.bfloat16)
    input_grad = jnp.dot(choose, pooled_grad, preferred_element_type=jnp.float32).astype(
        jnp.bfloat16
    )
    return (input_grad, weight_grads[0], weight_grads[1], weight_grads[2])


def swap(value):
    return lax.ppermute(value, "dp", [(0, 1), (1, 0)])


def shift_outer(value, count, inner, step):
    return lax.ppermute(
        value, "expert", [(place, (place + step * inner) % count) for place in range(count)]
    )


def swap_inner(value, count, partner):
    return lax.ppermute(value, "expert", [(place, place ^ partner) for place in range(count)])


VMEM = pl.BlockSpec(memory_space=pltpu.VMEM)
ANY = pl.BlockSpec(memory_space=pl.ANY)
NT = (((1,), (1,)), ((), ()))
TN = (((0,), (0,)), ((), ()))


def on_chip(body, outs, *args, scratch=(), spec=VMEM, limit=True):
    moved = sum(arg.size * arg.dtype.itemsize for arg in args)
    moved += sum(math.prod(shape) * jnp.dtype(dtype).itemsize for shape, dtype in outs)
    granted = {"vmem_limit_bytes": moved + (4 << 20)} if limit else {}
    return pl.pallas_call(
        body,
        out_shape=[jax.ShapeDtypeStruct(shape, dtype) for shape, dtype in outs],
        in_specs=[spec] * len(args),
        out_specs=[VMEM] * len(outs),
        scratch_shapes=list(scratch),
        compiler_params=pltpu.CompilerParams(**granted),
        cost_estimate=pl.CostEstimate(flops=0, bytes_accessed=moved, transcendentals=0),
    )(*args)


def read_kernel(
    ids_hbm, gates_hbm, packing_hbm, tokens_hbm, cotangent_hbm,
    table_ref, tokens_ref, cotangent_ref,
    ids_ref, gates_ref, packing_ref, ready,
):
    pairs = [
        (ids_hbm, ids_ref),
        (gates_hbm, gates_ref),
        (packing_hbm, packing_ref),
        (tokens_hbm, tokens_ref),
        (cotangent_hbm, cotangent_ref),
    ]
    copies = [
        pltpu.make_async_copy(source, target, ready.at[index])
        for index, (source, target) in enumerate(pairs)
    ]
    for copy in copies:
        copy.start()
    for copy in copies:
        copy.wait()
    slots = packing_ref.shape[1]
    count = table_ref.shape[0] - 16
    labels = lax.broadcasted_iota(jnp.int32, (count, slots), 0)
    total = jnp.zeros((count, slots), jnp.float32)
    for k in range(ids_ref.shape[0]):
        named = labels == ids_ref[k : k + 1, :]
        total = total + jnp.where(named, gates_ref[k : k + 1, :].astype(jnp.float32), 0.0)
    table_ref[:count, :] = total.astype(jnp.bfloat16)
    lists = jnp.broadcast_to(packing_ref[...], (16, slots)).astype(jnp.float32)
    table_ref[count:, :] = lists.astype(jnp.bfloat16)


def payload_kernel(table_ref, other_ref, cotangent_ref, payload_ref, here_ref):
    rows, width = cotangent_ref.shape
    count = table_ref.shape[0] - 16
    slots = table_ref.shape[1]
    homes = lax.broadcasted_iota(jnp.int32, (rows, slots), 0) + lax.axis_index("dp") * rows
    gates = jnp.zeros((rows, count), jnp.float32)
    for ref in (table_ref, other_ref):
        lists = ref[count:, :].astype(jnp.float32)[:1, :]
        matched = (lists == homes.astype(jnp.float32)).astype(jnp.float32).astype(jnp.bfloat16)
        gates = gates + lax.dot_general(
            matched, ref[:count, :], NT, preferred_element_type=jnp.float32
        )
    payload_ref[:, :width] = cotangent_ref[...]
    payload_ref[:, width:] = gates.astype(jnp.bfloat16)
    lanes = lax.broadcasted_iota(jnp.int32, here_ref.shape, 1)
    here_ref[...] = (lanes == lax.axis_index("expert")).astype(jnp.float32)


def weight_kernel(own_grads, other_grads, rows, other_rows, upstream, other_upstream, *outs):
    half = outs[0].shape[1]
    for index, out in enumerate(outs):
        own, other = (upstream, other_upstream) if index == 2 else (rows, other_rows)
        span = slice(index * half, (index + 1) * half)
        step = min(out.shape[-1], 1024)
        for left in range(0, out.shape[-1], step):
            columns = slice(left, left + step)
            total = lax.dot_general(
                own_grads[:, span], own[:, columns], TN, preferred_element_type=jnp.float32
            ) + lax.dot_general(
                other_grads[:, span], other[:, columns], TN, preferred_element_type=jnp.float32
            )
            out[0, :, columns] = total.astype(jnp.bfloat16)


def along_outer(value, count, inner):
    return [value] + [shift_outer(value, count, inner, step) for step in range(1, count // inner)]


def across_inner(column, count, inner):
    if inner < 4:
        return [column] + [swap_inner(column, count, partner) for partner in range(1, inner)]
    cut = column.shape[0] // 2
    first = swap_inner(column, count, 1)
    second = swap_inner(column, count, 2)
    far_top = swap_inner(first[:cut], count, 2)
    far_bottom = swap_inner(second[cut:], count, 1)
    return [column, first, second, far_top, far_bottom]


def return_inner(value, count, inner):
    blocks = value.reshape(inner, -1, value.shape[-1])
    total = blocks[0].astype(jnp.float32)
    for partner in range(1, inner):
        total = total + swap_inner(blocks[partner], count, partner).astype(jnp.float32)
    return total


def return_outer(value, count, inner):
    outer = count // inner
    blocks = value.reshape(outer, -1, value.shape[-1])
    rounded = blocks.astype(jnp.bfloat16)
    total = blocks[0]
    for step in range(1, outer):
        total = total + shift_outer(rounded[step], count, inner, -step).astype(jnp.float32)
    return total.astype(jnp.bfloat16)


def dense_local(tokens, cotangent, gate_values, expert_ids, packing, w_gate, w_up, w_down):
    model_width = tokens.shape[1]
    half = w_gate.shape[1]
    count = lax.axis_size("expert")
    inner = 4
    row_count = tokens.shape[0]
    low = jnp.bfloat16
    ids, gates, lists = expert_ids.T, gate_values.T, packing.reshape(1, row_count)
    token_blocks = along_outer(tokens, count, inner)
    table, own_tokens, own_cotangent = on_chip(
        read_kernel,
        [
            ((count + 16, row_count), low),
            (tokens.shape, low),
            (cotangent.shape, low),
        ],
        ids,
        gates,
        lists,
        tokens,
        cotangent,
        spec=ANY,
        limit=False,
        scratch=[
            pltpu.VMEM(ids.shape, ids.dtype),
            pltpu.VMEM(gates.shape, gates.dtype),
            pltpu.VMEM(lists.shape, lists.dtype),
            pltpu.SemaphoreType.DMA((5,)),
        ],
    )
    payload, here = on_chip(
        payload_kernel,
        [((row_count, model_width + count), low), ((8, count), jnp.float32)],
        table,
        swap(table),
        own_cotangent,
    )
    token_column = jnp.concatenate([own_tokens, *token_blocks[1:]], axis=0)
    payload, token_column = lax.optimization_barrier((payload, token_column))
    upstream_column = jnp.concatenate(along_outer(payload, count, inner), axis=0)
    token_columns = across_inner(token_column, count, inner)
    own_weights = jnp.concatenate([w_gate[0], w_up[0], w_down[0]], axis=0)
    sent_weights, token_columns[1] = lax.optimization_barrier((own_weights, token_columns[1]))
    other = swap(sent_weights)
    inputs = jnp.concatenate(token_columns, axis=0)
    other_inputs = swap(inputs)
    upstream = jnp.concatenate(across_inner(upstream_column, count, inner), axis=0)
    gate = jnp.sum(
        upstream[:, model_width:].astype(jnp.float32) * here[:1], axis=1, keepdims=True
    )
    upstream = upstream[:, :model_width]
    gate_up = jnp.concatenate(
        [own_weights[:half], other[:half], own_weights[half : 2 * half], other[half : 2 * half]],
        axis=0,
    )
    down = jnp.concatenate([own_weights[2 * half :], other[2 * half :]], axis=0)
    pre = jnp.dot(inputs, gate_up.T, preferred_element_type=jnp.float32)
    gate_pre, up_pre = pre[:, : 2 * half], pre[:, 2 * half :]
    hidden_grad = gate * jnp.dot(upstream, down.T, preferred_element_type=jnp.float32)
    sigmoid_val = jax.nn.sigmoid(gate_pre)
    activated = gate_pre * sigmoid_val
    hidden = (gate * activated * up_pre).astype(jnp.bfloat16)
    silu_slope = sigmoid_val * (1.0 + gate_pre * (1.0 - sigmoid_val))
    gate_grad = (hidden_grad * up_pre * silu_slope).astype(jnp.bfloat16)
    up_grad = (hidden_grad * activated).astype(jnp.bfloat16)
    both_grad = jnp.concatenate([gate_grad, up_grad], axis=1)
    partial_grad = jnp.dot(both_grad, gate_up, preferred_element_type=jnp.float32)
    partial_grad = partial_grad.astype(jnp.bfloat16)
    column_sum = return_inner(partial_grad, count, inner)
    grads = (gate_grad, up_grad, hidden)
    own_grads = jnp.concatenate([grad[:, :half] for grad in grads], axis=1)
    sent_grads = jnp.concatenate([grad[:, half:] for grad in grads], axis=1)
    sent_grads, upstream, _ = lax.optimization_barrier((sent_grads, upstream, partial_grad))
    other_grads = swap(sent_grads)
    other_upstream = swap(upstream)
    column_sum, other_grads, other_inputs, other_upstream = lax.optimization_barrier(
        (column_sum, other_grads, other_inputs, other_upstream)
    )
    input_grad = return_outer(column_sum, count, inner)
    weight_grads = on_chip(
        weight_kernel,
        [((1, half, model_width), low)] * 3,
        own_grads,
        other_grads,
        inputs,
        other_inputs,
        upstream,
        other_upstream,
    )
    return (input_grad, *weight_grads)


def local(tokens, cotangent, gate_values, expert_ids, packing, w_gate, w_up, w_down):
    row_count, top = expert_ids.shape
    count = lax.axis_size("expert")
    expert_count = count * w_gate.shape[0]
    capacity = min(row_count, max(2, row_count * top // expert_count + 1))
    few = capacity * 4 <= row_count
    regular = lax.axis_size("dp") == 2 and count % 4 == 0 and w_gate.shape[0] == 1
    chosen = dense_local if regular and not few else routed_local
    return chosen(
        tokens, cotangent, gate_values, expert_ids, packing, w_gate, w_up, w_down
    )


def solution(mesh):
    in_specs = (
        P(("groups", "dp", "expert"), None),
        P(("groups", "dp", "expert"), None),
        P(("groups", "dp", "expert"), None),
        P(("groups", "dp", "expert"), None),
        P(("groups", "dp", "expert")),
        P("expert", "dp", None),
        P("expert", "dp", None),
        P("expert", "dp", None),
    )
    out_specs = (
        P(("groups", "dp", "expert"), None),
        P(("groups", "expert"), "dp", None),
        P(("groups", "expert"), "dp", None),
        P(("groups", "expert"), "dp", None),
    )
    return jax.shard_map(local, mesh=mesh, in_specs=in_specs, out_specs=out_specs, check_vma=False)
```

```python
import math

import jax
import jax.numpy as jnp
from jax import lax
from jax.experimental import pallas as pl
from jax.experimental.pallas import tpu as pltpu
from jax.sharding import PartitionSpec as P


def slot_table(route_ids, route_gates, expert_count, capacity):
    row_count, top_count = route_ids.shape
    flat_ids = route_ids.reshape(-1)
    labels = jnp.arange(expert_count, dtype=jnp.int32)
    onehot = (flat_ids[:, None] == labels[None, :]).astype(jnp.int32)
    earlier = jnp.cumsum(onehot, axis=0) - onehot
    rank_in = jnp.sum(earlier * onehot, axis=1)
    position = flat_ids * capacity + rank_in
    places = jnp.arange(expert_count * capacity, dtype=jnp.int32)
    matched = places[:, None] == position[None, :]
    owner_row = jnp.arange(row_count * top_count, dtype=jnp.int32) // top_count
    occupied = jnp.any(matched, axis=1)
    slot_row = jnp.sum(jnp.where(matched, owner_row[None, :], 0), axis=1)
    flat_gates = route_gates.reshape(-1).astype(jnp.float32)
    slot_gate = jnp.sum(jnp.where(matched, flat_gates[None, :], 0.0), axis=1)
    return (position.reshape(row_count, top_count), occupied, slot_row, slot_gate)


def pick_rows(slot_lists, pooled):
    sources = jnp.arange(pooled.shape[0], dtype=jnp.int32)
    choose = (slot_lists[:, None] == sources[None, :]).astype(jnp.bfloat16)
    return jnp.dot(choose, pooled, preferred_element_type=jnp.float32).astype(jnp.bfloat16)


def fill_slots(rebal_rows, rebal_upstream, occupied, slot_row, slot_gate):
    send_rows = jnp.where(occupied[:, None], rebal_rows[slot_row], jnp.zeros((), jnp.bfloat16))
    scaled = slot_gate[:, None] * rebal_upstream[slot_row].astype(jnp.float32)
    send_upstream = jnp.where(occupied[:, None], scaled, 0.0).astype(jnp.bfloat16)
    return (send_rows, send_upstream)


def expert_terms(inputs, upstream, gate_mat, up_mat, down_mat):
    gate_pre = jnp.dot(inputs, gate_mat.T, preferred_element_type=jnp.float32)
    up_pre = jnp.dot(inputs, up_mat.T, preferred_element_type=jnp.float32)
    sigmoid_val = jax.nn.sigmoid(gate_pre)
    activated = gate_pre * sigmoid_val
    hidden = (activated * up_pre).astype(jnp.bfloat16)
    hidden_grad = jnp.dot(upstream, down_mat.T, preferred_element_type=jnp.float32)
    silu_slope = sigmoid_val * (1.0 + gate_pre * (1.0 - sigmoid_val))
    gate_grad = (hidden_grad * up_pre * silu_slope).astype(jnp.bfloat16)
    up_grad = (hidden_grad * activated).astype(jnp.bfloat16)
    weight_grads = (
        jnp.dot(gate_grad.T, inputs, preferred_element_type=jnp.float32).astype(jnp.bfloat16)[None],
        jnp.dot(up_grad.T, inputs, preferred_element_type=jnp.float32).astype(jnp.bfloat16)[None],
        jnp.dot(hidden.T, upstream, preferred_element_type=jnp.float32).astype(jnp.bfloat16)[None],
    )
    partial_grad = jnp.dot(gate_grad, gate_mat, preferred_element_type=jnp.float32)
    partial_grad = partial_grad + jnp.dot(up_grad, up_mat, preferred_element_type=jnp.float32)
    return (weight_grads, partial_grad)


def routed_local(tokens, cotangent, gate_values, expert_ids, packing, w_gate, w_up, w_down):
    row_count, top_count = expert_ids.shape
    model_width = tokens.shape[1]
    dp_size = lax.axis_size("dp")
    expert_count = lax.axis_size("expert") * w_gate.shape[0]
    capacity = min(row_count, max(2, row_count * top_count // expert_count + 1))
    gate_mat = w_gate[0]
    up_mat = w_up[0]
    down_mat = w_down[0]
    pooled_rows, pooled_upstream, pooled_gates = (
        lax.all_gather(tokens, "dp", axis=0, tiled=True),
        lax.all_gather(cotangent, "dp", axis=0, tiled=True),
        lax.all_gather(gate_values, "dp", axis=0, tiled=True),
    )
    lists_all, pooled_ids = (
        lax.all_gather(packing, "dp", axis=0, tiled=True),
        lax.all_gather(expert_ids, "dp", axis=0, tiled=True),
    )
    member_rows = []
    member_upstream = []
    member_positions = []
    for member in range(dp_size):
        low = member * row_count
        slot_lists = lists_all[low : low + row_count]
        position, occupied, slot_row, slot_gate = slot_table(
            pooled_ids[low : low + row_count],
            pooled_gates[low : low + row_count],
            expert_count,
            capacity,
        )
        send_rows, send_upstream = fill_slots(
            pick_rows(slot_lists, pooled_rows),
            pick_rows(slot_lists, pooled_upstream),
            occupied,
            slot_row,
            slot_gate,
        )
        member_rows.append(send_rows.reshape(expert_count, capacity * model_width))
        member_upstream.append(send_upstream.reshape(expert_count, capacity * model_width))
        member_positions.append(position)
    own_position = jnp.stack(member_positions)[lax.axis_index("dp")]
    send_rows = jnp.concatenate(member_rows, axis=1).reshape(
        expert_count * dp_size * capacity, model_width
    )
    send_upstream = jnp.concatenate(member_upstream, axis=1).reshape(
        expert_count * dp_size * capacity, model_width
    )
    recv_rows, recv_upstream = (
        lax.all_to_all(send_rows, "expert", split_axis=0, concat_axis=0, tiled=True),
        lax.all_to_all(send_upstream, "expert", split_axis=0, concat_axis=0, tiled=True),
    )
    weight_grads, partial_grad = expert_terms(recv_rows, recv_upstream, gate_mat, up_mat, down_mat)
    summed = lax.psum_scatter(
        partial_grad.reshape(expert_count, dp_size * capacity * model_width).astype(jnp.bfloat16),
        "dp",
        scatter_dimension=1,
        tiled=True,
    ).astype(jnp.float32)
    slot_grad = summed.reshape(expert_count * capacity, model_width).astype(jnp.bfloat16)
    returned = lax.all_to_all(slot_grad, "expert", split_axis=0, concat_axis=0, tiled=True)
    rebal_grad = jnp.sum(returned[own_position].astype(jnp.float32), axis=1).astype(jnp.bfloat16)
    pooled_grad = lax.all_gather(rebal_grad, "dp", axis=0, tiled=True)
    home_index = lax.axis_index("dp") * row_count + jnp.arange(row_count, dtype=jnp.int32)
    choose = (lists_all[None, :] == home_index[:, None]).astype(jnp.bfloat16)
    input_grad = jnp.dot(choose, pooled_grad, preferred_element_type=jnp.float32).astype(
        jnp.bfloat16
    )
    return (input_grad, weight_grads[0], weight_grads[1], weight_grads[2])


def swap(value):
    return lax.ppermute(value, "dp", [(0, 1), (1, 0)])


def shift_outer(value, count, inner, step):
    return lax.ppermute(
        value, "expert", [(place, (place + step * inner) % count) for place in range(count)]
    )


def swap_inner(value, count, partner):
    return lax.ppermute(value, "expert", [(place, place ^ partner) for place in range(count)])


VMEM = pl.BlockSpec(memory_space=pltpu.VMEM)
ANY = pl.BlockSpec(memory_space=pl.ANY)
LANES = 128
NT = (((1,), (1,)), ((), ()))
TN = (((0,), (0,)), ((), ()))


def on_chip(body, outs, *args, scratch=(), spec=VMEM, limit=True):
    moved = sum(arg.size * arg.dtype.itemsize for arg in args)
    moved += sum(math.prod(shape) * jnp.dtype(dtype).itemsize for shape, dtype in outs)
    granted = {"vmem_limit_bytes": moved + (4 << 20)} if limit else {}
    return pl.pallas_call(
        body,
        out_shape=[jax.ShapeDtypeStruct(shape, dtype) for shape, dtype in outs],
        in_specs=[spec] * len(args),
        out_specs=[VMEM] * len(outs),
        scratch_shapes=list(scratch),
        compiler_params=pltpu.CompilerParams(**granted),
        cost_estimate=pl.CostEstimate(flops=0, bytes_accessed=moved, transcendentals=0),
    )(*args)


def fetch(ready, *pairs):
    copies = [
        pltpu.make_async_copy(source, target, ready.at[index])
        for index, (source, target) in enumerate(pairs)
    ]
    for copy in copies:
        copy.start()
    for copy in copies:
        copy.wait()


def weights_kernel(gate_hbm, up_hbm, down_hbm, weights_ref, ready):
    half = gate_hbm.shape[1]
    sources = (gate_hbm, up_hbm, down_hbm)
    fetch(
        ready,
        *(
            (source.at[0], weights_ref.at[index * half : (index + 1) * half])
            for index, source in enumerate(sources)
        ),
    )


def rows_kernel(
    ids_hbm, gates_hbm, packing_hbm, tokens_hbm, cotangent_hbm, rows_ref,
    ids_ref, gates_ref, packing_ref, ready,
):
    width = tokens_hbm.shape[1]
    fetch(
        ready,
        (tokens_hbm, rows_ref.at[:, :width]),
        (cotangent_hbm, rows_ref.at[:, width : 2 * width]),
        (ids_hbm, ids_ref),
        (gates_hbm, gates_ref),
        (packing_hbm, packing_ref),
    )
    slots = packing_ref.shape[1]
    labels = lax.broadcasted_iota(jnp.int32, (LANES, slots), 0)
    table = jnp.where(labels == LANES - 1, packing_ref[...].astype(jnp.float32), 0.0)
    for k in range(ids_ref.shape[0]):
        named = labels == ids_ref[k : k + 1, :]
        table = table + jnp.where(named, gates_ref[k : k + 1, :].astype(jnp.float32), 0.0)
    across = lax.broadcasted_iota(jnp.int32, (slots, slots), 0)
    down = lax.broadcasted_iota(jnp.int32, (slots, slots), 1)
    same = (across == down).astype(jnp.float32).astype(jnp.bfloat16)
    routing = lax.dot_general(
        same, table.astype(jnp.bfloat16), NT, preferred_element_type=jnp.float32
    )
    rows_ref[:, 2 * width :] = routing.astype(jnp.bfloat16)


def column_kernel(*refs):
    column_ref, routing_ref = refs[-2:]
    depth = refs[0].shape[0]
    for index, ref in enumerate(refs[:-2]):
        span = slice(index * depth, (index + 1) * depth)
        column_ref[span, :] = ref[...]
        routing_ref[span, :] = ref[:, ref.shape[1] - LANES :]


def gates_kernel(own_ref, other_ref, gates_ref, here_ref):
    outer = 4
    depth = own_ref.shape[0] // outer
    homes = lax.broadcasted_iota(jnp.int32, (depth, depth), 1) + lax.axis_index("dp") * depth
    for index in range(outer):
        span = slice(index * depth, (index + 1) * depth)
        gates = jnp.zeros((depth, LANES), jnp.float32)
        for ref in (own_ref, other_ref):
            routing = ref[span, :]
            held = routing.astype(jnp.float32)[:, LANES - 1 :]
            matched = (held == homes.astype(jnp.float32)).astype(jnp.float32)
            gates = gates + lax.dot_general(
                matched.astype(jnp.bfloat16), routing, TN, preferred_element_type=jnp.float32
            )
        gates_ref[span, :] = gates.astype(jnp.bfloat16)
    lanes = lax.broadcasted_iota(jnp.int32, here_ref.shape, 1)
    here_ref[...] = (lanes == lax.axis_index("expert")).astype(jnp.float32)


def weight_kernel(own_grads, other_grads, rows, other_rows, *outs):
    half, width = outs[0].shape[1:]
    for index, out in enumerate(outs):
        side = slice(width, 2 * width) if index == 2 else slice(0, width)
        own, other = rows.at[:, side], other_rows.at[:, side]
        span = slice(index * half, (index + 1) * half)
        step = min(out.shape[-1], 1024)
        for left in range(0, out.shape[-1], step):
            columns = slice(left, left + step)
            total = lax.dot_general(
                own_grads[:, span], own[:, columns], TN, preferred_element_type=jnp.float32
            ) + lax.dot_general(
                other_grads[:, span], other[:, columns], TN, preferred_element_type=jnp.float32
            )
            out[0, :, columns] = total.astype(jnp.bfloat16)


def along_outer(value, count, inner):
    return [value] + [shift_outer(value, count, inner, step) for step in range(1, count // inner)]


def across_inner(column, count, inner):
    if inner < 4:
        return [column] + [swap_inner(column, count, partner) for partner in range(1, inner)]
    cut = column.shape[0] // 2
    first = swap_inner(column, count, 1)
    second = swap_inner(column, count, 2)
    far_top = swap_inner(first[:cut], count, 2)
    far_bottom = swap_inner(second[cut:], count, 1)
    return [column, first, second, far_top, far_bottom]


def return_inner(value, count, inner):
    blocks = value.reshape(inner, -1, value.shape[-1])
    total = blocks[0].astype(jnp.float32)
    for partner in range(1, inner):
        total = total + swap_inner(blocks[partner], count, partner).astype(jnp.float32)
    return total


def return_outer(value, count, inner):
    outer = count // inner
    blocks = value.reshape(outer, -1, value.shape[-1])
    rounded = blocks.astype(jnp.bfloat16)
    total = blocks[0]
    for step in range(1, outer):
        total = total + shift_outer(rounded[step], count, inner, -step).astype(jnp.float32)
    return total.astype(jnp.bfloat16)


def dense_local(tokens, cotangent, gate_values, expert_ids, packing, w_gate, w_up, w_down):
    model_width = tokens.shape[1]
    half = w_gate.shape[1]
    count = lax.axis_size("expert")
    inner = 4
    row_count = tokens.shape[0]
    low = jnp.bfloat16
    ids, gates, lists = expert_ids.T, gate_values.T, packing.reshape(1, row_count)
    copies = dict(spec=ANY, limit=False)
    (own_rows,) = on_chip(
        rows_kernel,
        [((row_count, 2 * model_width + LANES), low)],
        ids,
        gates,
        lists,
        tokens,
        cotangent,
        scratch=[
            pltpu.VMEM(ids.shape, ids.dtype),
            pltpu.VMEM(gates.shape, gates.dtype),
            pltpu.VMEM(lists.shape, lists.dtype),
            pltpu.SemaphoreType.DMA((5,)),
        ],
        **copies,
    )
    (own_weights,) = on_chip(
        weights_kernel,
        [((3 * half, model_width), low)],
        w_gate,
        w_up,
        w_down,
        scratch=[pltpu.SemaphoreType.DMA((3,))],
        **copies,
    )
    depth = row_count * count // inner
    column, routing = on_chip(
        column_kernel,
        [((depth, 2 * model_width + LANES), low), ((depth, LANES), low)],
        *along_outer(own_rows, count, inner),
    )
    gates, here = on_chip(
        gates_kernel,
        [((depth, LANES), low), ((8, LANES), jnp.float32)],
        routing,
        swap(routing),
    )
    gates = jnp.concatenate(
        [gates] + [swap_inner(gates, count, partner) for partner in range(1, inner)], axis=0
    )
    own_weights, column = lax.optimization_barrier((own_weights, column))
    other = swap(own_weights)
    rows = jnp.concatenate(across_inner(column, count, inner), axis=0)
    inputs, upstream = rows[:, :model_width], rows[:, model_width : 2 * model_width]
    gate = jnp.sum(gates.astype(jnp.float32) * here[:1], axis=1, keepdims=True)
    gate_up = jnp.concatenate(
        [own_weights[:half], other[:half], own_weights[half : 2 * half], other[half : 2 * half]],
        axis=0,
    )
    down = jnp.concatenate([own_weights[2 * half :], other[2 * half :]], axis=0)
    pre = jnp.dot(inputs, gate_up.T, preferred_element_type=jnp.float32)
    gate_pre, up_pre = pre[:, : 2 * half], pre[:, 2 * half :]
    hidden_grad = gate * jnp.dot(upstream, down.T, preferred_element_type=jnp.float32)
    sigmoid_val = jax.nn.sigmoid(gate_pre)
    activated = gate_pre * sigmoid_val
    hidden = (gate * activated * up_pre).astype(jnp.bfloat16)
    silu_slope = sigmoid_val * (1.0 + gate_pre * (1.0 - sigmoid_val))
    gate_grad = (hidden_grad * up_pre * silu_slope).astype(jnp.bfloat16)
    up_grad = (hidden_grad * activated).astype(jnp.bfloat16)
    both_grad = jnp.concatenate([gate_grad, up_grad], axis=1)
    partial_grad = jnp.dot(both_grad, gate_up, preferred_element_type=jnp.float32)
    partial_grad = partial_grad.astype(jnp.bfloat16)
    column_sum = return_inner(partial_grad, count, inner)
    grads = (gate_grad, up_grad, hidden)
    own_grads = jnp.concatenate([grad[:, :half] for grad in grads], axis=1)
    sent_grads = jnp.concatenate([grad[:, half:] for grad in grads], axis=1)
    sent_grads, rows, _ = lax.optimization_barrier((sent_grads, rows, partial_grad))
    other_grads = swap(sent_grads)
    other_rows = swap(rows)
    column_sum, other_grads, other_rows = lax.optimization_barrier(
        (column_sum, other_grads, other_rows)
    )
    input_grad = return_outer(column_sum, count, inner)
    weight_grads = on_chip(
        weight_kernel,
        [((1, half, model_width), low)] * 3,
        own_grads,
        other_grads,
        rows,
        other_rows,
    )
    return (input_grad, *weight_grads)


def local(tokens, cotangent, gate_values, expert_ids, packing, w_gate, w_up, w_down):
    row_count, top = expert_ids.shape
    count = lax.axis_size("expert")
    expert_count = count * w_gate.shape[0]
    capacity = min(row_count, max(2, row_count * top // expert_count + 1))
    few = capacity * 4 <= row_count
    regular = lax.axis_size("dp") == 2 and count % 4 == 0 and w_gate.shape[0] == 1
    chosen = dense_local if regular and not few else routed_local
    return chosen(
        tokens, cotangent, gate_values, expert_ids, packing, w_gate, w_up, w_down
    )


def solution(mesh):
    in_specs = (
        P(("groups", "dp", "expert"), None),
        P(("groups", "dp", "expert"), None),
        P(("groups", "dp", "expert"), None),
        P(("groups", "dp", "expert"), None),
        P(("groups", "dp", "expert")),
        P("expert", "dp", None),
        P("expert", "dp", None),
        P("expert", "dp", None),
    )
    out_specs = (
        P(("groups", "dp", "expert"), None),
        P(("groups", "expert"), "dp", None),
        P(("groups", "expert"), "dp", None),
        P(("groups", "expert"), "dp", None),
    )
    return jax.shard_map(local, mesh=mesh, in_specs=in_specs, out_specs=out_specs, check_vma=False)
```

```python
import math

import jax
import jax.numpy as jnp
from jax import lax
from jax.experimental import pallas as pl
from jax.experimental.pallas import tpu as pltpu
from jax.sharding import PartitionSpec as P


def slot_table(route_ids, route_gates, expert_count, capacity):
    row_count, top_count = route_ids.shape
    flat_ids = route_ids.reshape(-1)
    labels = jnp.arange(expert_count, dtype=jnp.int32)
    onehot = (flat_ids[:, None] == labels[None, :]).astype(jnp.int32)
    earlier = jnp.cumsum(onehot, axis=0) - onehot
    rank_in = jnp.sum(earlier * onehot, axis=1)
    position = flat_ids * capacity + rank_in
    places = jnp.arange(expert_count * capacity, dtype=jnp.int32)
    matched = places[:, None] == position[None, :]
    owner_row = jnp.arange(row_count * top_count, dtype=jnp.int32) // top_count
    occupied = jnp.any(matched, axis=1)
    slot_row = jnp.sum(jnp.where(matched, owner_row[None, :], 0), axis=1)
    flat_gates = route_gates.reshape(-1).astype(jnp.float32)
    slot_gate = jnp.sum(jnp.where(matched, flat_gates[None, :], 0.0), axis=1)
    return (position.reshape(row_count, top_count), occupied, slot_row, slot_gate)


def pick_rows(slot_lists, pooled):
    sources = jnp.arange(pooled.shape[0], dtype=jnp.int32)
    choose = (slot_lists[:, None] == sources[None, :]).astype(jnp.bfloat16)
    return jnp.dot(choose, pooled, preferred_element_type=jnp.float32).astype(jnp.bfloat16)


def fill_slots(rebal_rows, rebal_upstream, occupied, slot_row, slot_gate):
    send_rows = jnp.where(occupied[:, None], rebal_rows[slot_row], jnp.zeros((), jnp.bfloat16))
    scaled = slot_gate[:, None] * rebal_upstream[slot_row].astype(jnp.float32)
    send_upstream = jnp.where(occupied[:, None], scaled, 0.0).astype(jnp.bfloat16)
    return (send_rows, send_upstream)


def expert_terms(inputs, upstream, gate_mat, up_mat, down_mat):
    gate_pre = jnp.dot(inputs, gate_mat.T, preferred_element_type=jnp.float32)
    up_pre = jnp.dot(inputs, up_mat.T, preferred_element_type=jnp.float32)
    sigmoid_val = jax.nn.sigmoid(gate_pre)
    activated = gate_pre * sigmoid_val
    hidden = (activated * up_pre).astype(jnp.bfloat16)
    hidden_grad = jnp.dot(upstream, down_mat.T, preferred_element_type=jnp.float32)
    silu_slope = sigmoid_val * (1.0 + gate_pre * (1.0 - sigmoid_val))
    gate_grad = (hidden_grad * up_pre * silu_slope).astype(jnp.bfloat16)
    up_grad = (hidden_grad * activated).astype(jnp.bfloat16)
    weight_grads = (
        jnp.dot(gate_grad.T, inputs, preferred_element_type=jnp.float32).astype(jnp.bfloat16)[None],
        jnp.dot(up_grad.T, inputs, preferred_element_type=jnp.float32).astype(jnp.bfloat16)[None],
        jnp.dot(hidden.T, upstream, preferred_element_type=jnp.float32).astype(jnp.bfloat16)[None],
    )
    partial_grad = jnp.dot(gate_grad, gate_mat, preferred_element_type=jnp.float32)
    partial_grad = partial_grad + jnp.dot(up_grad, up_mat, preferred_element_type=jnp.float32)
    return (weight_grads, partial_grad)


def routed_local(tokens, cotangent, gate_values, expert_ids, packing, w_gate, w_up, w_down):
    row_count, top_count = expert_ids.shape
    model_width = tokens.shape[1]
    dp_size = lax.axis_size("dp")
    expert_count = lax.axis_size("expert") * w_gate.shape[0]
    capacity = min(row_count, max(2, row_count * top_count // expert_count + 1))
    gate_mat = w_gate[0]
    up_mat = w_up[0]
    down_mat = w_down[0]
    pooled_rows, pooled_upstream, pooled_gates = (
        lax.all_gather(tokens, "dp", axis=0, tiled=True),
        lax.all_gather(cotangent, "dp", axis=0, tiled=True),
        lax.all_gather(gate_values, "dp", axis=0, tiled=True),
    )
    lists_all, pooled_ids = (
        lax.all_gather(packing, "dp", axis=0, tiled=True),
        lax.all_gather(expert_ids, "dp", axis=0, tiled=True),
    )
    member_rows = []
    member_upstream = []
    member_positions = []
    for member in range(dp_size):
        low = member * row_count
        slot_lists = lists_all[low : low + row_count]
        position, occupied, slot_row, slot_gate = slot_table(
            pooled_ids[low : low + row_count],
            pooled_gates[low : low + row_count],
            expert_count,
            capacity,
        )
        send_rows, send_upstream = fill_slots(
            pick_rows(slot_lists, pooled_rows),
            pick_rows(slot_lists, pooled_upstream),
            occupied,
            slot_row,
            slot_gate,
        )
        member_rows.append(send_rows.reshape(expert_count, capacity * model_width))
        member_upstream.append(send_upstream.reshape(expert_count, capacity * model_width))
        member_positions.append(position)
    own_position = jnp.stack(member_positions)[lax.axis_index("dp")]
    send_rows = jnp.concatenate(member_rows, axis=1).reshape(
        expert_count * dp_size * capacity, model_width
    )
    send_upstream = jnp.concatenate(member_upstream, axis=1).reshape(
        expert_count * dp_size * capacity, model_width
    )
    recv_rows, recv_upstream = (
        lax.all_to_all(send_rows, "expert", split_axis=0, concat_axis=0, tiled=True),
        lax.all_to_all(send_upstream, "expert", split_axis=0, concat_axis=0, tiled=True),
    )
    weight_grads, partial_grad = expert_terms(recv_rows, recv_upstream, gate_mat, up_mat, down_mat)
    summed = lax.psum_scatter(
        partial_grad.reshape(expert_count, dp_size * capacity * model_width).astype(jnp.bfloat16),
        "dp",
        scatter_dimension=1,
        tiled=True,
    ).astype(jnp.float32)
    slot_grad = summed.reshape(expert_count * capacity, model_width).astype(jnp.bfloat16)
    returned = lax.all_to_all(slot_grad, "expert", split_axis=0, concat_axis=0, tiled=True)
    rebal_grad = jnp.sum(returned[own_position].astype(jnp.float32), axis=1).astype(jnp.bfloat16)
    pooled_grad = lax.all_gather(rebal_grad, "dp", axis=0, tiled=True)
    home_index = lax.axis_index("dp") * row_count + jnp.arange(row_count, dtype=jnp.int32)
    choose = (lists_all[None, :] == home_index[:, None]).astype(jnp.bfloat16)
    input_grad = jnp.dot(choose, pooled_grad, preferred_element_type=jnp.float32).astype(
        jnp.bfloat16
    )
    return (input_grad, weight_grads[0], weight_grads[1], weight_grads[2])


def swap(value):
    return lax.ppermute(value, "dp", [(0, 1), (1, 0)])


def shift_outer(value, count, inner, step):
    return lax.ppermute(
        value, "expert", [(place, (place + step * inner) % count) for place in range(count)]
    )


def swap_inner(value, count, partner):
    return lax.ppermute(value, "expert", [(place, place ^ partner) for place in range(count)])


VMEM = pl.BlockSpec(memory_space=pltpu.VMEM)
ANY = pl.BlockSpec(memory_space=pl.ANY)
NT = (((1,), (1,)), ((), ()))
TN = (((0,), (0,)), ((), ()))


def on_chip(body, outs, *args, scratch=(), spec=VMEM, limit=True):
    moved = sum(arg.size * arg.dtype.itemsize for arg in args)
    moved += sum(math.prod(shape) * jnp.dtype(dtype).itemsize for shape, dtype in outs)
    granted = {"vmem_limit_bytes": moved + (4 << 20)} if limit else {}
    return pl.pallas_call(
        body,
        out_shape=[jax.ShapeDtypeStruct(shape, dtype) for shape, dtype in outs],
        in_specs=[spec] * len(args),
        out_specs=[VMEM] * len(outs),
        scratch_shapes=list(scratch),
        compiler_params=pltpu.CompilerParams(**granted),
        cost_estimate=pl.CostEstimate(flops=0, bytes_accessed=moved, transcendentals=0),
    )(*args)


def read_kernel(
    ids_hbm, gates_hbm, packing_hbm, tokens_hbm, cotangent_hbm,
    table_ref, tokens_ref, cotangent_ref,
    ids_ref, gates_ref, packing_ref, ready,
):
    pairs = [
        (ids_hbm, ids_ref),
        (gates_hbm, gates_ref),
        (packing_hbm, packing_ref),
        (tokens_hbm, tokens_ref),
        (cotangent_hbm, cotangent_ref),
    ]
    copies = [
        pltpu.make_async_copy(source, target, ready.at[index])
        for index, (source, target) in enumerate(pairs)
    ]
    for copy in copies:
        copy.start()
    for copy in copies:
        copy.wait()
    slots = packing_ref.shape[1]
    count = table_ref.shape[0] - 16
    labels = lax.broadcasted_iota(jnp.int32, (count, slots), 0)
    total = jnp.zeros((count, slots), jnp.float32)
    for k in range(ids_ref.shape[0]):
        named = labels == ids_ref[k : k + 1, :]
        total = total + jnp.where(named, gates_ref[k : k + 1, :].astype(jnp.float32), 0.0)
    table_ref[:count, :] = total.astype(jnp.bfloat16)
    lists = jnp.broadcast_to(packing_ref[...], (16, slots)).astype(jnp.float32)
    table_ref[count:, :] = lists.astype(jnp.bfloat16)


def payload_kernel(table_ref, other_ref, cotangent_ref, payload_ref, here_ref):
    rows, width = cotangent_ref.shape
    count = table_ref.shape[0] - 16
    slots = table_ref.shape[1]
    homes = lax.broadcasted_iota(jnp.int32, (rows, slots), 0) + lax.axis_index("dp") * rows
    gates = jnp.zeros((rows, count), jnp.float32)
    for ref in (table_ref, other_ref):
        lists = ref[count:, :].astype(jnp.float32)[:1, :]
        matched = (lists == homes.astype(jnp.float32)).astype(jnp.float32).astype(jnp.bfloat16)
        gates = gates + lax.dot_general(
            matched, ref[:count, :], NT, preferred_element_type=jnp.float32
        )
    payload_ref[:, :width] = cotangent_ref[...]
    payload_ref[:, width:] = gates.astype(jnp.bfloat16)
    lanes = lax.broadcasted_iota(jnp.int32, here_ref.shape, 1)
    here_ref[...] = (lanes == lax.axis_index("expert")).astype(jnp.float32)


def weight_kernel(own_grads, other_grads, rows, other_rows, upstream, other_near, other_far, *outs):
    half, width = outs[0].shape[1:]
    height, cut = rows.shape[0], other_near.shape[0]
    step = min(width, 1024)
    for index, out in enumerate(outs):
        span = slice(index * half, (index + 1) * half)
        terms = [(own_grads, slice(0, height), rows), (other_grads, slice(0, height), other_rows)]
        if index == 2:
            terms = [
                (own_grads, slice(0, height), upstream),
                (other_grads, slice(0, cut), other_near),
                (other_grads, slice(cut, height), other_far),
            ]
        for left in range(0, width, step):
            columns = slice(left, left + step)
            total = jnp.zeros((half, step), jnp.float32)
            for grads, part, values in terms:
                total = total + lax.dot_general(
                    grads[part, span], values[:, columns], TN, preferred_element_type=jnp.float32
                )
            out[0, :, columns] = total.astype(jnp.bfloat16)


def stack_kernel(*refs):
    low = 0
    for ref in refs[:-1]:
        refs[-1][low : low + ref.shape[0], :] = ref[...]
        low += ref.shape[0]


def along_outer(value, count, inner):
    return [value] + [shift_outer(value, count, inner, step) for step in range(1, count // inner)]


def near_inner(column, count):
    return [swap_inner(column, count, 1), swap_inner(column, count, 2)]


def far_inner(near, count):
    cut = near[0].shape[0] // 2
    return [swap_inner(near[0][:cut], count, 2), swap_inner(near[1][cut:], count, 1)]


def return_inner(value, count, inner):
    blocks = value.reshape(inner, -1, value.shape[-1])
    total = blocks[0].astype(jnp.float32)
    for partner in range(1, inner):
        total = total + swap_inner(blocks[partner], count, partner).astype(jnp.float32)
    return total


def return_outer(value, count, inner):
    outer = count // inner
    blocks = value.reshape(outer, -1, value.shape[-1])
    rounded = blocks.astype(jnp.bfloat16)
    total = blocks[0]
    for step in range(1, outer):
        total = total + shift_outer(rounded[step], count, inner, -step).astype(jnp.float32)
    return total.astype(jnp.bfloat16)


def dense_local(tokens, cotangent, gate_values, expert_ids, packing, w_gate, w_up, w_down):
    model_width = tokens.shape[1]
    half = w_gate.shape[1]
    count = lax.axis_size("expert")
    inner = 4
    row_count = tokens.shape[0]
    low = jnp.bfloat16
    ids, gates, lists = expert_ids.T, gate_values.T, packing.reshape(1, row_count)
    token_blocks = along_outer(tokens, count, inner)
    table, own_tokens, own_cotangent = on_chip(
        read_kernel,
        [
            ((count + 16, row_count), low),
            (tokens.shape, low),
            (cotangent.shape, low),
        ],
        ids,
        gates,
        lists,
        tokens,
        cotangent,
        spec=ANY,
        limit=False,
        scratch=[
            pltpu.VMEM(ids.shape, ids.dtype),
            pltpu.VMEM(gates.shape, gates.dtype),
            pltpu.VMEM(lists.shape, lists.dtype),
            pltpu.SemaphoreType.DMA((5,)),
        ],
    )
    payload, here = on_chip(
        payload_kernel,
        [((row_count, model_width + count), low), ((8, count), jnp.float32)],
        table,
        swap(table),
        own_cotangent,
    )
    token_column = jnp.concatenate([own_tokens, *token_blocks[1:]], axis=0)
    others = [swap(weights[0]) for weights in (w_gate, w_up)]
    payload, token_column, others = lax.optimization_barrier((payload, token_column, others))
    upstream_column = jnp.concatenate(along_outer(payload, count, inner), axis=0)
    token_near = near_inner(token_column, count)
    token_near, upstream_column, sent_down = lax.optimization_barrier(
        (token_near, upstream_column, w_down[0])
    )
    upstream_near = near_inner(upstream_column, count)
    token_columns = [token_column, *token_near, *far_inner(token_near, count)]
    other_down = swap(sent_down)
    (gate_up,) = on_chip(
        stack_kernel,
        [((4 * half, model_width), low)],
        w_gate[0],
        others[0],
        w_up[0],
        others[1],
    )
    down = jnp.concatenate([w_down[0], other_down], axis=0)
    inputs = jnp.concatenate(token_columns, axis=0)
    other_inputs = swap(inputs)
    near = jnp.concatenate([upstream_column, *upstream_near], axis=0)
    other_near = swap(near)
    far = jnp.concatenate(far_inner(upstream_near, count), axis=0)
    upstream = jnp.concatenate([near, far], axis=0)
    gate = jnp.sum(
        upstream[:, model_width:].astype(jnp.float32) * here[:1], axis=1, keepdims=True
    )
    upstream = upstream[:, :model_width]
    pre = jnp.dot(inputs, gate_up.T, preferred_element_type=jnp.float32)
    gate_pre, up_pre = pre[:, : 2 * half], pre[:, 2 * half :]
    hidden_grad = gate * jnp.dot(upstream, down.T, preferred_element_type=jnp.float32)
    sigmoid_val = jax.nn.sigmoid(gate_pre)
    activated = gate_pre * sigmoid_val
    hidden = (gate * activated * up_pre).astype(jnp.bfloat16)
    silu_slope = sigmoid_val * (1.0 + gate_pre * (1.0 - sigmoid_val))
    gate_grad = (hidden_grad * up_pre * silu_slope).astype(jnp.bfloat16)
    up_grad = (hidden_grad * activated).astype(jnp.bfloat16)
    both_grad = jnp.concatenate([gate_grad, up_grad], axis=1)
    partial_grad = jnp.dot(both_grad, gate_up, preferred_element_type=jnp.float32)
    partial_grad = partial_grad.astype(jnp.bfloat16)
    column_sum = return_inner(partial_grad, count, inner)
    grads = (gate_grad, up_grad, hidden)
    own_grads = jnp.concatenate([grad[:, :half] for grad in grads], axis=1)
    sent_grads = jnp.concatenate([grad[:, half:] for grad in grads], axis=1)
    sent_grads, far, _ = lax.optimization_barrier((sent_grads, far, partial_grad))
    other_grads = swap(sent_grads)
    other_far = swap(far)
    column_sum, other_grads, other_inputs, other_near, other_far = lax.optimization_barrier(
        (column_sum, other_grads, other_inputs, other_near, other_far)
    )
    input_grad = return_outer(column_sum, count, inner)
    weight_grads = on_chip(
        weight_kernel,
        [((1, half, model_width), low)] * 3,
        own_grads,
        other_grads,
        inputs,
        other_inputs,
        upstream,
        other_near,
        other_far,
    )
    return (input_grad, *weight_grads)


def local(tokens, cotangent, gate_values, expert_ids, packing, w_gate, w_up, w_down):
    row_count, top = expert_ids.shape
    count = lax.axis_size("expert")
    expert_count = count * w_gate.shape[0]
    capacity = min(row_count, max(2, row_count * top // expert_count + 1))
    few = capacity * 4 <= row_count
    regular = lax.axis_size("dp") == 2 and count % 4 == 0 and w_gate.shape[0] == 1
    chosen = dense_local if regular and not few else routed_local
    return chosen(
        tokens, cotangent, gate_values, expert_ids, packing, w_gate, w_up, w_down
    )


def solution(mesh):
    in_specs = (
        P(("groups", "dp", "expert"), None),
        P(("groups", "dp", "expert"), None),
        P(("groups", "dp", "expert"), None),
        P(("groups", "dp", "expert"), None),
        P(("groups", "dp", "expert")),
        P("expert", "dp", None),
        P("expert", "dp", None),
        P("expert", "dp", None),
    )
    out_specs = (
        P(("groups", "dp", "expert"), None),
        P(("groups", "expert"), "dp", None),
        P(("groups", "expert"), "dp", None),
        P(("groups", "expert"), "dp", None),
    )
    return jax.shard_map(local, mesh=mesh, in_specs=in_specs, out_specs=out_specs, check_vma=False)
```

```python
import math

import jax
import jax.numpy as jnp
from jax import lax
from jax.experimental import pallas as pl
from jax.experimental.pallas import tpu as pltpu
from jax.sharding import PartitionSpec as P


def slot_table(route_ids, route_gates, expert_count, capacity):
    row_count, top_count = route_ids.shape
    flat_ids = route_ids.reshape(-1)
    labels = jnp.arange(expert_count, dtype=jnp.int32)
    onehot = (flat_ids[:, None] == labels[None, :]).astype(jnp.int32)
    earlier = jnp.cumsum(onehot, axis=0) - onehot
    rank_in = jnp.sum(earlier * onehot, axis=1)
    position = flat_ids * capacity + rank_in
    places = jnp.arange(expert_count * capacity, dtype=jnp.int32)
    matched = places[:, None] == position[None, :]
    owner_row = jnp.arange(row_count * top_count, dtype=jnp.int32) // top_count
    occupied = jnp.any(matched, axis=1)
    slot_row = jnp.sum(jnp.where(matched, owner_row[None, :], 0), axis=1)
    flat_gates = route_gates.reshape(-1).astype(jnp.float32)
    slot_gate = jnp.sum(jnp.where(matched, flat_gates[None, :], 0.0), axis=1)
    return (position.reshape(row_count, top_count), occupied, slot_row, slot_gate)


def pick_rows(slot_lists, pooled):
    sources = jnp.arange(pooled.shape[0], dtype=jnp.int32)
    choose = (slot_lists[:, None] == sources[None, :]).astype(jnp.bfloat16)
    return jnp.dot(choose, pooled, preferred_element_type=jnp.float32).astype(jnp.bfloat16)


def fill_slots(rebal_rows, rebal_upstream, occupied, slot_row, slot_gate):
    send_rows = jnp.where(occupied[:, None], rebal_rows[slot_row], jnp.zeros((), jnp.bfloat16))
    scaled = slot_gate[:, None] * rebal_upstream[slot_row].astype(jnp.float32)
    send_upstream = jnp.where(occupied[:, None], scaled, 0.0).astype(jnp.bfloat16)
    return (send_rows, send_upstream)


def expert_terms(inputs, upstream, gate_mat, up_mat, down_mat):
    gate_pre = jnp.dot(inputs, gate_mat.T, preferred_element_type=jnp.float32)
    up_pre = jnp.dot(inputs, up_mat.T, preferred_element_type=jnp.float32)
    sigmoid_val = jax.nn.sigmoid(gate_pre)
    activated = gate_pre * sigmoid_val
    hidden = (activated * up_pre).astype(jnp.bfloat16)
    hidden_grad = jnp.dot(upstream, down_mat.T, preferred_element_type=jnp.float32)
    silu_slope = sigmoid_val * (1.0 + gate_pre * (1.0 - sigmoid_val))
    gate_grad = (hidden_grad * up_pre * silu_slope).astype(jnp.bfloat16)
    up_grad = (hidden_grad * activated).astype(jnp.bfloat16)
    weight_grads = (
        jnp.dot(gate_grad.T, inputs, preferred_element_type=jnp.float32).astype(jnp.bfloat16)[None],
        jnp.dot(up_grad.T, inputs, preferred_element_type=jnp.float32).astype(jnp.bfloat16)[None],
        jnp.dot(hidden.T, upstream, preferred_element_type=jnp.float32).astype(jnp.bfloat16)[None],
    )
    partial_grad = jnp.dot(gate_grad, gate_mat, preferred_element_type=jnp.float32)
    partial_grad = partial_grad + jnp.dot(up_grad, up_mat, preferred_element_type=jnp.float32)
    return (weight_grads, partial_grad)


def routed_local(tokens, cotangent, gate_values, expert_ids, packing, w_gate, w_up, w_down):
    row_count, top_count = expert_ids.shape
    model_width = tokens.shape[1]
    dp_size = lax.axis_size("dp")
    expert_count = lax.axis_size("expert") * w_gate.shape[0]
    capacity = min(row_count, max(2, row_count * top_count // expert_count + 1))
    gate_mat = w_gate[0]
    up_mat = w_up[0]
    down_mat = w_down[0]
    pooled_rows, pooled_upstream, pooled_gates = (
        lax.all_gather(tokens, "dp", axis=0, tiled=True),
        lax.all_gather(cotangent, "dp", axis=0, tiled=True),
        lax.all_gather(gate_values, "dp", axis=0, tiled=True),
    )
    lists_all, pooled_ids = (
        lax.all_gather(packing, "dp", axis=0, tiled=True),
        lax.all_gather(expert_ids, "dp", axis=0, tiled=True),
    )
    member_rows = []
    member_upstream = []
    member_positions = []
    for member in range(dp_size):
        low = member * row_count
        slot_lists = lists_all[low : low + row_count]
        position, occupied, slot_row, slot_gate = slot_table(
            pooled_ids[low : low + row_count],
            pooled_gates[low : low + row_count],
            expert_count,
            capacity,
        )
        send_rows, send_upstream = fill_slots(
            pick_rows(slot_lists, pooled_rows),
            pick_rows(slot_lists, pooled_upstream),
            occupied,
            slot_row,
            slot_gate,
        )
        member_rows.append(send_rows.reshape(expert_count, capacity * model_width))
        member_upstream.append(send_upstream.reshape(expert_count, capacity * model_width))
        member_positions.append(position)
    own_position = jnp.stack(member_positions)[lax.axis_index("dp")]
    send_rows = jnp.concatenate(member_rows, axis=1).reshape(
        expert_count * dp_size * capacity, model_width
    )
    send_upstream = jnp.concatenate(member_upstream, axis=1).reshape(
        expert_count * dp_size * capacity, model_width
    )
    recv_rows, recv_upstream = (
        lax.all_to_all(send_rows, "expert", split_axis=0, concat_axis=0, tiled=True),
        lax.all_to_all(send_upstream, "expert", split_axis=0, concat_axis=0, tiled=True),
    )
    weight_grads, partial_grad = expert_terms(recv_rows, recv_upstream, gate_mat, up_mat, down_mat)
    summed = lax.psum_scatter(
        partial_grad.reshape(expert_count, dp_size * capacity * model_width).astype(jnp.bfloat16),
        "dp",
        scatter_dimension=1,
        tiled=True,
    ).astype(jnp.float32)
    slot_grad = summed.reshape(expert_count * capacity, model_width).astype(jnp.bfloat16)
    returned = lax.all_to_all(slot_grad, "expert", split_axis=0, concat_axis=0, tiled=True)
    rebal_grad = jnp.sum(returned[own_position].astype(jnp.float32), axis=1).astype(jnp.bfloat16)
    pooled_grad = lax.all_gather(rebal_grad, "dp", axis=0, tiled=True)
    home_index = lax.axis_index("dp") * row_count + jnp.arange(row_count, dtype=jnp.int32)
    choose = (lists_all[None, :] == home_index[:, None]).astype(jnp.bfloat16)
    input_grad = jnp.dot(choose, pooled_grad, preferred_element_type=jnp.float32).astype(
        jnp.bfloat16
    )
    return (input_grad, weight_grads[0], weight_grads[1], weight_grads[2])


def swap(value):
    return lax.ppermute(value, "dp", [(0, 1), (1, 0)])


def swap_outer(value, count, inner, partner):
    return swap_inner(value, count, partner * inner)


def swap_inner(value, count, partner):
    return lax.ppermute(value, "expert", [(place, place ^ partner) for place in range(count)])


VMEM = pl.BlockSpec(memory_space=pltpu.VMEM)
ANY = pl.BlockSpec(memory_space=pl.ANY)
NT = (((1,), (1,)), ((), ()))
TN = (((0,), (0,)), ((), ()))


def on_chip(body, outs, *args, scratch=(), spec=VMEM, limit=True):
    moved = sum(arg.size * arg.dtype.itemsize for arg in args)
    moved += sum(math.prod(shape) * jnp.dtype(dtype).itemsize for shape, dtype in outs)
    granted = {"vmem_limit_bytes": moved + (4 << 20)} if limit else {}
    return pl.pallas_call(
        body,
        out_shape=[jax.ShapeDtypeStruct(shape, dtype) for shape, dtype in outs],
        in_specs=[spec] * len(args),
        out_specs=[VMEM] * len(outs),
        scratch_shapes=list(scratch),
        compiler_params=pltpu.CompilerParams(**granted),
        cost_estimate=pl.CostEstimate(flops=0, bytes_accessed=moved, transcendentals=0),
    )(*args)


def fetch(ready, *pairs):
    copies = [
        pltpu.make_async_copy(source, target, ready.at[index])
        for index, (source, target) in enumerate(pairs)
    ]
    for copy in copies:
        copy.start()
    for copy in copies:
        copy.wait()


def weights_kernel(gate_hbm, up_hbm, down_hbm, weights_ref, ready):
    half = gate_hbm.shape[1]
    sources = (gate_hbm, up_hbm, down_hbm)
    fetch(
        ready,
        *(
            (source.at[0], weights_ref.at[index * half : (index + 1) * half])
            for index, source in enumerate(sources)
        ),
    )


def read_kernel(
    ids_hbm, gates_hbm, packing_hbm, tokens_hbm, cotangent_hbm,
    table_ref, tokens_ref, cotangent_ref,
    ids_ref, gates_ref, packing_ref, ready,
):
    fetch(
        ready,
        (ids_hbm, ids_ref),
        (gates_hbm, gates_ref),
        (packing_hbm, packing_ref),
        (tokens_hbm, tokens_ref),
        (cotangent_hbm, cotangent_ref),
    )
    slots = packing_ref.shape[1]
    count = table_ref.shape[0] - 16
    labels = lax.broadcasted_iota(jnp.int32, (count, slots), 0)
    total = jnp.zeros((count, slots), jnp.float32)
    for k in range(ids_ref.shape[0]):
        named = labels == ids_ref[k : k + 1, :]
        total = total + jnp.where(named, gates_ref[k : k + 1, :].astype(jnp.float32), 0.0)
    table_ref[:count, :] = total.astype(jnp.bfloat16)
    lists = jnp.broadcast_to(packing_ref[...], (16, slots)).astype(jnp.float32)
    table_ref[count:, :] = lists.astype(jnp.bfloat16)


def payload_kernel(table_ref, other_ref, cotangent_ref, payload_ref, here_ref):
    rows, width = cotangent_ref.shape
    count = table_ref.shape[0] - 16
    slots = table_ref.shape[1]
    homes = lax.broadcasted_iota(jnp.int32, (rows, slots), 0) + lax.axis_index("dp") * rows
    gates = jnp.zeros((rows, count), jnp.float32)
    for ref in (table_ref, other_ref):
        lists = ref[count:, :].astype(jnp.float32)[:1, :]
        matched = (lists == homes.astype(jnp.float32)).astype(jnp.float32).astype(jnp.bfloat16)
        gates = gates + lax.dot_general(
            matched, ref[:count, :], NT, preferred_element_type=jnp.float32
        )
    payload_ref[:, :width] = cotangent_ref[...]
    payload_ref[:, width:] = gates.astype(jnp.bfloat16)
    lanes = lax.broadcasted_iota(jnp.int32, here_ref.shape, 1)
    here_ref[...] = (lanes == lax.axis_index("expert")).astype(jnp.float32)


def weight_kernel(own_grads, other_grads, rows, other_rows, upstream, other_upstream, *outs):
    half = outs[0].shape[1]
    for index, out in enumerate(outs):
        own, other = (upstream, other_upstream) if index == 2 else (rows, other_rows)
        span = slice(index * half, (index + 1) * half)
        step = min(out.shape[-1], 1024)
        for left in range(0, out.shape[-1], step):
            columns = slice(left, left + step)
            total = lax.dot_general(
                own_grads[:, span], own[:, columns], TN, preferred_element_type=jnp.float32
            ) + lax.dot_general(
                other_grads[:, span], other[:, columns], TN, preferred_element_type=jnp.float32
            )
            out[0, :, columns] = total.astype(jnp.bfloat16)


def along_outer(value, count, inner):
    return [value] + [swap_outer(value, count, inner, step) for step in range(1, count // inner)]


def across_inner(column, count, inner):
    if inner < 4:
        return [column] + [swap_inner(column, count, partner) for partner in range(1, inner)]
    cut = column.shape[0] // 2
    first = swap_inner(column, count, 1)
    second = swap_inner(column, count, 2)
    far_top = swap_inner(first[:cut], count, 2)
    far_bottom = swap_inner(second[cut:], count, 1)
    return [column, first, second, far_top, far_bottom]


def return_inner(value, count, inner):
    blocks = value.reshape(inner, -1, value.shape[-1])
    total = blocks[0].astype(jnp.float32)
    for partner in range(1, inner):
        total = total + swap_inner(blocks[partner], count, partner).astype(jnp.float32)
    return total


def return_outer(value, count, inner):
    outer = count // inner
    blocks = value.reshape(outer, -1, value.shape[-1])
    rounded = blocks.astype(jnp.bfloat16)
    total = blocks[0]
    for step in range(1, outer):
        total = total + swap_outer(rounded[step], count, inner, step).astype(jnp.float32)
    return total.astype(jnp.bfloat16)


def dense_local(tokens, cotangent, gate_values, expert_ids, packing, w_gate, w_up, w_down):
    model_width = tokens.shape[1]
    half = w_gate.shape[1]
    count = lax.axis_size("expert")
    inner = 4
    row_count = tokens.shape[0]
    low = jnp.bfloat16
    ids, gates, lists = expert_ids.T, gate_values.T, packing.reshape(1, row_count)
    token_blocks = along_outer(tokens, count, inner)
    table, own_tokens, own_cotangent = on_chip(
        read_kernel,
        [
            ((count + 16, row_count), low),
            (tokens.shape, low),
            (cotangent.shape, low),
        ],
        ids,
        gates,
        lists,
        tokens,
        cotangent,
        spec=ANY,
        limit=False,
        scratch=[
            pltpu.VMEM(ids.shape, ids.dtype),
            pltpu.VMEM(gates.shape, gates.dtype),
            pltpu.VMEM(lists.shape, lists.dtype),
            pltpu.SemaphoreType.DMA((5,)),
        ],
    )
    payload, here = on_chip(
        payload_kernel,
        [((row_count, model_width + count), low), ((8, count), jnp.float32)],
        table,
        swap(table),
        own_cotangent,
    )
    token_column = jnp.concatenate([own_tokens, *token_blocks[1:]], axis=0)
    payload, token_column = lax.optimization_barrier((payload, token_column))
    (own_weights,) = on_chip(
        weights_kernel,
        [((3 * half, model_width), low)],
        w_gate,
        w_up,
        w_down,
        spec=ANY,
        limit=False,
        scratch=[pltpu.SemaphoreType.DMA((3,))],
    )
    upstream_column = jnp.concatenate(along_outer(payload, count, inner), axis=0)
    token_columns = across_inner(token_column, count, inner)
    sent_weights, token_columns[1] = lax.optimization_barrier((own_weights, token_columns[1]))
    other = swap(sent_weights)
    inputs = jnp.concatenate(token_columns, axis=0)
    other_inputs = swap(inputs)
    upstream = jnp.concatenate(across_inner(upstream_column, count, inner), axis=0)
    gate = jnp.sum(
        upstream[:, model_width:].astype(jnp.float32) * here[:1], axis=1, keepdims=True
    )
    upstream = upstream[:, :model_width]
    gate_up = jnp.concatenate(
        [own_weights[:half], other[:half], own_weights[half : 2 * half], other[half : 2 * half]],
        axis=0,
    )
    down = jnp.concatenate([own_weights[2 * half :], other[2 * half :]], axis=0)
    pre = jnp.dot(inputs, gate_up.T, preferred_element_type=jnp.float32)
    gate_pre, up_pre = pre[:, : 2 * half], pre[:, 2 * half :]
    hidden_grad = gate * jnp.dot(upstream, down.T, preferred_element_type=jnp.float32)
    sigmoid_val = jax.nn.sigmoid(gate_pre)
    activated = gate_pre * sigmoid_val
    hidden = (gate * activated * up_pre).astype(jnp.bfloat16)
    silu_slope = sigmoid_val * (1.0 + gate_pre * (1.0 - sigmoid_val))
    gate_grad = (hidden_grad * up_pre * silu_slope).astype(jnp.bfloat16)
    up_grad = (hidden_grad * activated).astype(jnp.bfloat16)
    both_grad = jnp.concatenate([gate_grad, up_grad], axis=1)
    partial_grad = jnp.dot(both_grad, gate_up, preferred_element_type=jnp.float32)
    partial_grad = partial_grad.astype(jnp.bfloat16)
    column_sum = return_inner(partial_grad, count, inner)
    grads = (gate_grad, up_grad, hidden)
    own_grads = jnp.concatenate([grad[:, :half] for grad in grads], axis=1)
    sent_grads = jnp.concatenate([grad[:, half:] for grad in grads], axis=1)
    sent_grads, upstream, _ = lax.optimization_barrier((sent_grads, upstream, partial_grad))
    other_grads = swap(sent_grads)
    other_upstream = swap(upstream)
    column_sum, other_grads, other_inputs, other_upstream = lax.optimization_barrier(
        (column_sum, other_grads, other_inputs, other_upstream)
    )
    input_grad = return_outer(column_sum, count, inner)
    weight_grads = on_chip(
        weight_kernel,
        [((1, half, model_width), low)] * 3,
        own_grads,
        other_grads,
        inputs,
        other_inputs,
        upstream,
        other_upstream,
    )
    return (input_grad, *weight_grads)


def local(tokens, cotangent, gate_values, expert_ids, packing, w_gate, w_up, w_down):
    row_count, top = expert_ids.shape
    count = lax.axis_size("expert")
    expert_count = count * w_gate.shape[0]
    capacity = min(row_count, max(2, row_count * top // expert_count + 1))
    few = capacity * 4 <= row_count
    regular = lax.axis_size("dp") == 2 and count % 4 == 0 and w_gate.shape[0] == 1
    chosen = dense_local if regular and not few else routed_local
    return chosen(
        tokens, cotangent, gate_values, expert_ids, packing, w_gate, w_up, w_down
    )


def solution(mesh):
    in_specs = (
        P(("groups", "dp", "expert"), None),
        P(("groups", "dp", "expert"), None),
        P(("groups", "dp", "expert"), None),
        P(("groups", "dp", "expert"), None),
        P(("groups", "dp", "expert")),
        P("expert", "dp", None),
        P("expert", "dp", None),
        P("expert", "dp", None),
    )
    out_specs = (
        P(("groups", "dp", "expert"), None),
        P(("groups", "expert"), "dp", None),
        P(("groups", "expert"), "dp", None),
        P(("groups", "expert"), "dp", None),
    )
    return jax.shard_map(local, mesh=mesh, in_specs=in_specs, out_specs=out_specs, check_vma=False)
```

```python
import math

import jax
import jax.numpy as jnp
from jax import lax
from jax.experimental import pallas as pl
from jax.experimental.pallas import tpu as pltpu
from jax.sharding import PartitionSpec as P


def slot_table(route_ids, route_gates, expert_count, capacity):
    row_count, top_count = route_ids.shape
    flat_ids = route_ids.reshape(-1)
    labels = jnp.arange(expert_count, dtype=jnp.int32)
    onehot = (flat_ids[:, None] == labels[None, :]).astype(jnp.int32)
    earlier = jnp.cumsum(onehot, axis=0) - onehot
    rank_in = jnp.sum(earlier * onehot, axis=1)
    position = flat_ids * capacity + rank_in
    places = jnp.arange(expert_count * capacity, dtype=jnp.int32)
    matched = places[:, None] == position[None, :]
    owner_row = jnp.arange(row_count * top_count, dtype=jnp.int32) // top_count
    occupied = jnp.any(matched, axis=1)
    slot_row = jnp.sum(jnp.where(matched, owner_row[None, :], 0), axis=1)
    flat_gates = route_gates.reshape(-1).astype(jnp.float32)
    slot_gate = jnp.sum(jnp.where(matched, flat_gates[None, :], 0.0), axis=1)
    return (position.reshape(row_count, top_count), occupied, slot_row, slot_gate)


def pick_rows(slot_lists, pooled):
    sources = jnp.arange(pooled.shape[0], dtype=jnp.int32)
    choose = (slot_lists[:, None] == sources[None, :]).astype(jnp.bfloat16)
    return jnp.dot(choose, pooled, preferred_element_type=jnp.float32).astype(jnp.bfloat16)


def fill_slots(rebal_rows, rebal_upstream, occupied, slot_row, slot_gate):
    send_rows = jnp.where(occupied[:, None], rebal_rows[slot_row], jnp.zeros((), jnp.bfloat16))
    scaled = slot_gate[:, None] * rebal_upstream[slot_row].astype(jnp.float32)
    send_upstream = jnp.where(occupied[:, None], scaled, 0.0).astype(jnp.bfloat16)
    return (send_rows, send_upstream)


def expert_terms(inputs, upstream, gate_mat, up_mat, down_mat):
    gate_pre = jnp.dot(inputs, gate_mat.T, preferred_element_type=jnp.float32)
    up_pre = jnp.dot(inputs, up_mat.T, preferred_element_type=jnp.float32)
    sigmoid_val = jax.nn.sigmoid(gate_pre)
    activated = gate_pre * sigmoid_val
    hidden = (activated * up_pre).astype(jnp.bfloat16)
    hidden_grad = jnp.dot(upstream, down_mat.T, preferred_element_type=jnp.float32)
    silu_slope = sigmoid_val * (1.0 + gate_pre * (1.0 - sigmoid_val))
    gate_grad = (hidden_grad * up_pre * silu_slope).astype(jnp.bfloat16)
    up_grad = (hidden_grad * activated).astype(jnp.bfloat16)
    weight_grads = (
        jnp.dot(gate_grad.T, inputs, preferred_element_type=jnp.float32).astype(jnp.bfloat16)[None],
        jnp.dot(up_grad.T, inputs, preferred_element_type=jnp.float32).astype(jnp.bfloat16)[None],
        jnp.dot(hidden.T, upstream, preferred_element_type=jnp.float32).astype(jnp.bfloat16)[None],
    )
    partial_grad = jnp.dot(gate_grad, gate_mat, preferred_element_type=jnp.float32)
    partial_grad = partial_grad + jnp.dot(up_grad, up_mat, preferred_element_type=jnp.float32)
    return (weight_grads, partial_grad)


def routed_local(tokens, cotangent, gate_values, expert_ids, packing, w_gate, w_up, w_down):
    row_count, top_count = expert_ids.shape
    model_width = tokens.shape[1]
    dp_size = lax.axis_size("dp")
    expert_count = lax.axis_size("expert") * w_gate.shape[0]
    capacity = min(row_count, max(2, row_count * top_count // expert_count + 1))
    gate_mat = w_gate[0]
    up_mat = w_up[0]
    down_mat = w_down[0]
    pooled_rows, pooled_upstream, pooled_gates = (
        lax.all_gather(tokens, "dp", axis=0, tiled=True),
        lax.all_gather(cotangent, "dp", axis=0, tiled=True),
        lax.all_gather(gate_values, "dp", axis=0, tiled=True),
    )
    lists_all, pooled_ids = (
        lax.all_gather(packing, "dp", axis=0, tiled=True),
        lax.all_gather(expert_ids, "dp", axis=0, tiled=True),
    )
    member_rows = []
    member_upstream = []
    member_positions = []
    for member in range(dp_size):
        low = member * row_count
        slot_lists = lists_all[low : low + row_count]
        position, occupied, slot_row, slot_gate = slot_table(
            pooled_ids[low : low + row_count],
            pooled_gates[low : low + row_count],
            expert_count,
            capacity,
        )
        send_rows, send_upstream = fill_slots(
            pick_rows(slot_lists, pooled_rows),
            pick_rows(slot_lists, pooled_upstream),
            occupied,
            slot_row,
            slot_gate,
        )
        member_rows.append(send_rows.reshape(expert_count, capacity * model_width))
        member_upstream.append(send_upstream.reshape(expert_count, capacity * model_width))
        member_positions.append(position)
    own_position = jnp.stack(member_positions)[lax.axis_index("dp")]
    send_rows = jnp.concatenate(member_rows, axis=1).reshape(
        expert_count * dp_size * capacity, model_width
    )
    send_upstream = jnp.concatenate(member_upstream, axis=1).reshape(
        expert_count * dp_size * capacity, model_width
    )
    recv_rows, recv_upstream = (
        lax.all_to_all(send_rows, "expert", split_axis=0, concat_axis=0, tiled=True),
        lax.all_to_all(send_upstream, "expert", split_axis=0, concat_axis=0, tiled=True),
    )
    weight_grads, partial_grad = expert_terms(recv_rows, recv_upstream, gate_mat, up_mat, down_mat)
    summed = lax.psum_scatter(
        partial_grad.reshape(expert_count, dp_size * capacity * model_width).astype(jnp.bfloat16),
        "dp",
        scatter_dimension=1,
        tiled=True,
    ).astype(jnp.float32)
    slot_grad = summed.reshape(expert_count * capacity, model_width).astype(jnp.bfloat16)
    returned = lax.all_to_all(slot_grad, "expert", split_axis=0, concat_axis=0, tiled=True)
    rebal_grad = jnp.sum(returned[own_position].astype(jnp.float32), axis=1).astype(jnp.bfloat16)
    pooled_grad = lax.all_gather(rebal_grad, "dp", axis=0, tiled=True)
    home_index = lax.axis_index("dp") * row_count + jnp.arange(row_count, dtype=jnp.int32)
    choose = (lists_all[None, :] == home_index[:, None]).astype(jnp.bfloat16)
    input_grad = jnp.dot(choose, pooled_grad, preferred_element_type=jnp.float32).astype(
        jnp.bfloat16
    )
    return (input_grad, weight_grads[0], weight_grads[1], weight_grads[2])


def swap(value):
    return lax.ppermute(value, "dp", [(0, 1), (1, 0)])


def shift_outer(value, count, inner, step):
    return lax.ppermute(
        value, "expert", [(place, (place + step * inner) % count) for place in range(count)]
    )


def swap_inner(value, count, partner):
    return lax.ppermute(value, "expert", [(place, place ^ partner) for place in range(count)])


VMEM = pl.BlockSpec(memory_space=pltpu.VMEM)
ANY = pl.BlockSpec(memory_space=pl.ANY)
NT = (((1,), (1,)), ((), ()))
TN = (((0,), (0,)), ((), ()))


def on_chip(body, outs, *args, scratch=(), spec=VMEM, limit=True):
    moved = sum(arg.size * arg.dtype.itemsize for arg in args)
    moved += sum(math.prod(shape) * jnp.dtype(dtype).itemsize for shape, dtype in outs)
    granted = {"vmem_limit_bytes": moved + (4 << 20)} if limit else {}
    return pl.pallas_call(
        body,
        out_shape=[jax.ShapeDtypeStruct(shape, dtype) for shape, dtype in outs],
        in_specs=[spec] * len(args),
        out_specs=[VMEM] * len(outs),
        scratch_shapes=list(scratch),
        compiler_params=pltpu.CompilerParams(**granted),
        cost_estimate=pl.CostEstimate(flops=0, bytes_accessed=moved, transcendentals=0),
    )(*args)


def read_kernel(
    ids_hbm, gates_hbm, packing_hbm, tokens_hbm, cotangent_hbm,
    table_ref, tokens_ref, cotangent_ref,
    ids_ref, gates_ref, packing_ref, ready,
):
    pairs = [
        (ids_hbm, ids_ref),
        (gates_hbm, gates_ref),
        (packing_hbm, packing_ref),
        (tokens_hbm, tokens_ref),
        (cotangent_hbm, cotangent_ref),
    ]
    copies = [
        pltpu.make_async_copy(source, target, ready.at[index])
        for index, (source, target) in enumerate(pairs)
    ]
    for copy in copies:
        copy.start()
    for copy in copies:
        copy.wait()
    slots = packing_ref.shape[1]
    count = table_ref.shape[0] - 16
    labels = lax.broadcasted_iota(jnp.int32, (count, slots), 0)
    total = jnp.zeros((count, slots), jnp.float32)
    for k in range(ids_ref.shape[0]):
        named = labels == ids_ref[k : k + 1, :]
        total = total + jnp.where(named, gates_ref[k : k + 1, :].astype(jnp.float32), 0.0)
    table_ref[:count, :] = total.astype(jnp.bfloat16)
    lists = jnp.broadcast_to(packing_ref[...], (16, slots)).astype(jnp.float32)
    table_ref[count:, :] = lists.astype(jnp.bfloat16)


def payload_kernel(table_ref, other_ref, cotangent_ref, payload_ref, here_ref):
    rows, width = cotangent_ref.shape
    count = table_ref.shape[0] - 16
    slots = table_ref.shape[1]
    homes = lax.broadcasted_iota(jnp.int32, (rows, slots), 0) + lax.axis_index("dp") * rows
    gates = jnp.zeros((rows, count), jnp.float32)
    for ref in (table_ref, other_ref):
        lists = ref[count:, :].astype(jnp.float32)[:1, :]
        matched = (lists == homes.astype(jnp.float32)).astype(jnp.float32).astype(jnp.bfloat16)
        gates = gates + lax.dot_general(
            matched, ref[:count, :], NT, preferred_element_type=jnp.float32
        )
    payload_ref[:, :width] = cotangent_ref[...]
    payload_ref[:, width:] = gates.astype(jnp.bfloat16)
    lanes = lax.broadcasted_iota(jnp.int32, here_ref.shape, 1)
    here_ref[...] = (lanes == lax.axis_index("expert")).astype(jnp.float32)


def weight_kernel(own_grads, other_grads, rows, other_rows, upstream, other_upstream, *outs):
    half = outs[0].shape[1]
    for index, out in enumerate(outs):
        own, other = (upstream, other_upstream) if index == 2 else (rows, other_rows)
        span = slice(index * half, (index + 1) * half)
        step = min(out.shape[-1], 1024)
        for left in range(0, out.shape[-1], step):
            columns = slice(left, left + step)
            total = lax.dot_general(
                own_grads[:, span], own[:, columns], TN, preferred_element_type=jnp.float32
            ) + lax.dot_general(
                other_grads[:, span], other[:, columns], TN, preferred_element_type=jnp.float32
            )
            out[0, :, columns] = total.astype(jnp.bfloat16)


def along_outer(value, count, inner):
    return [value] + [shift_outer(value, count, inner, step) for step in range(1, count // inner)]


def stack_kernel(*refs):
    low = 0
    for ref in refs[:-1]:
        refs[-1][low : low + ref.shape[0], :] = ref[...]
        low += ref.shape[0]


def stack(blocks):
    rows = sum(block.shape[0] for block in blocks)
    return on_chip(stack_kernel, [((rows, blocks[0].shape[1]), blocks[0].dtype)], *blocks)[0]


def near_inner(column, count):
    return [swap_inner(column, count, 1), swap_inner(column, count, 2)]


def far_inner(near, count):
    cut = near[0].shape[0] // 2
    return [swap_inner(near[0][:cut], count, 2), swap_inner(near[1][cut:], count, 1)]


def return_inner(value, count, inner):
    blocks = value.reshape(inner, -1, value.shape[-1])
    total = blocks[0].astype(jnp.float32)
    for partner in range(1, inner):
        total = total + swap_inner(blocks[partner], count, partner).astype(jnp.float32)
    return total


def return_outer(value, count, inner):
    outer = count // inner
    blocks = value.reshape(outer, -1, value.shape[-1])
    rounded = blocks.astype(jnp.bfloat16)
    total = blocks[0]
    for step in range(1, outer):
        total = total + shift_outer(rounded[step], count, inner, -step).astype(jnp.float32)
    return total.astype(jnp.bfloat16)


def dense_local(tokens, cotangent, gate_values, expert_ids, packing, w_gate, w_up, w_down):
    model_width = tokens.shape[1]
    half = w_gate.shape[1]
    count = lax.axis_size("expert")
    inner = 4
    row_count = tokens.shape[0]
    low = jnp.bfloat16
    ids, gates, lists = expert_ids.T, gate_values.T, packing.reshape(1, row_count)
    token_blocks = along_outer(tokens, count, inner)
    table, own_tokens, own_cotangent = on_chip(
        read_kernel,
        [
            ((count + 16, row_count), low),
            (tokens.shape, low),
            (cotangent.shape, low),
        ],
        ids,
        gates,
        lists,
        tokens,
        cotangent,
        spec=ANY,
        limit=False,
        scratch=[
            pltpu.VMEM(ids.shape, ids.dtype),
            pltpu.VMEM(gates.shape, gates.dtype),
            pltpu.VMEM(lists.shape, lists.dtype),
            pltpu.SemaphoreType.DMA((5,)),
        ],
    )
    payload, here = on_chip(
        payload_kernel,
        [((row_count, model_width + count), low), ((8, count), jnp.float32)],
        table,
        swap(table),
        own_cotangent,
    )
    token_column = jnp.concatenate([own_tokens, *token_blocks[1:]], axis=0)
    payload, token_column = lax.optimization_barrier((payload, token_column))
    token_near = near_inner(token_column, count)
    upstream_column = stack(along_outer(payload, count, inner))
    near_rows = stack([token_column, *token_near])
    near_rows, upstream_column, weights = lax.optimization_barrier(
        (near_rows, upstream_column, [w_gate[0], w_up[0], w_down[0]])
    )
    own_weights = jnp.concatenate(weights, axis=0)
    depth = token_column.shape[0]
    token_near = [near_rows[depth : 2 * depth], near_rows[2 * depth :]]
    upstream_near = near_inner(upstream_column, count)
    token_far = far_inner(token_near, count)
    other = swap(own_weights)
    inputs = jnp.concatenate([near_rows, *token_far], axis=0)
    upstream_near, inputs = lax.optimization_barrier((upstream_near, inputs))
    upstream = jnp.concatenate(
        [upstream_column, *upstream_near, *far_inner(upstream_near, count)], axis=0
    )
    other_inputs = swap(inputs)
    gate = jnp.sum(
        upstream[:, model_width:].astype(jnp.float32) * here[:1], axis=1, keepdims=True
    )
    upstream = upstream[:, :model_width]
    gate_up = jnp.concatenate(
        [own_weights[:half], other[:half], own_weights[half : 2 * half], other[half : 2 * half]],
        axis=0,
    )
    down = jnp.concatenate([own_weights[2 * half :], other[2 * half :]], axis=0)
    pre = jnp.dot(inputs, gate_up.T, preferred_element_type=jnp.float32)
    gate_pre, up_pre = pre[:, : 2 * half], pre[:, 2 * half :]
    hidden_grad = gate * jnp.dot(upstream, down.T, preferred_element_type=jnp.float32)
    sigmoid_val = jax.nn.sigmoid(gate_pre)
    activated = gate_pre * sigmoid_val
    hidden = (gate * activated * up_pre).astype(jnp.bfloat16)
    silu_slope = sigmoid_val * (1.0 + gate_pre * (1.0 - sigmoid_val))
    gate_grad = (hidden_grad * up_pre * silu_slope).astype(jnp.bfloat16)
    up_grad = (hidden_grad * activated).astype(jnp.bfloat16)
    both_grad = jnp.concatenate([gate_grad, up_grad], axis=1)
    partial_grad = jnp.dot(both_grad, gate_up, preferred_element_type=jnp.float32)
    partial_grad = partial_grad.astype(jnp.bfloat16)
    column_sum = return_inner(partial_grad, count, inner)
    grads = (gate_grad, up_grad, hidden)
    own_grads = jnp.concatenate([grad[:, :half] for grad in grads], axis=1)
    sent_grads = jnp.concatenate([grad[:, half:] for grad in grads], axis=1)
    sent_grads, upstream, _ = lax.optimization_barrier((sent_grads, upstream, partial_grad))
    other_grads = swap(sent_grads)
    other_upstream = swap(upstream)
    column_sum, other_grads, other_inputs, other_upstream = lax.optimization_barrier(
        (column_sum, other_grads, other_inputs, other_upstream)
    )
    input_grad = return_outer(column_sum, count, inner)
    weight_grads = on_chip(
        weight_kernel,
        [((1, half, model_width), low)] * 3,
        own_grads,
        other_grads,
        inputs,
        other_inputs,
        upstream,
        other_upstream,
    )
    return (input_grad, *weight_grads)


def local(tokens, cotangent, gate_values, expert_ids, packing, w_gate, w_up, w_down):
    row_count, top = expert_ids.shape
    count = lax.axis_size("expert")
    expert_count = count * w_gate.shape[0]
    capacity = min(row_count, max(2, row_count * top // expert_count + 1))
    few = capacity * 4 <= row_count
    regular = lax.axis_size("dp") == 2 and count % 4 == 0 and w_gate.shape[0] == 1
    chosen = dense_local if regular and not few else routed_local
    return chosen(
        tokens, cotangent, gate_values, expert_ids, packing, w_gate, w_up, w_down
    )


def solution(mesh):
    in_specs = (
        P(("groups", "dp", "expert"), None),
        P(("groups", "dp", "expert"), None),
        P(("groups", "dp", "expert"), None),
        P(("groups", "dp", "expert"), None),
        P(("groups", "dp", "expert")),
        P("expert", "dp", None),
        P("expert", "dp", None),
        P("expert", "dp", None),
    )
    out_specs = (
        P(("groups", "dp", "expert"), None),
        P(("groups", "expert"), "dp", None),
        P(("groups", "expert"), "dp", None),
        P(("groups", "expert"), "dp", None),
    )
    return jax.shard_map(local, mesh=mesh, in_specs=in_specs, out_specs=out_specs, check_vma=False)
```

```python
import math

import jax
import jax.numpy as jnp
from jax import lax
from jax.experimental import pallas as pl
from jax.experimental.pallas import tpu as pltpu
from jax.sharding import PartitionSpec as P


def slot_table(route_ids, route_gates, expert_count, capacity):
    row_count, top_count = route_ids.shape
    flat_ids = route_ids.reshape(-1)
    labels = jnp.arange(expert_count, dtype=jnp.int32)
    onehot = (flat_ids[:, None] == labels[None, :]).astype(jnp.int32)
    earlier = jnp.cumsum(onehot, axis=0) - onehot
    rank_in = jnp.sum(earlier * onehot, axis=1)
    position = flat_ids * capacity + rank_in
    places = jnp.arange(expert_count * capacity, dtype=jnp.int32)
    matched = places[:, None] == position[None, :]
    owner_row = jnp.arange(row_count * top_count, dtype=jnp.int32) // top_count
    occupied = jnp.any(matched, axis=1)
    slot_row = jnp.sum(jnp.where(matched, owner_row[None, :], 0), axis=1)
    flat_gates = route_gates.reshape(-1).astype(jnp.float32)
    slot_gate = jnp.sum(jnp.where(matched, flat_gates[None, :], 0.0), axis=1)
    return (position.reshape(row_count, top_count), occupied, slot_row, slot_gate)


def pick_rows(slot_lists, pooled):
    sources = jnp.arange(pooled.shape[0], dtype=jnp.int32)
    choose = (slot_lists[:, None] == sources[None, :]).astype(jnp.bfloat16)
    return jnp.dot(choose, pooled, preferred_element_type=jnp.float32).astype(jnp.bfloat16)


def fill_slots(rebal_rows, rebal_upstream, occupied, slot_row, slot_gate):
    send_rows = jnp.where(occupied[:, None], rebal_rows[slot_row], jnp.zeros((), jnp.bfloat16))
    scaled = slot_gate[:, None] * rebal_upstream[slot_row].astype(jnp.float32)
    send_upstream = jnp.where(occupied[:, None], scaled, 0.0).astype(jnp.bfloat16)
    return (send_rows, send_upstream)


def expert_terms(inputs, upstream, gate_mat, up_mat, down_mat):
    gate_pre = jnp.dot(inputs, gate_mat.T, preferred_element_type=jnp.float32)
    up_pre = jnp.dot(inputs, up_mat.T, preferred_element_type=jnp.float32)
    sigmoid_val = jax.nn.sigmoid(gate_pre)
    activated = gate_pre * sigmoid_val
    hidden = (activated * up_pre).astype(jnp.bfloat16)
    hidden_grad = jnp.dot(upstream, down_mat.T, preferred_element_type=jnp.float32)
    silu_slope = sigmoid_val * (1.0 + gate_pre * (1.0 - sigmoid_val))
    gate_grad = (hidden_grad * up_pre * silu_slope).astype(jnp.bfloat16)
    up_grad = (hidden_grad * activated).astype(jnp.bfloat16)
    weight_grads = (
        jnp.dot(gate_grad.T, inputs, preferred_element_type=jnp.float32).astype(jnp.bfloat16)[None],
        jnp.dot(up_grad.T, inputs, preferred_element_type=jnp.float32).astype(jnp.bfloat16)[None],
        jnp.dot(hidden.T, upstream, preferred_element_type=jnp.float32).astype(jnp.bfloat16)[None],
    )
    partial_grad = jnp.dot(gate_grad, gate_mat, preferred_element_type=jnp.float32)
    partial_grad = partial_grad + jnp.dot(up_grad, up_mat, preferred_element_type=jnp.float32)
    return (weight_grads, partial_grad)


def routed_local(tokens, cotangent, gate_values, expert_ids, packing, w_gate, w_up, w_down):
    row_count, top_count = expert_ids.shape
    model_width = tokens.shape[1]
    dp_size = lax.axis_size("dp")
    expert_count = lax.axis_size("expert") * w_gate.shape[0]
    capacity = min(row_count, max(2, row_count * top_count // expert_count + 1))
    gate_mat = w_gate[0]
    up_mat = w_up[0]
    down_mat = w_down[0]
    pooled_rows, pooled_upstream, pooled_gates = (
        lax.all_gather(tokens, "dp", axis=0, tiled=True),
        lax.all_gather(cotangent, "dp", axis=0, tiled=True),
        lax.all_gather(gate_values, "dp", axis=0, tiled=True),
    )
    lists_all, pooled_ids = (
        lax.all_gather(packing, "dp", axis=0, tiled=True),
        lax.all_gather(expert_ids, "dp", axis=0, tiled=True),
    )
    member_rows = []
    member_upstream = []
    member_positions = []
    for member in range(dp_size):
        low = member * row_count
        slot_lists = lists_all[low : low + row_count]
        position, occupied, slot_row, slot_gate = slot_table(
            pooled_ids[low : low + row_count],
            pooled_gates[low : low + row_count],
            expert_count,
            capacity,
        )
        send_rows, send_upstream = fill_slots(
            pick_rows(slot_lists, pooled_rows),
            pick_rows(slot_lists, pooled_upstream),
            occupied,
            slot_row,
            slot_gate,
        )
        member_rows.append(send_rows.reshape(expert_count, capacity * model_width))
        member_upstream.append(send_upstream.reshape(expert_count, capacity * model_width))
        member_positions.append(position)
    own_position = jnp.stack(member_positions)[lax.axis_index("dp")]
    send_rows = jnp.concatenate(member_rows, axis=1).reshape(
        expert_count * dp_size * capacity, model_width
    )
    send_upstream = jnp.concatenate(member_upstream, axis=1).reshape(
        expert_count * dp_size * capacity, model_width
    )
    recv_rows, recv_upstream = (
        lax.all_to_all(send_rows, "expert", split_axis=0, concat_axis=0, tiled=True),
        lax.all_to_all(send_upstream, "expert", split_axis=0, concat_axis=0, tiled=True),
    )
    weight_grads, partial_grad = expert_terms(recv_rows, recv_upstream, gate_mat, up_mat, down_mat)
    summed = lax.psum_scatter(
        partial_grad.reshape(expert_count, dp_size * capacity * model_width).astype(jnp.bfloat16),
        "dp",
        scatter_dimension=1,
        tiled=True,
    ).astype(jnp.float32)
    slot_grad = summed.reshape(expert_count * capacity, model_width).astype(jnp.bfloat16)
    returned = lax.all_to_all(slot_grad, "expert", split_axis=0, concat_axis=0, tiled=True)
    rebal_grad = jnp.sum(returned[own_position].astype(jnp.float32), axis=1).astype(jnp.bfloat16)
    pooled_grad = lax.all_gather(rebal_grad, "dp", axis=0, tiled=True)
    home_index = lax.axis_index("dp") * row_count + jnp.arange(row_count, dtype=jnp.int32)
    choose = (lists_all[None, :] == home_index[:, None]).astype(jnp.bfloat16)
    input_grad = jnp.dot(choose, pooled_grad, preferred_element_type=jnp.float32).astype(
        jnp.bfloat16
    )
    return (input_grad, weight_grads[0], weight_grads[1], weight_grads[2])


def swap(value):
    return lax.ppermute(value, "dp", [(0, 1), (1, 0)])


def shift_outer(value, count, inner, step):
    return lax.ppermute(
        value, "expert", [(place, (place + step * inner) % count) for place in range(count)]
    )


def swap_inner(value, count, partner):
    return lax.ppermute(value, "expert", [(place, place ^ partner) for place in range(count)])


VMEM = pl.BlockSpec(memory_space=pltpu.VMEM)
ANY = pl.BlockSpec(memory_space=pl.ANY)
NT = (((1,), (1,)), ((), ()))
TN = (((0,), (0,)), ((), ()))


def on_chip(body, outs, *args, scratch=(), spec=VMEM, limit=True):
    moved = sum(arg.size * arg.dtype.itemsize for arg in args)
    moved += sum(math.prod(shape) * jnp.dtype(dtype).itemsize for shape, dtype in outs)
    granted = {"vmem_limit_bytes": moved + (4 << 20)} if limit else {}
    return pl.pallas_call(
        body,
        out_shape=[jax.ShapeDtypeStruct(shape, dtype) for shape, dtype in outs],
        in_specs=[spec] * len(args),
        out_specs=[VMEM] * len(outs),
        scratch_shapes=list(scratch),
        compiler_params=pltpu.CompilerParams(**granted),
        cost_estimate=pl.CostEstimate(flops=0, bytes_accessed=moved, transcendentals=0),
    )(*args)


def read_kernel(
    ids_hbm, gates_hbm, packing_hbm, tokens_hbm, cotangent_hbm,
    table_ref, tokens_ref, cotangent_ref,
    ids_ref, gates_ref, packing_ref, ready,
):
    pairs = [
        (ids_hbm, ids_ref),
        (gates_hbm, gates_ref),
        (packing_hbm, packing_ref),
        (tokens_hbm, tokens_ref),
        (cotangent_hbm, cotangent_ref),
    ]
    copies = [
        pltpu.make_async_copy(source, target, ready.at[index])
        for index, (source, target) in enumerate(pairs)
    ]
    for copy in copies:
        copy.start()
    for copy in copies:
        copy.wait()
    slots = packing_ref.shape[1]
    count = table_ref.shape[0] - 16
    labels = lax.broadcasted_iota(jnp.int32, (count, slots), 0)
    total = jnp.zeros((count, slots), jnp.float32)
    for k in range(ids_ref.shape[0]):
        named = labels == ids_ref[k : k + 1, :]
        total = total + jnp.where(named, gates_ref[k : k + 1, :].astype(jnp.float32), 0.0)
    table_ref[:count, :] = total.astype(jnp.bfloat16)
    lists = jnp.broadcast_to(packing_ref[...], (16, slots)).astype(jnp.float32)
    table_ref[count:, :] = lists.astype(jnp.bfloat16)


def payload_kernel(table_ref, other_ref, cotangent_ref, payload_ref, here_ref):
    rows, width = cotangent_ref.shape
    count = table_ref.shape[0] - 16
    slots = table_ref.shape[1]
    homes = lax.broadcasted_iota(jnp.int32, (rows, slots), 0) + lax.axis_index("dp") * rows
    gates = jnp.zeros((rows, count), jnp.float32)
    for ref in (table_ref, other_ref):
        lists = ref[count:, :].astype(jnp.float32)[:1, :]
        matched = (lists == homes.astype(jnp.float32)).astype(jnp.float32).astype(jnp.bfloat16)
        gates = gates + lax.dot_general(
            matched, ref[:count, :], NT, preferred_element_type=jnp.float32
        )
    payload_ref[:, :width] = cotangent_ref[...]
    payload_ref[:, width:] = gates.astype(jnp.bfloat16)
    lanes = lax.broadcasted_iota(jnp.int32, here_ref.shape, 1)
    here_ref[...] = (lanes == lax.axis_index("expert")).astype(jnp.float32)


def weight_kernel(own_grads, other_grads, rows, other_rows, upstream, other_upstream, *outs):
    half = outs[0].shape[1]
    for index, out in enumerate(outs):
        own, other = (upstream, other_upstream) if index == 2 else (rows, other_rows)
        span = slice(index * half, (index + 1) * half)
        step = min(out.shape[-1], 1024)
        for left in range(0, out.shape[-1], step):
            columns = slice(left, left + step)
            total = lax.dot_general(
                own_grads[:, span], own[:, columns], TN, preferred_element_type=jnp.float32
            ) + lax.dot_general(
                other_grads[:, span], other[:, columns], TN, preferred_element_type=jnp.float32
            )
            out[0, :, columns] = total.astype(jnp.bfloat16)


def along_outer(value, count, inner):
    return [value] + [shift_outer(value, count, inner, step) for step in range(1, count // inner)]


def across_inner(column, count, inner):
    if inner < 4:
        return [column] + [swap_inner(column, count, partner) for partner in range(1, inner)]
    cut = column.shape[0] // 2
    first = swap_inner(column, count, 1)
    second = swap_inner(column, count, 2)
    far_top = swap_inner(first[:cut], count, 2)
    far_bottom = swap_inner(second[cut:], count, 1)
    return [column, first, second, far_top, far_bottom]


def return_inner(value, count, inner):
    blocks = value.reshape(inner, -1, value.shape[-1])
    total = blocks[0].astype(jnp.float32)
    for partner in range(1, inner):
        total = total + swap_inner(blocks[partner], count, partner).astype(jnp.float32)
    return total


def return_outer(value, count, inner):
    outer = count // inner
    blocks = value.reshape(outer, -1, value.shape[-1])
    rounded = blocks.astype(jnp.bfloat16)
    total = blocks[0]
    for step in range(1, outer):
        total = total + shift_outer(rounded[step], count, inner, -step).astype(jnp.float32)
    return total.astype(jnp.bfloat16)


def dense_local(tokens, cotangent, gate_values, expert_ids, packing, w_gate, w_up, w_down):
    model_width = tokens.shape[1]
    half = w_gate.shape[1]
    count = lax.axis_size("expert")
    inner = 4
    row_count = tokens.shape[0]
    low = jnp.bfloat16
    ids, gates, lists = expert_ids.T, gate_values.T, packing.reshape(1, row_count)
    token_blocks = along_outer(tokens, count, inner)
    table, own_tokens, own_cotangent = on_chip(
        read_kernel,
        [
            ((count + 16, row_count), low),
            (tokens.shape, low),
            (cotangent.shape, low),
        ],
        ids,
        gates,
        lists,
        tokens,
        cotangent,
        spec=ANY,
        limit=False,
        scratch=[
            pltpu.VMEM(ids.shape, ids.dtype),
            pltpu.VMEM(gates.shape, gates.dtype),
            pltpu.VMEM(lists.shape, lists.dtype),
            pltpu.SemaphoreType.DMA((5,)),
        ],
    )
    payload, here = on_chip(
        payload_kernel,
        [((row_count, model_width + count), low), ((8, count), jnp.float32)],
        table,
        swap(table),
        own_cotangent,
    )
    token_column = jnp.concatenate([own_tokens, *token_blocks[1:]], axis=0)
    early = shift_outer(payload, count, inner, 2)
    payload, token_column = lax.optimization_barrier((payload, token_column))
    upstream_blocks = [payload, shift_outer(payload, count, inner, 1), early]
    upstream_blocks.append(shift_outer(payload, count, inner, 3))
    upstream_column = jnp.concatenate(upstream_blocks, axis=0)
    token_columns = across_inner(token_column, count, inner)
    own_weights = jnp.concatenate([w_gate[0], w_up[0], w_down[0]], axis=0)
    sent_weights, token_columns[1] = lax.optimization_barrier((own_weights, token_columns[1]))
    other = swap(sent_weights)
    inputs = jnp.concatenate(token_columns, axis=0)
    other_inputs = swap(inputs)
    upstream = jnp.concatenate(across_inner(upstream_column, count, inner), axis=0)
    gate = jnp.sum(
        upstream[:, model_width:].astype(jnp.float32) * here[:1], axis=1, keepdims=True
    )
    upstream = upstream[:, :model_width]
    gate_up = jnp.concatenate(
        [own_weights[:half], other[:half], own_weights[half : 2 * half], other[half : 2 * half]],
        axis=0,
    )
    down = jnp.concatenate([own_weights[2 * half :], other[2 * half :]], axis=0)
    pre = jnp.dot(inputs, gate_up.T, preferred_element_type=jnp.float32)
    gate_pre, up_pre = pre[:, : 2 * half], pre[:, 2 * half :]
    hidden_grad = gate * jnp.dot(upstream, down.T, preferred_element_type=jnp.float32)
    sigmoid_val = jax.nn.sigmoid(gate_pre)
    activated = gate_pre * sigmoid_val
    hidden = (gate * activated * up_pre).astype(jnp.bfloat16)
    silu_slope = sigmoid_val * (1.0 + gate_pre * (1.0 - sigmoid_val))
    gate_grad = (hidden_grad * up_pre * silu_slope).astype(jnp.bfloat16)
    up_grad = (hidden_grad * activated).astype(jnp.bfloat16)
    both_grad = jnp.concatenate([gate_grad, up_grad], axis=1)
    partial_grad = jnp.dot(both_grad, gate_up, preferred_element_type=jnp.float32)
    partial_grad = partial_grad.astype(jnp.bfloat16)
    column_sum = return_inner(partial_grad, count, inner)
    grads = (gate_grad, up_grad, hidden)
    own_grads = jnp.concatenate([grad[:, :half] for grad in grads], axis=1)
    sent_grads = jnp.concatenate([grad[:, half:] for grad in grads], axis=1)
    sent_grads, upstream, _ = lax.optimization_barrier((sent_grads, upstream, partial_grad))
    other_grads = swap(sent_grads)
    other_upstream = swap(upstream)
    column_sum, other_grads, other_inputs, other_upstream = lax.optimization_barrier(
        (column_sum, other_grads, other_inputs, other_upstream)
    )
    input_grad = return_outer(column_sum, count, inner)
    weight_grads = on_chip(
        weight_kernel,
        [((1, half, model_width), low)] * 3,
        own_grads,
        other_grads,
        inputs,
        other_inputs,
        upstream,
        other_upstream,
    )
    return (input_grad, *weight_grads)


def local(tokens, cotangent, gate_values, expert_ids, packing, w_gate, w_up, w_down):
    row_count, top = expert_ids.shape
    count = lax.axis_size("expert")
    expert_count = count * w_gate.shape[0]
    capacity = min(row_count, max(2, row_count * top // expert_count + 1))
    few = capacity * 4 <= row_count
    regular = lax.axis_size("dp") == 2 and count % 4 == 0 and w_gate.shape[0] == 1
    chosen = dense_local if regular and not few else routed_local
    return chosen(
        tokens, cotangent, gate_values, expert_ids, packing, w_gate, w_up, w_down
    )


def solution(mesh):
    in_specs = (
        P(("groups", "dp", "expert"), None),
        P(("groups", "dp", "expert"), None),
        P(("groups", "dp", "expert"), None),
        P(("groups", "dp", "expert"), None),
        P(("groups", "dp", "expert")),
        P("expert", "dp", None),
        P("expert", "dp", None),
        P("expert", "dp", None),
    )
    out_specs = (
        P(("groups", "dp", "expert"), None),
        P(("groups", "expert"), "dp", None),
        P(("groups", "expert"), "dp", None),
        P(("groups", "expert"), "dp", None),
    )
    return jax.shard_map(local, mesh=mesh, in_specs=in_specs, out_specs=out_specs, check_vma=False)
```

```python
import math

import jax
import jax.numpy as jnp
from jax import lax
from jax.experimental import pallas as pl
from jax.experimental.pallas import tpu as pltpu
from jax.sharding import PartitionSpec as P


def slot_table(route_ids, route_gates, expert_count, capacity):
    row_count, top_count = route_ids.shape
    flat_ids = route_ids.reshape(-1)
    labels = jnp.arange(expert_count, dtype=jnp.int32)
    onehot = (flat_ids[:, None] == labels[None, :]).astype(jnp.int32)
    earlier = jnp.cumsum(onehot, axis=0) - onehot
    rank_in = jnp.sum(earlier * onehot, axis=1)
    position = flat_ids * capacity + rank_in
    places = jnp.arange(expert_count * capacity, dtype=jnp.int32)
    matched = places[:, None] == position[None, :]
    owner_row = jnp.arange(row_count * top_count, dtype=jnp.int32) // top_count
    occupied = jnp.any(matched, axis=1)
    slot_row = jnp.sum(jnp.where(matched, owner_row[None, :], 0), axis=1)
    flat_gates = route_gates.reshape(-1).astype(jnp.float32)
    slot_gate = jnp.sum(jnp.where(matched, flat_gates[None, :], 0.0), axis=1)
    return (position.reshape(row_count, top_count), occupied, slot_row, slot_gate)


def pick_rows(slot_lists, pooled):
    sources = jnp.arange(pooled.shape[0], dtype=jnp.int32)
    choose = (slot_lists[:, None] == sources[None, :]).astype(jnp.bfloat16)
    return jnp.dot(choose, pooled, preferred_element_type=jnp.float32).astype(jnp.bfloat16)


def fill_slots(rebal_rows, rebal_upstream, occupied, slot_row, slot_gate):
    send_rows = jnp.where(occupied[:, None], rebal_rows[slot_row], jnp.zeros((), jnp.bfloat16))
    scaled = slot_gate[:, None] * rebal_upstream[slot_row].astype(jnp.float32)
    send_upstream = jnp.where(occupied[:, None], scaled, 0.0).astype(jnp.bfloat16)
    return (send_rows, send_upstream)


def expert_terms(inputs, upstream, gate_mat, up_mat, down_mat):
    gate_pre = jnp.dot(inputs, gate_mat.T, preferred_element_type=jnp.float32)
    up_pre = jnp.dot(inputs, up_mat.T, preferred_element_type=jnp.float32)
    sigmoid_val = jax.nn.sigmoid(gate_pre)
    activated = gate_pre * sigmoid_val
    hidden = (activated * up_pre).astype(jnp.bfloat16)
    hidden_grad = jnp.dot(upstream, down_mat.T, preferred_element_type=jnp.float32)
    silu_slope = sigmoid_val * (1.0 + gate_pre * (1.0 - sigmoid_val))
    gate_grad = (hidden_grad * up_pre * silu_slope).astype(jnp.bfloat16)
    up_grad = (hidden_grad * activated).astype(jnp.bfloat16)
    weight_grads = (
        jnp.dot(gate_grad.T, inputs, preferred_element_type=jnp.float32).astype(jnp.bfloat16)[None],
        jnp.dot(up_grad.T, inputs, preferred_element_type=jnp.float32).astype(jnp.bfloat16)[None],
        jnp.dot(hidden.T, upstream, preferred_element_type=jnp.float32).astype(jnp.bfloat16)[None],
    )
    partial_grad = jnp.dot(gate_grad, gate_mat, preferred_element_type=jnp.float32)
    partial_grad = partial_grad + jnp.dot(up_grad, up_mat, preferred_element_type=jnp.float32)
    return (weight_grads, partial_grad)


def routed_local(tokens, cotangent, gate_values, expert_ids, packing, w_gate, w_up, w_down):
    row_count, top_count = expert_ids.shape
    model_width = tokens.shape[1]
    dp_size = lax.axis_size("dp")
    expert_count = lax.axis_size("expert") * w_gate.shape[0]
    capacity = min(row_count, max(2, row_count * top_count // expert_count + 1))
    gate_mat = w_gate[0]
    up_mat = w_up[0]
    down_mat = w_down[0]
    pooled_rows, pooled_upstream, pooled_gates = (
        lax.all_gather(tokens, "dp", axis=0, tiled=True),
        lax.all_gather(cotangent, "dp", axis=0, tiled=True),
        lax.all_gather(gate_values, "dp", axis=0, tiled=True),
    )
    lists_all, pooled_ids = (
        lax.all_gather(packing, "dp", axis=0, tiled=True),
        lax.all_gather(expert_ids, "dp", axis=0, tiled=True),
    )
    member_rows = []
    member_upstream = []
    member_positions = []
    for member in range(dp_size):
        low = member * row_count
        slot_lists = lists_all[low : low + row_count]
        position, occupied, slot_row, slot_gate = slot_table(
            pooled_ids[low : low + row_count],
            pooled_gates[low : low + row_count],
            expert_count,
            capacity,
        )
        send_rows, send_upstream = fill_slots(
            pick_rows(slot_lists, pooled_rows),
            pick_rows(slot_lists, pooled_upstream),
            occupied,
            slot_row,
            slot_gate,
        )
        member_rows.append(send_rows.reshape(expert_count, capacity * model_width))
        member_upstream.append(send_upstream.reshape(expert_count, capacity * model_width))
        member_positions.append(position)
    own_position = jnp.stack(member_positions)[lax.axis_index("dp")]
    send_rows = jnp.concatenate(member_rows, axis=1).reshape(
        expert_count * dp_size * capacity, model_width
    )
    send_upstream = jnp.concatenate(member_upstream, axis=1).reshape(
        expert_count * dp_size * capacity, model_width
    )
    recv_rows, recv_upstream = (
        lax.all_to_all(send_rows, "expert", split_axis=0, concat_axis=0, tiled=True),
        lax.all_to_all(send_upstream, "expert", split_axis=0, concat_axis=0, tiled=True),
    )
    weight_grads, partial_grad = expert_terms(recv_rows, recv_upstream, gate_mat, up_mat, down_mat)
    summed = lax.psum_scatter(
        partial_grad.reshape(expert_count, dp_size * capacity * model_width).astype(jnp.bfloat16),
        "dp",
        scatter_dimension=1,
        tiled=True,
    ).astype(jnp.float32)
    slot_grad = summed.reshape(expert_count * capacity, model_width).astype(jnp.bfloat16)
    returned = lax.all_to_all(slot_grad, "expert", split_axis=0, concat_axis=0, tiled=True)
    rebal_grad = jnp.sum(returned[own_position].astype(jnp.float32), axis=1).astype(jnp.bfloat16)
    pooled_grad = lax.all_gather(rebal_grad, "dp", axis=0, tiled=True)
    home_index = lax.axis_index("dp") * row_count + jnp.arange(row_count, dtype=jnp.int32)
    choose = (lists_all[None, :] == home_index[:, None]).astype(jnp.bfloat16)
    input_grad = jnp.dot(choose, pooled_grad, preferred_element_type=jnp.float32).astype(
        jnp.bfloat16
    )
    return (input_grad, weight_grads[0], weight_grads[1], weight_grads[2])


def swap(value):
    return lax.ppermute(value, "dp", [(0, 1), (1, 0)])


def shift_outer(value, count, inner, step):
    return lax.ppermute(
        value, "expert", [(place, (place + step * inner) % count) for place in range(count)]
    )


def swap_inner(value, count, partner):
    return lax.ppermute(value, "expert", [(place, place ^ partner) for place in range(count)])


VMEM = pl.BlockSpec(memory_space=pltpu.VMEM)
ANY = pl.BlockSpec(memory_space=pl.ANY)
NT = (((1,), (1,)), ((), ()))
TN = (((0,), (0,)), ((), ()))


def on_chip(body, outs, *args, scratch=(), spec=VMEM, limit=True):
    moved = sum(arg.size * arg.dtype.itemsize for arg in args)
    moved += sum(math.prod(shape) * jnp.dtype(dtype).itemsize for shape, dtype in outs)
    granted = {"vmem_limit_bytes": moved + (4 << 20)} if limit else {}
    return pl.pallas_call(
        body,
        out_shape=[jax.ShapeDtypeStruct(shape, dtype) for shape, dtype in outs],
        in_specs=[spec] * len(args),
        out_specs=[VMEM] * len(outs),
        scratch_shapes=list(scratch),
        compiler_params=pltpu.CompilerParams(**granted),
        cost_estimate=pl.CostEstimate(flops=0, bytes_accessed=moved, transcendentals=0),
    )(*args)


def read_kernel(
    ids_hbm, gates_hbm, packing_hbm, tokens_hbm, cotangent_hbm,
    table_ref, tokens_ref, cotangent_ref,
    ids_ref, gates_ref, packing_ref, ready,
):
    pairs = [
        (ids_hbm, ids_ref),
        (gates_hbm, gates_ref),
        (packing_hbm, packing_ref),
        (tokens_hbm, tokens_ref),
        (cotangent_hbm, cotangent_ref),
    ]
    copies = [
        pltpu.make_async_copy(source, target, ready.at[index])
        for index, (source, target) in enumerate(pairs)
    ]
    for copy in copies:
        copy.start()
    for copy in copies:
        copy.wait()
    slots = packing_ref.shape[1]
    count = table_ref.shape[0] - 16
    labels = lax.broadcasted_iota(jnp.int32, (count, slots), 0)
    total = jnp.zeros((count, slots), jnp.float32)
    for k in range(ids_ref.shape[0]):
        named = labels == ids_ref[k : k + 1, :]
        total = total + jnp.where(named, gates_ref[k : k + 1, :].astype(jnp.float32), 0.0)
    table_ref[:count, :] = total.astype(jnp.bfloat16)
    lists = jnp.broadcast_to(packing_ref[...], (16, slots)).astype(jnp.float32)
    table_ref[count:, :] = lists.astype(jnp.bfloat16)


def payload_kernel(table_ref, other_ref, cotangent_ref, payload_ref, here_ref):
    rows, width = cotangent_ref.shape
    count = table_ref.shape[0] - 16
    slots = table_ref.shape[1]
    homes = lax.broadcasted_iota(jnp.int32, (rows, slots), 0) + lax.axis_index("dp") * rows
    gates = jnp.zeros((rows, count), jnp.float32)
    for ref in (table_ref, other_ref):
        lists = ref[count:, :].astype(jnp.float32)[:1, :]
        matched = (lists == homes.astype(jnp.float32)).astype(jnp.float32).astype(jnp.bfloat16)
        gates = gates + lax.dot_general(
            matched, ref[:count, :], NT, preferred_element_type=jnp.float32
        )
    payload_ref[:, :width] = cotangent_ref[...]
    payload_ref[:, width:] = gates.astype(jnp.bfloat16)
    lanes = lax.broadcasted_iota(jnp.int32, here_ref.shape, 1)
    here_ref[...] = (lanes == lax.axis_index("expert")).astype(jnp.float32)


def weight_kernel(own_grads, other_grads, rows, other_rows, upstream, other_upstream, *outs):
    half = outs[0].shape[1]
    for index, out in enumerate(outs):
        own, other = (upstream, other_upstream) if index == 2 else (rows, other_rows)
        span = slice(index * half, (index + 1) * half)
        step = min(out.shape[-1], 1024)
        for left in range(0, out.shape[-1], step):
            columns = slice(left, left + step)
            total = lax.dot_general(
                own_grads[:, span], own[:, columns], TN, preferred_element_type=jnp.float32
            ) + lax.dot_general(
                other_grads[:, span], other[:, columns], TN, preferred_element_type=jnp.float32
            )
            out[0, :, columns] = total.astype(jnp.bfloat16)


def join_kernel(own_ref, other_ref, gate_up_ref, down_ref):
    half = own_ref.shape[0] // 3
    for index, ref in enumerate((own_ref, other_ref)):
        for kind in range(2):
            low = (2 * kind + index) * half
            gate_up_ref[low : low + half, :] = ref[kind * half : (kind + 1) * half, :]
        down_ref[index * half : (index + 1) * half, :] = ref[2 * half :, :]


def along_outer(value, count, inner):
    return [value] + [shift_outer(value, count, inner, step) for step in range(1, count // inner)]


def across_inner(column, count, inner):
    if inner < 4:
        return [column] + [swap_inner(column, count, partner) for partner in range(1, inner)]
    cut = column.shape[0] // 2
    first = swap_inner(column, count, 1)
    second = swap_inner(column, count, 2)
    far_top = swap_inner(first[:cut], count, 2)
    far_bottom = swap_inner(second[cut:], count, 1)
    return [column, first, second, far_top, far_bottom]


def return_inner(value, count, inner):
    blocks = value.reshape(inner, -1, value.shape[-1])
    total = blocks[0].astype(jnp.float32)
    for partner in range(1, inner):
        total = total + swap_inner(blocks[partner], count, partner).astype(jnp.float32)
    return total


def return_outer(value, count, inner):
    outer = count // inner
    blocks = value.reshape(outer, -1, value.shape[-1])
    rounded = blocks.astype(jnp.bfloat16)
    total = blocks[0]
    for step in range(1, outer):
        total = total + shift_outer(rounded[step], count, inner, -step).astype(jnp.float32)
    return total.astype(jnp.bfloat16)


def dense_local(tokens, cotangent, gate_values, expert_ids, packing, w_gate, w_up, w_down):
    model_width = tokens.shape[1]
    half = w_gate.shape[1]
    count = lax.axis_size("expert")
    inner = 4
    row_count = tokens.shape[0]
    low = jnp.bfloat16
    ids, gates, lists = expert_ids.T, gate_values.T, packing.reshape(1, row_count)
    token_blocks = along_outer(tokens, count, inner)
    table, own_tokens, own_cotangent = on_chip(
        read_kernel,
        [
            ((count + 16, row_count), low),
            (tokens.shape, low),
            (cotangent.shape, low),
        ],
        ids,
        gates,
        lists,
        tokens,
        cotangent,
        spec=ANY,
        limit=False,
        scratch=[
            pltpu.VMEM(ids.shape, ids.dtype),
            pltpu.VMEM(gates.shape, gates.dtype),
            pltpu.VMEM(lists.shape, lists.dtype),
            pltpu.SemaphoreType.DMA((5,)),
        ],
    )
    payload, here = on_chip(
        payload_kernel,
        [((row_count, model_width + count), low), ((8, count), jnp.float32)],
        table,
        swap(table),
        own_cotangent,
    )
    token_column = jnp.concatenate([own_tokens, *token_blocks[1:]], axis=0)
    early = shift_outer(payload, count, inner, 2)
    payload, token_column = lax.optimization_barrier((payload, token_column))
    upstream_blocks = [payload, shift_outer(payload, count, inner, 1), early]
    upstream_blocks.append(shift_outer(payload, count, inner, 3))
    upstream_column = jnp.concatenate(upstream_blocks, axis=0)
    token_columns = across_inner(token_column, count, inner)
    own_weights = jnp.concatenate([w_gate[0], w_up[0], w_down[0]], axis=0)
    sent_weights, token_columns[1] = lax.optimization_barrier((own_weights, token_columns[1]))
    other = swap(sent_weights)
    inputs = jnp.concatenate(token_columns, axis=0)
    other_inputs = swap(inputs)
    upstream = jnp.concatenate(across_inner(upstream_column, count, inner), axis=0)
    gate = jnp.sum(
        upstream[:, model_width:].astype(jnp.float32) * here[:1], axis=1, keepdims=True
    )
    upstream = upstream[:, :model_width]
    gate_up, down = on_chip(
        join_kernel,
        [((4 * half, model_width), low), ((2 * half, model_width), low)],
        own_weights,
        other,
    )
    pre = jnp.dot(inputs, gate_up.T, preferred_element_type=jnp.float32)
    gate_pre, up_pre = pre[:, : 2 * half], pre[:, 2 * half :]
    hidden_grad = gate * jnp.dot(upstream, down.T, preferred_element_type=jnp.float32)
    sigmoid_val = jax.nn.sigmoid(gate_pre)
    activated = gate_pre * sigmoid_val
    hidden = (gate * activated * up_pre).astype(jnp.bfloat16)
    silu_slope = sigmoid_val * (1.0 + gate_pre * (1.0 - sigmoid_val))
    gate_grad = (hidden_grad * up_pre * silu_slope).astype(jnp.bfloat16)
    up_grad = (hidden_grad * activated).astype(jnp.bfloat16)
    both_grad = jnp.concatenate([gate_grad, up_grad], axis=1)
    partial_grad = jnp.dot(both_grad, gate_up, preferred_element_type=jnp.float32)
    partial_grad = partial_grad.astype(jnp.bfloat16)
    column_sum = return_inner(partial_grad, count, inner)
    grads = (gate_grad, up_grad, hidden)
    own_grads = jnp.concatenate([grad[:, :half] for grad in grads], axis=1)
    sent_grads = jnp.concatenate([grad[:, half:] for grad in grads], axis=1)
    sent_grads, upstream, _ = lax.optimization_barrier((sent_grads, upstream, partial_grad))
    other_grads = swap(sent_grads)
    other_upstream = swap(upstream)
    column_sum, other_grads, other_inputs, other_upstream = lax.optimization_barrier(
        (column_sum, other_grads, other_inputs, other_upstream)
    )
    input_grad = return_outer(column_sum, count, inner)
    weight_grads = on_chip(
        weight_kernel,
        [((1, half, model_width), low)] * 3,
        own_grads,
        other_grads,
        inputs,
        other_inputs,
        upstream,
        other_upstream,
    )
    return (input_grad, *weight_grads)


def local(tokens, cotangent, gate_values, expert_ids, packing, w_gate, w_up, w_down):
    row_count, top = expert_ids.shape
    count = lax.axis_size("expert")
    expert_count = count * w_gate.shape[0]
    capacity = min(row_count, max(2, row_count * top // expert_count + 1))
    few = capacity * 4 <= row_count
    regular = lax.axis_size("dp") == 2 and count % 4 == 0 and w_gate.shape[0] == 1
    chosen = dense_local if regular and not few else routed_local
    return chosen(
        tokens, cotangent, gate_values, expert_ids, packing, w_gate, w_up, w_down
    )


def solution(mesh):
    in_specs = (
        P(("groups", "dp", "expert"), None),
        P(("groups", "dp", "expert"), None),
        P(("groups", "dp", "expert"), None),
        P(("groups", "dp", "expert"), None),
        P(("groups", "dp", "expert")),
        P("expert", "dp", None),
        P("expert", "dp", None),
        P("expert", "dp", None),
    )
    out_specs = (
        P(("groups", "dp", "expert"), None),
        P(("groups", "expert"), "dp", None),
        P(("groups", "expert"), "dp", None),
        P(("groups", "expert"), "dp", None),
    )
    return jax.shard_map(local, mesh=mesh, in_specs=in_specs, out_specs=out_specs, check_vma=False)
```

```python
import math

import jax
import jax.numpy as jnp
from jax import lax
from jax.experimental import pallas as pl
from jax.experimental.pallas import tpu as pltpu
from jax.sharding import PartitionSpec as P


def slot_table(route_ids, route_gates, expert_count, capacity):
    row_count, top_count = route_ids.shape
    flat_ids = route_ids.reshape(-1)
    labels = jnp.arange(expert_count, dtype=jnp.int32)
    onehot = (flat_ids[:, None] == labels[None, :]).astype(jnp.int32)
    earlier = jnp.cumsum(onehot, axis=0) - onehot
    rank_in = jnp.sum(earlier * onehot, axis=1)
    position = flat_ids * capacity + rank_in
    places = jnp.arange(expert_count * capacity, dtype=jnp.int32)
    matched = places[:, None] == position[None, :]
    owner_row = jnp.arange(row_count * top_count, dtype=jnp.int32) // top_count
    occupied = jnp.any(matched, axis=1)
    slot_row = jnp.sum(jnp.where(matched, owner_row[None, :], 0), axis=1)
    flat_gates = route_gates.reshape(-1).astype(jnp.float32)
    slot_gate = jnp.sum(jnp.where(matched, flat_gates[None, :], 0.0), axis=1)
    return (position.reshape(row_count, top_count), occupied, slot_row, slot_gate)


def pick_rows(slot_lists, pooled):
    sources = jnp.arange(pooled.shape[0], dtype=jnp.int32)
    choose = (slot_lists[:, None] == sources[None, :]).astype(jnp.bfloat16)
    return jnp.dot(choose, pooled, preferred_element_type=jnp.float32).astype(jnp.bfloat16)


def fill_slots(rebal_rows, rebal_upstream, occupied, slot_row, slot_gate):
    send_rows = jnp.where(occupied[:, None], rebal_rows[slot_row], jnp.zeros((), jnp.bfloat16))
    scaled = slot_gate[:, None] * rebal_upstream[slot_row].astype(jnp.float32)
    send_upstream = jnp.where(occupied[:, None], scaled, 0.0).astype(jnp.bfloat16)
    return (send_rows, send_upstream)


def expert_terms(inputs, upstream, gate_mat, up_mat, down_mat):
    gate_pre = jnp.dot(inputs, gate_mat.T, preferred_element_type=jnp.float32)
    up_pre = jnp.dot(inputs, up_mat.T, preferred_element_type=jnp.float32)
    sigmoid_val = jax.nn.sigmoid(gate_pre)
    activated = gate_pre * sigmoid_val
    hidden = (activated * up_pre).astype(jnp.bfloat16)
    hidden_grad = jnp.dot(upstream, down_mat.T, preferred_element_type=jnp.float32)
    silu_slope = sigmoid_val * (1.0 + gate_pre * (1.0 - sigmoid_val))
    gate_grad = (hidden_grad * up_pre * silu_slope).astype(jnp.bfloat16)
    up_grad = (hidden_grad * activated).astype(jnp.bfloat16)
    weight_grads = (
        jnp.dot(gate_grad.T, inputs, preferred_element_type=jnp.float32).astype(jnp.bfloat16)[None],
        jnp.dot(up_grad.T, inputs, preferred_element_type=jnp.float32).astype(jnp.bfloat16)[None],
        jnp.dot(hidden.T, upstream, preferred_element_type=jnp.float32).astype(jnp.bfloat16)[None],
    )
    partial_grad = jnp.dot(gate_grad, gate_mat, preferred_element_type=jnp.float32)
    partial_grad = partial_grad + jnp.dot(up_grad, up_mat, preferred_element_type=jnp.float32)
    return (weight_grads, partial_grad)


def routed_local(tokens, cotangent, gate_values, expert_ids, packing, w_gate, w_up, w_down):
    row_count, top_count = expert_ids.shape
    model_width = tokens.shape[1]
    dp_size = lax.axis_size("dp")
    expert_count = lax.axis_size("expert") * w_gate.shape[0]
    capacity = min(row_count, max(2, row_count * top_count // expert_count + 1))
    gate_mat = w_gate[0]
    up_mat = w_up[0]
    down_mat = w_down[0]
    pooled_rows, pooled_upstream, pooled_gates = (
        lax.all_gather(tokens, "dp", axis=0, tiled=True),
        lax.all_gather(cotangent, "dp", axis=0, tiled=True),
        lax.all_gather(gate_values, "dp", axis=0, tiled=True),
    )
    lists_all, pooled_ids = (
        lax.all_gather(packing, "dp", axis=0, tiled=True),
        lax.all_gather(expert_ids, "dp", axis=0, tiled=True),
    )
    member_rows = []
    member_upstream = []
    member_positions = []
    for member in range(dp_size):
        low = member * row_count
        slot_lists = lists_all[low : low + row_count]
        position, occupied, slot_row, slot_gate = slot_table(
            pooled_ids[low : low + row_count],
            pooled_gates[low : low + row_count],
            expert_count,
            capacity,
        )
        send_rows, send_upstream = fill_slots(
            pick_rows(slot_lists, pooled_rows),
            pick_rows(slot_lists, pooled_upstream),
            occupied,
            slot_row,
            slot_gate,
        )
        member_rows.append(send_rows.reshape(expert_count, capacity * model_width))
        member_upstream.append(send_upstream.reshape(expert_count, capacity * model_width))
        member_positions.append(position)
    own_position = jnp.stack(member_positions)[lax.axis_index("dp")]
    send_rows = jnp.concatenate(member_rows, axis=1).reshape(
        expert_count * dp_size * capacity, model_width
    )
    send_upstream = jnp.concatenate(member_upstream, axis=1).reshape(
        expert_count * dp_size * capacity, model_width
    )
    recv_rows, recv_upstream = (
        lax.all_to_all(send_rows, "expert", split_axis=0, concat_axis=0, tiled=True),
        lax.all_to_all(send_upstream, "expert", split_axis=0, concat_axis=0, tiled=True),
    )
    weight_grads, partial_grad = expert_terms(recv_rows, recv_upstream, gate_mat, up_mat, down_mat)
    summed = lax.psum_scatter(
        partial_grad.reshape(expert_count, dp_size * capacity * model_width).astype(jnp.bfloat16),
        "dp",
        scatter_dimension=1,
        tiled=True,
    ).astype(jnp.float32)
    slot_grad = summed.reshape(expert_count * capacity, model_width).astype(jnp.bfloat16)
    returned = lax.all_to_all(slot_grad, "expert", split_axis=0, concat_axis=0, tiled=True)
    rebal_grad = jnp.sum(returned[own_position].astype(jnp.float32), axis=1).astype(jnp.bfloat16)
    pooled_grad = lax.all_gather(rebal_grad, "dp", axis=0, tiled=True)
    home_index = lax.axis_index("dp") * row_count + jnp.arange(row_count, dtype=jnp.int32)
    choose = (lists_all[None, :] == home_index[:, None]).astype(jnp.bfloat16)
    input_grad = jnp.dot(choose, pooled_grad, preferred_element_type=jnp.float32).astype(
        jnp.bfloat16
    )
    return (input_grad, weight_grads[0], weight_grads[1], weight_grads[2])


def swap(value):
    return lax.ppermute(value, "dp", [(0, 1), (1, 0)])


def shift_outer(value, count, inner, step):
    return lax.ppermute(
        value, "expert", [(place, (place + step * inner) % count) for place in range(count)]
    )


def swap_inner(value, count, partner):
    return lax.ppermute(value, "expert", [(place, place ^ partner) for place in range(count)])


VMEM = pl.BlockSpec(memory_space=pltpu.VMEM)
ANY = pl.BlockSpec(memory_space=pl.ANY)
NT = (((1,), (1,)), ((), ()))
TN = (((0,), (0,)), ((), ()))


def on_chip(body, outs, *args, scratch=(), spec=VMEM, limit=True):
    moved = sum(arg.size * arg.dtype.itemsize for arg in args)
    moved += sum(math.prod(shape) * jnp.dtype(dtype).itemsize for shape, dtype in outs)
    granted = {"vmem_limit_bytes": moved + (4 << 20)} if limit else {}
    return pl.pallas_call(
        body,
        out_shape=[jax.ShapeDtypeStruct(shape, dtype) for shape, dtype in outs],
        in_specs=[spec] * len(args),
        out_specs=[VMEM] * len(outs),
        scratch_shapes=list(scratch),
        compiler_params=pltpu.CompilerParams(**granted),
        cost_estimate=pl.CostEstimate(flops=0, bytes_accessed=moved, transcendentals=0),
    )(*args)


def read_kernel(
    ids_hbm, gates_hbm, packing_hbm, tokens_hbm, cotangent_hbm,
    table_ref, tokens_ref, cotangent_ref,
    ids_ref, gates_ref, packing_ref, ready,
):
    pairs = [
        (ids_hbm, ids_ref),
        (gates_hbm, gates_ref),
        (packing_hbm, packing_ref),
        (tokens_hbm, tokens_ref),
        (cotangent_hbm, cotangent_ref),
    ]
    copies = [
        pltpu.make_async_copy(source, target, ready.at[index])
        for index, (source, target) in enumerate(pairs)
    ]
    for copy in copies:
        copy.start()
    for copy in copies:
        copy.wait()
    slots = packing_ref.shape[1]
    count = table_ref.shape[0] - 16
    labels = lax.broadcasted_iota(jnp.int32, (count, slots), 0)
    total = jnp.zeros((count, slots), jnp.float32)
    for k in range(ids_ref.shape[0]):
        named = labels == ids_ref[k : k + 1, :]
        total = total + jnp.where(named, gates_ref[k : k + 1, :].astype(jnp.float32), 0.0)
    table_ref[:count, :] = total.astype(jnp.bfloat16)
    lists = jnp.broadcast_to(packing_ref[...], (16, slots)).astype(jnp.float32)
    table_ref[count:, :] = lists.astype(jnp.bfloat16)


def payload_kernel(table_ref, other_ref, cotangent_ref, payload_ref, here_ref):
    rows, width = cotangent_ref.shape
    count = table_ref.shape[0] - 16
    slots = table_ref.shape[1]
    homes = lax.broadcasted_iota(jnp.int32, (rows, slots), 0) + lax.axis_index("dp") * rows
    gates = jnp.zeros((rows, count), jnp.float32)
    for ref in (table_ref, other_ref):
        lists = ref[count:, :].astype(jnp.float32)[:1, :]
        matched = (lists == homes.astype(jnp.float32)).astype(jnp.float32).astype(jnp.bfloat16)
        gates = gates + lax.dot_general(
            matched, ref[:count, :], NT, preferred_element_type=jnp.float32
        )
    payload_ref[:, :width] = cotangent_ref[...]
    payload_ref[:, width:] = gates.astype(jnp.bfloat16)
    lanes = lax.broadcasted_iota(jnp.int32, here_ref.shape, 1)
    here_ref[...] = (lanes == lax.axis_index("expert")).astype(jnp.float32)


def weight_kernel(own_grads, other_grads, rows, other_rows, upstream, other_upstream, *outs):
    half = outs[0].shape[1]
    for index, out in enumerate(outs):
        own, other = (upstream, other_upstream) if index == 2 else (rows, other_rows)
        span = slice(index * half, (index + 1) * half)
        step = min(out.shape[-1], 1024)
        for left in range(0, out.shape[-1], step):
            columns = slice(left, left + step)
            total = lax.dot_general(
                own_grads[:, span], own[:, columns], TN, preferred_element_type=jnp.float32
            ) + lax.dot_general(
                other_grads[:, span], other[:, columns], TN, preferred_element_type=jnp.float32
            )
            out[0, :, columns] = total.astype(jnp.bfloat16)


def join_kernel(own_ref, other_ref, gate_up_ref, down_ref):
    half = own_ref.shape[0] // 3
    for index, ref in enumerate((own_ref, other_ref)):
        for kind in range(2):
            low = (2 * kind + index) * half
            gate_up_ref[low : low + half, :] = ref[kind * half : (kind + 1) * half, :]
        down_ref[index * half : (index + 1) * half, :] = ref[2 * half :, :]


def pair_kernel(left_ref, right_ref, other_left_ref, other_right_ref, sum_ref, other_sum_ref):
    for one, two, out in (
        (left_ref, right_ref, sum_ref),
        (other_left_ref, other_right_ref, other_sum_ref),
    ):
        total = one[...].astype(jnp.float32) + two[...].astype(jnp.float32)
        out[...] = total.astype(out.dtype)


def along_outer(value, count, inner):
    return [value] + [shift_outer(value, count, inner, step) for step in range(1, count // inner)]


def across_inner(column, count, inner):
    if inner < 4:
        return [column] + [swap_inner(column, count, partner) for partner in range(1, inner)]
    cut = column.shape[0] // 2
    first = swap_inner(column, count, 1)
    second = swap_inner(column, count, 2)
    far_top = swap_inner(first[:cut], count, 2)
    far_bottom = swap_inner(second[cut:], count, 1)
    return [column, first, second, far_top, far_bottom]


def return_inner(value, count):
    own, first, second, far = jnp.split(value, 4, axis=0)
    cut = own.shape[0] // 2
    top = swap_inner(far[:cut], count, 2)
    bottom = swap_inner(far[cut:], count, 1)
    first_bottom = swap_inner(first[cut:], count, 1)
    second_top = swap_inner(second[:cut], count, 2)
    sent_first, sent_second = on_chip(
        pair_kernel, [(top.shape, top.dtype)] * 2, first[:cut], top, second[cut:], bottom
    )
    first_top = swap_inner(sent_first, count, 1)
    second_bottom = swap_inner(sent_second, count, 2)
    total = own.astype(jnp.float32)
    for upper, lower in ((first_top, first_bottom), (second_top, second_bottom)):
        total = total + jnp.concatenate([upper, lower], axis=0).astype(jnp.float32)
    return total


def return_outer(value, count, inner):
    outer = count // inner
    blocks = value.reshape(outer, -1, value.shape[-1])
    rounded = blocks.astype(jnp.bfloat16)
    total = blocks[0]
    for step in range(1, outer):
        total = total + shift_outer(rounded[step], count, inner, -step).astype(jnp.float32)
    return total.astype(jnp.bfloat16)


def dense_local(tokens, cotangent, gate_values, expert_ids, packing, w_gate, w_up, w_down):
    model_width = tokens.shape[1]
    half = w_gate.shape[1]
    count = lax.axis_size("expert")
    inner = 4
    row_count = tokens.shape[0]
    low = jnp.bfloat16
    ids, gates, lists = expert_ids.T, gate_values.T, packing.reshape(1, row_count)
    token_blocks = along_outer(tokens, count, inner)
    table, own_tokens, own_cotangent = on_chip(
        read_kernel,
        [
            ((count + 16, row_count), low),
            (tokens.shape, low),
            (cotangent.shape, low),
        ],
        ids,
        gates,
        lists,
        tokens,
        cotangent,
        spec=ANY,
        limit=False,
        scratch=[
            pltpu.VMEM(ids.shape, ids.dtype),
            pltpu.VMEM(gates.shape, gates.dtype),
            pltpu.VMEM(lists.shape, lists.dtype),
            pltpu.SemaphoreType.DMA((5,)),
        ],
    )
    payload, here = on_chip(
        payload_kernel,
        [((row_count, model_width + count), low), ((8, count), jnp.float32)],
        table,
        swap(table),
        own_cotangent,
    )
    token_column = jnp.concatenate([own_tokens, *token_blocks[1:]], axis=0)
    early = shift_outer(payload, count, inner, 2)
    payload, token_column = lax.optimization_barrier((payload, token_column))
    upstream_blocks = [payload, shift_outer(payload, count, inner, 1), early]
    upstream_blocks.append(shift_outer(payload, count, inner, 3))
    upstream_column = jnp.concatenate(upstream_blocks, axis=0)
    token_columns = across_inner(token_column, count, inner)
    own_weights = jnp.concatenate([w_gate[0], w_up[0], w_down[0]], axis=0)
    sent_weights, token_columns[1] = lax.optimization_barrier((own_weights, token_columns[1]))
    other = swap(sent_weights)
    inputs = jnp.concatenate(token_columns, axis=0)
    other_inputs = swap(inputs)
    upstream = jnp.concatenate(across_inner(upstream_column, count, inner), axis=0)
    gate = jnp.sum(
        upstream[:, model_width:].astype(jnp.float32) * here[:1], axis=1, keepdims=True
    )
    upstream = upstream[:, :model_width]
    gate_up, down = on_chip(
        join_kernel,
        [((4 * half, model_width), low), ((2 * half, model_width), low)],
        own_weights,
        other,
    )
    pre = jnp.dot(inputs, gate_up.T, preferred_element_type=jnp.float32)
    gate_pre, up_pre = pre[:, : 2 * half], pre[:, 2 * half :]
    hidden_grad = gate * jnp.dot(upstream, down.T, preferred_element_type=jnp.float32)
    sigmoid_val = jax.nn.sigmoid(gate_pre)
    activated = gate_pre * sigmoid_val
    hidden = (gate * activated * up_pre).astype(jnp.bfloat16)
    silu_slope = sigmoid_val * (1.0 + gate_pre * (1.0 - sigmoid_val))
    gate_grad = (hidden_grad * up_pre * silu_slope).astype(jnp.bfloat16)
    up_grad = (hidden_grad * activated).astype(jnp.bfloat16)
    both_grad = jnp.concatenate([gate_grad, up_grad], axis=1)
    partial_grad = jnp.dot(both_grad, gate_up, preferred_element_type=jnp.float32)
    partial_grad = partial_grad.astype(jnp.bfloat16)
    partial_grad, other_inputs = lax.optimization_barrier((partial_grad, other_inputs))
    column_sum = return_inner(partial_grad, count)
    grads = (gate_grad, up_grad, hidden)
    own_grads = jnp.concatenate([grad[:, :half] for grad in grads], axis=1)
    sent_grads = jnp.concatenate([grad[:, half:] for grad in grads], axis=1)
    sent_grads, upstream, _ = lax.optimization_barrier((sent_grads, upstream, partial_grad))
    other_grads = swap(sent_grads)
    other_upstream = swap(upstream)
    column_sum, other_grads, other_upstream = lax.optimization_barrier(
        (column_sum, other_grads, other_upstream)
    )
    input_grad = return_outer(column_sum, count, inner)
    weight_grads = on_chip(
        weight_kernel,
        [((1, half, model_width), low)] * 3,
        own_grads,
        other_grads,
        inputs,
        other_inputs,
        upstream,
        other_upstream,
    )
    return (input_grad, *weight_grads)


def local(tokens, cotangent, gate_values, expert_ids, packing, w_gate, w_up, w_down):
    row_count, top = expert_ids.shape
    count = lax.axis_size("expert")
    expert_count = count * w_gate.shape[0]
    capacity = min(row_count, max(2, row_count * top // expert_count + 1))
    few = capacity * 4 <= row_count
    regular = lax.axis_size("dp") == 2 and count % 4 == 0 and w_gate.shape[0] == 1
    chosen = dense_local if regular and not few else routed_local
    return chosen(
        tokens, cotangent, gate_values, expert_ids, packing, w_gate, w_up, w_down
    )


def solution(mesh):
    in_specs = (
        P(("groups", "dp", "expert"), None),
        P(("groups", "dp", "expert"), None),
        P(("groups", "dp", "expert"), None),
        P(("groups", "dp", "expert"), None),
        P(("groups", "dp", "expert")),
        P("expert", "dp", None),
        P("expert", "dp", None),
        P("expert", "dp", None),
    )
    out_specs = (
        P(("groups", "dp", "expert"), None),
        P(("groups", "expert"), "dp", None),
        P(("groups", "expert"), "dp", None),
        P(("groups", "expert"), "dp", None),
    )
    return jax.shard_map(local, mesh=mesh, in_specs=in_specs, out_specs=out_specs, check_vma=False)
```

```python
import math

import jax
import jax.numpy as jnp
from jax import lax
from jax.experimental import pallas as pl
from jax.experimental.pallas import tpu as pltpu
from jax.sharding import PartitionSpec as P


def slot_table(route_ids, route_gates, expert_count, capacity):
    row_count, top_count = route_ids.shape
    flat_ids = route_ids.reshape(-1)
    labels = jnp.arange(expert_count, dtype=jnp.int32)
    onehot = (flat_ids[:, None] == labels[None, :]).astype(jnp.int32)
    earlier = jnp.cumsum(onehot, axis=0) - onehot
    rank_in = jnp.sum(earlier * onehot, axis=1)
    position = flat_ids * capacity + rank_in
    places = jnp.arange(expert_count * capacity, dtype=jnp.int32)
    matched = places[:, None] == position[None, :]
    owner_row = jnp.arange(row_count * top_count, dtype=jnp.int32) // top_count
    occupied = jnp.any(matched, axis=1)
    slot_row = jnp.sum(jnp.where(matched, owner_row[None, :], 0), axis=1)
    flat_gates = route_gates.reshape(-1).astype(jnp.float32)
    slot_gate = jnp.sum(jnp.where(matched, flat_gates[None, :], 0.0), axis=1)
    return (position.reshape(row_count, top_count), occupied, slot_row, slot_gate)


def pick_rows(slot_lists, pooled):
    sources = jnp.arange(pooled.shape[0], dtype=jnp.int32)
    choose = (slot_lists[:, None] == sources[None, :]).astype(jnp.bfloat16)
    return jnp.dot(choose, pooled, preferred_element_type=jnp.float32).astype(jnp.bfloat16)


def fill_slots(rebal_rows, rebal_upstream, occupied, slot_row, slot_gate):
    send_rows = jnp.where(occupied[:, None], rebal_rows[slot_row], jnp.zeros((), jnp.bfloat16))
    scaled = slot_gate[:, None] * rebal_upstream[slot_row].astype(jnp.float32)
    send_upstream = jnp.where(occupied[:, None], scaled, 0.0).astype(jnp.bfloat16)
    return (send_rows, send_upstream)


def expert_terms(inputs, upstream, gate_mat, up_mat, down_mat):
    gate_pre = jnp.dot(inputs, gate_mat.T, preferred_element_type=jnp.float32)
    up_pre = jnp.dot(inputs, up_mat.T, preferred_element_type=jnp.float32)
    sigmoid_val = jax.nn.sigmoid(gate_pre)
    activated = gate_pre * sigmoid_val
    hidden = (activated * up_pre).astype(jnp.bfloat16)
    hidden_grad = jnp.dot(upstream, down_mat.T, preferred_element_type=jnp.float32)
    silu_slope = sigmoid_val * (1.0 + gate_pre * (1.0 - sigmoid_val))
    gate_grad = (hidden_grad * up_pre * silu_slope).astype(jnp.bfloat16)
    up_grad = (hidden_grad * activated).astype(jnp.bfloat16)
    weight_grads = (
        jnp.dot(gate_grad.T, inputs, preferred_element_type=jnp.float32).astype(jnp.bfloat16)[None],
        jnp.dot(up_grad.T, inputs, preferred_element_type=jnp.float32).astype(jnp.bfloat16)[None],
        jnp.dot(hidden.T, upstream, preferred_element_type=jnp.float32).astype(jnp.bfloat16)[None],
    )
    partial_grad = jnp.dot(gate_grad, gate_mat, preferred_element_type=jnp.float32)
    partial_grad = partial_grad + jnp.dot(up_grad, up_mat, preferred_element_type=jnp.float32)
    return (weight_grads, partial_grad)


def routed_local(tokens, cotangent, gate_values, expert_ids, packing, w_gate, w_up, w_down):
    row_count, top_count = expert_ids.shape
    model_width = tokens.shape[1]
    dp_size = lax.axis_size("dp")
    expert_count = lax.axis_size("expert") * w_gate.shape[0]
    capacity = min(row_count, max(2, row_count * top_count // expert_count + 1))
    gate_mat = w_gate[0]
    up_mat = w_up[0]
    down_mat = w_down[0]
    pooled_rows, pooled_upstream, pooled_gates = (
        lax.all_gather(tokens, "dp", axis=0, tiled=True),
        lax.all_gather(cotangent, "dp", axis=0, tiled=True),
        lax.all_gather(gate_values, "dp", axis=0, tiled=True),
    )
    lists_all, pooled_ids = (
        lax.all_gather(packing, "dp", axis=0, tiled=True),
        lax.all_gather(expert_ids, "dp", axis=0, tiled=True),
    )
    member_rows = []
    member_upstream = []
    member_positions = []
    for member in range(dp_size):
        low = member * row_count
        slot_lists = lists_all[low : low + row_count]
        position, occupied, slot_row, slot_gate = slot_table(
            pooled_ids[low : low + row_count],
            pooled_gates[low : low + row_count],
            expert_count,
            capacity,
        )
        send_rows, send_upstream = fill_slots(
            pick_rows(slot_lists, pooled_rows),
            pick_rows(slot_lists, pooled_upstream),
            occupied,
            slot_row,
            slot_gate,
        )
        member_rows.append(send_rows.reshape(expert_count, capacity * model_width))
        member_upstream.append(send_upstream.reshape(expert_count, capacity * model_width))
        member_positions.append(position)
    own_position = jnp.stack(member_positions)[lax.axis_index("dp")]
    send_rows = jnp.concatenate(member_rows, axis=1).reshape(
        expert_count * dp_size * capacity, model_width
    )
    send_upstream = jnp.concatenate(member_upstream, axis=1).reshape(
        expert_count * dp_size * capacity, model_width
    )
    recv_rows, recv_upstream = (
        lax.all_to_all(send_rows, "expert", split_axis=0, concat_axis=0, tiled=True),
        lax.all_to_all(send_upstream, "expert", split_axis=0, concat_axis=0, tiled=True),
    )
    weight_grads, partial_grad = expert_terms(recv_rows, recv_upstream, gate_mat, up_mat, down_mat)
    summed = lax.psum_scatter(
        partial_grad.reshape(expert_count, dp_size * capacity * model_width).astype(jnp.bfloat16),
        "dp",
        scatter_dimension=1,
        tiled=True,
    ).astype(jnp.float32)
    slot_grad = summed.reshape(expert_count * capacity, model_width).astype(jnp.bfloat16)
    returned = lax.all_to_all(slot_grad, "expert", split_axis=0, concat_axis=0, tiled=True)
    rebal_grad = jnp.sum(returned[own_position].astype(jnp.float32), axis=1).astype(jnp.bfloat16)
    pooled_grad = lax.all_gather(rebal_grad, "dp", axis=0, tiled=True)
    home_index = lax.axis_index("dp") * row_count + jnp.arange(row_count, dtype=jnp.int32)
    choose = (lists_all[None, :] == home_index[:, None]).astype(jnp.bfloat16)
    input_grad = jnp.dot(choose, pooled_grad, preferred_element_type=jnp.float32).astype(
        jnp.bfloat16
    )
    return (input_grad, weight_grads[0], weight_grads[1], weight_grads[2])


def swap(value):
    return lax.ppermute(value, "dp", [(0, 1), (1, 0)])


def shift_outer(value, count, inner, step):
    return lax.ppermute(
        value, "expert", [(place, (place + step * inner) % count) for place in range(count)]
    )


def swap_inner(value, count, partner):
    return lax.ppermute(value, "expert", [(place, place ^ partner) for place in range(count)])


VMEM = pl.BlockSpec(memory_space=pltpu.VMEM)
ANY = pl.BlockSpec(memory_space=pl.ANY)
NT = (((1,), (1,)), ((), ()))
TN = (((0,), (0,)), ((), ()))


def on_chip(body, outs, *args, scratch=(), spec=VMEM, limit=True):
    moved = sum(arg.size * arg.dtype.itemsize for arg in args)
    moved += sum(math.prod(shape) * jnp.dtype(dtype).itemsize for shape, dtype in outs)
    granted = {"vmem_limit_bytes": moved + (4 << 20)} if limit else {}
    return pl.pallas_call(
        body,
        out_shape=[jax.ShapeDtypeStruct(shape, dtype) for shape, dtype in outs],
        in_specs=[spec] * len(args),
        out_specs=[VMEM] * len(outs),
        scratch_shapes=list(scratch),
        compiler_params=pltpu.CompilerParams(**granted),
        cost_estimate=pl.CostEstimate(flops=0, bytes_accessed=moved, transcendentals=0),
    )(*args)


def read_kernel(
    ids_hbm, gates_hbm, packing_hbm, tokens_hbm, cotangent_hbm,
    table_ref, tokens_ref, cotangent_ref,
    ids_ref, gates_ref, packing_ref, ready,
):
    pairs = [
        (ids_hbm, ids_ref),
        (gates_hbm, gates_ref),
        (packing_hbm, packing_ref),
        (tokens_hbm, tokens_ref),
        (cotangent_hbm, cotangent_ref),
    ]
    copies = [
        pltpu.make_async_copy(source, target, ready.at[index])
        for index, (source, target) in enumerate(pairs)
    ]
    for copy in copies:
        copy.start()
    for copy in copies:
        copy.wait()
    slots = packing_ref.shape[1]
    count = table_ref.shape[0] - 16
    labels = lax.broadcasted_iota(jnp.int32, (count, slots), 0)
    total = jnp.zeros((count, slots), jnp.float32)
    for k in range(ids_ref.shape[0]):
        named = labels == ids_ref[k : k + 1, :]
        total = total + jnp.where(named, gates_ref[k : k + 1, :].astype(jnp.float32), 0.0)
    table_ref[:count, :] = total.astype(jnp.bfloat16)
    lists = jnp.broadcast_to(packing_ref[...], (16, slots)).astype(jnp.float32)
    table_ref[count:, :] = lists.astype(jnp.bfloat16)


def payload_kernel(table_ref, other_ref, cotangent_ref, payload_ref, here_ref):
    rows, width = cotangent_ref.shape
    count = table_ref.shape[0] - 16
    slots = table_ref.shape[1]
    homes = lax.broadcasted_iota(jnp.int32, (rows, slots), 0) + lax.axis_index("dp") * rows
    gates = jnp.zeros((rows, count), jnp.float32)
    for ref in (table_ref, other_ref):
        lists = ref[count:, :].astype(jnp.float32)[:1, :]
        matched = (lists == homes.astype(jnp.float32)).astype(jnp.float32).astype(jnp.bfloat16)
        gates = gates + lax.dot_general(
            matched, ref[:count, :], NT, preferred_element_type=jnp.float32
        )
    payload_ref[:, :width] = cotangent_ref[...]
    payload_ref[:, width:] = gates.astype(jnp.bfloat16)
    lanes = lax.broadcasted_iota(jnp.int32, here_ref.shape, 1)
    here_ref[...] = (lanes == lax.axis_index("expert")).astype(jnp.float32)


def weight_kernel(own_grads, other_grads, rows, other_rows, upstream, other_upstream, *outs):
    half = outs[0].shape[1]
    for index, out in enumerate(outs):
        own, other = (upstream, other_upstream) if index == 2 else (rows, other_rows)
        span = slice(index * half, (index + 1) * half)
        step = min(out.shape[-1], 1024)
        for left in range(0, out.shape[-1], step):
            columns = slice(left, left + step)
            total = lax.dot_general(
                own_grads[:, span], own[:, columns], TN, preferred_element_type=jnp.float32
            ) + lax.dot_general(
                other_grads[:, span], other[:, columns], TN, preferred_element_type=jnp.float32
            )
            out[0, :, columns] = total.astype(jnp.bfloat16)


def join_kernel(own_ref, other_ref, gate_up_ref, down_ref):
    half = own_ref.shape[0] // 3
    for index, ref in enumerate((own_ref, other_ref)):
        for kind in range(2):
            low = (2 * kind + index) * half
            gate_up_ref[low : low + half, :] = ref[kind * half : (kind + 1) * half, :]
        down_ref[index * half : (index + 1) * half, :] = ref[2 * half :, :]


def pair_kernel(left_ref, right_ref, other_left_ref, other_right_ref, sum_ref, other_sum_ref):
    for one, two, out in (
        (left_ref, right_ref, sum_ref),
        (other_left_ref, other_right_ref, other_sum_ref),
    ):
        total = one[...].astype(jnp.float32) + two[...].astype(jnp.float32)
        out[...] = total.astype(out.dtype)


def along_outer(value, count, inner):
    return [value] + [shift_outer(value, count, inner, step) for step in range(1, count // inner)]


def across_inner(column, count, inner):
    cut = column.shape[0] // 2
    first = swap_inner(column, count, 1)
    second = swap_inner(column, count, 2)
    far_top = swap_inner(first[:cut], count, 2)
    far_bottom = swap_inner(second[cut:], count, 1)
    return [column, first, second, far_top, far_bottom]


def across_halves(column, count):
    cut = column.shape[0] // 2
    top, bottom = column[:cut], column[cut:]
    first_top = swap_inner(top, count, 1)
    second_bottom = swap_inner(bottom, count, 2)
    first_bottom = swap_inner(bottom, count, 1)
    second_top = swap_inner(top, count, 2)
    far_top = swap_inner(first_top, count, 2)
    far_bottom = swap_inner(second_bottom, count, 1)
    return [column, first_top, first_bottom, second_top, second_bottom, far_top, far_bottom]


def return_inner(value, count):
    own, first, second, far = jnp.split(value, 4, axis=0)
    cut = own.shape[0] // 2
    top = swap_inner(far[:cut], count, 2)
    bottom = swap_inner(far[cut:], count, 1)
    first_bottom = swap_inner(first[cut:], count, 1)
    second_top = swap_inner(second[:cut], count, 2)
    sent_first, sent_second = on_chip(
        pair_kernel, [(top.shape, top.dtype)] * 2, first[:cut], top, second[cut:], bottom
    )
    first_top = swap_inner(sent_first, count, 1)
    second_bottom = swap_inner(sent_second, count, 2)
    total = own.astype(jnp.float32)
    for upper, lower in ((first_top, first_bottom), (second_top, second_bottom)):
        total = total + jnp.concatenate([upper, lower], axis=0).astype(jnp.float32)
    return total


def return_outer(value, count, inner):
    outer = count // inner
    blocks = value.reshape(outer, -1, value.shape[-1])
    rounded = blocks.astype(jnp.bfloat16)
    total = blocks[0]
    for step in range(1, outer):
        total = total + shift_outer(rounded[step], count, inner, -step).astype(jnp.float32)
    return total.astype(jnp.bfloat16)


def dense_local(tokens, cotangent, gate_values, expert_ids, packing, w_gate, w_up, w_down):
    model_width = tokens.shape[1]
    half = w_gate.shape[1]
    count = lax.axis_size("expert")
    inner = 4
    row_count = tokens.shape[0]
    low = jnp.bfloat16
    ids, gates, lists = expert_ids.T, gate_values.T, packing.reshape(1, row_count)
    token_blocks = along_outer(tokens, count, inner)
    table, own_tokens, own_cotangent = on_chip(
        read_kernel,
        [
            ((count + 16, row_count), low),
            (tokens.shape, low),
            (cotangent.shape, low),
        ],
        ids,
        gates,
        lists,
        tokens,
        cotangent,
        spec=ANY,
        limit=False,
        scratch=[
            pltpu.VMEM(ids.shape, ids.dtype),
            pltpu.VMEM(gates.shape, gates.dtype),
            pltpu.VMEM(lists.shape, lists.dtype),
            pltpu.SemaphoreType.DMA((5,)),
        ],
    )
    payload, here = on_chip(
        payload_kernel,
        [((row_count, model_width + count), low), ((8, count), jnp.float32)],
        table,
        swap(table),
        own_cotangent,
    )
    token_column = jnp.concatenate([own_tokens, *token_blocks[1:]], axis=0)
    early = shift_outer(payload, count, inner, 2)
    payload, token_column = lax.optimization_barrier((payload, token_column))
    upstream_blocks = [payload, shift_outer(payload, count, inner, 1), early]
    upstream_blocks.append(shift_outer(payload, count, inner, 3))
    upstream_column = jnp.concatenate(upstream_blocks, axis=0)
    token_columns = across_inner(token_column, count, inner)
    own_weights = jnp.concatenate([w_gate[0], w_up[0], w_down[0]], axis=0)
    sent_weights, token_columns[1] = lax.optimization_barrier((own_weights, token_columns[1]))
    other = swap(sent_weights)
    inputs = jnp.concatenate(token_columns, axis=0)
    other_inputs = swap(inputs)
    upstream = jnp.concatenate(across_halves(upstream_column, count), axis=0)
    gate = jnp.sum(
        upstream[:, model_width:].astype(jnp.float32) * here[:1], axis=1, keepdims=True
    )
    upstream = upstream[:, :model_width]
    gate_up, down = on_chip(
        join_kernel,
        [((4 * half, model_width), low), ((2 * half, model_width), low)],
        own_weights,
        other,
    )
    pre = jnp.dot(inputs, gate_up.T, preferred_element_type=jnp.float32)
    gate_pre, up_pre = pre[:, : 2 * half], pre[:, 2 * half :]
    hidden_grad = gate * jnp.dot(upstream, down.T, preferred_element_type=jnp.float32)
    sigmoid_val = jax.nn.sigmoid(gate_pre)
    activated = gate_pre * sigmoid_val
    hidden = (gate * activated * up_pre).astype(jnp.bfloat16)
    silu_slope = sigmoid_val * (1.0 + gate_pre * (1.0 - sigmoid_val))
    gate_grad = (hidden_grad * up_pre * silu_slope).astype(jnp.bfloat16)
    up_grad = (hidden_grad * activated).astype(jnp.bfloat16)
    both_grad = jnp.concatenate([gate_grad, up_grad], axis=1)
    partial_grad = jnp.dot(both_grad, gate_up, preferred_element_type=jnp.float32)
    partial_grad = partial_grad.astype(jnp.bfloat16)
    partial_grad, other_inputs = lax.optimization_barrier((partial_grad, other_inputs))
    column_sum = return_inner(partial_grad, count)
    grads = (gate_grad, up_grad, hidden)
    own_grads = jnp.concatenate([grad[:, :half] for grad in grads], axis=1)
    sent_grads = jnp.concatenate([grad[:, half:] for grad in grads], axis=1)
    sent_grads, upstream, _ = lax.optimization_barrier((sent_grads, upstream, partial_grad))
    other_grads = swap(sent_grads)
    other_upstream = swap(upstream)
    column_sum, other_grads, other_upstream = lax.optimization_barrier(
        (column_sum, other_grads, other_upstream)
    )
    input_grad = return_outer(column_sum, count, inner)
    weight_grads = on_chip(
        weight_kernel,
        [((1, half, model_width), low)] * 3,
        own_grads,
        other_grads,
        inputs,
        other_inputs,
        upstream,
        other_upstream,
    )
    return (input_grad, *weight_grads)


def local(tokens, cotangent, gate_values, expert_ids, packing, w_gate, w_up, w_down):
    row_count, top = expert_ids.shape
    count = lax.axis_size("expert")
    expert_count = count * w_gate.shape[0]
    capacity = min(row_count, max(2, row_count * top // expert_count + 1))
    few = capacity * 4 <= row_count
    regular = lax.axis_size("dp") == 2 and count % 4 == 0 and w_gate.shape[0] == 1
    chosen = dense_local if regular and not few else routed_local
    return chosen(
        tokens, cotangent, gate_values, expert_ids, packing, w_gate, w_up, w_down
    )


def solution(mesh):
    in_specs = (
        P(("groups", "dp", "expert"), None),
        P(("groups", "dp", "expert"), None),
        P(("groups", "dp", "expert"), None),
        P(("groups", "dp", "expert"), None),
        P(("groups", "dp", "expert")),
        P("expert", "dp", None),
        P("expert", "dp", None),
        P("expert", "dp", None),
    )
    out_specs = (
        P(("groups", "dp", "expert"), None),
        P(("groups", "expert"), "dp", None),
        P(("groups", "expert"), "dp", None),
        P(("groups", "expert"), "dp", None),
    )
    return jax.shard_map(local, mesh=mesh, in_specs=in_specs, out_specs=out_specs, check_vma=False)
```

```python
import math

import jax
import jax.numpy as jnp
from jax import lax
from jax.experimental import pallas as pl
from jax.experimental.pallas import tpu as pltpu
from jax.sharding import PartitionSpec as P


def slot_table(route_ids, route_gates, expert_count, capacity):
    row_count, top_count = route_ids.shape
    flat_ids = route_ids.reshape(-1)
    labels = jnp.arange(expert_count, dtype=jnp.int32)
    onehot = (flat_ids[:, None] == labels[None, :]).astype(jnp.int32)
    earlier = jnp.cumsum(onehot, axis=0) - onehot
    rank_in = jnp.sum(earlier * onehot, axis=1)
    position = flat_ids * capacity + rank_in
    places = jnp.arange(expert_count * capacity, dtype=jnp.int32)
    matched = places[:, None] == position[None, :]
    owner_row = jnp.arange(row_count * top_count, dtype=jnp.int32) // top_count
    occupied = jnp.any(matched, axis=1)
    slot_row = jnp.sum(jnp.where(matched, owner_row[None, :], 0), axis=1)
    flat_gates = route_gates.reshape(-1).astype(jnp.float32)
    slot_gate = jnp.sum(jnp.where(matched, flat_gates[None, :], 0.0), axis=1)
    return (position.reshape(row_count, top_count), occupied, slot_row, slot_gate)


def pick_rows(slot_lists, pooled):
    sources = jnp.arange(pooled.shape[0], dtype=jnp.int32)
    choose = (slot_lists[:, None] == sources[None, :]).astype(jnp.bfloat16)
    return jnp.dot(choose, pooled, preferred_element_type=jnp.float32).astype(jnp.bfloat16)


def fill_slots(rebal_rows, rebal_upstream, occupied, slot_row, slot_gate):
    send_rows = jnp.where(occupied[:, None], rebal_rows[slot_row], jnp.zeros((), jnp.bfloat16))
    scaled = slot_gate[:, None] * rebal_upstream[slot_row].astype(jnp.float32)
    send_upstream = jnp.where(occupied[:, None], scaled, 0.0).astype(jnp.bfloat16)
    return (send_rows, send_upstream)


def expert_terms(inputs, upstream, gate_mat, up_mat, down_mat):
    gate_pre = jnp.dot(inputs, gate_mat.T, preferred_element_type=jnp.float32)
    up_pre = jnp.dot(inputs, up_mat.T, preferred_element_type=jnp.float32)
    sigmoid_val = jax.nn.sigmoid(gate_pre)
    activated = gate_pre * sigmoid_val
    hidden = (activated * up_pre).astype(jnp.bfloat16)
    hidden_grad = jnp.dot(upstream, down_mat.T, preferred_element_type=jnp.float32)
    silu_slope = sigmoid_val * (1.0 + gate_pre * (1.0 - sigmoid_val))
    gate_grad = (hidden_grad * up_pre * silu_slope).astype(jnp.bfloat16)
    up_grad = (hidden_grad * activated).astype(jnp.bfloat16)
    weight_grads = (
        jnp.dot(gate_grad.T, inputs, preferred_element_type=jnp.float32).astype(jnp.bfloat16)[None],
        jnp.dot(up_grad.T, inputs, preferred_element_type=jnp.float32).astype(jnp.bfloat16)[None],
        jnp.dot(hidden.T, upstream, preferred_element_type=jnp.float32).astype(jnp.bfloat16)[None],
    )
    partial_grad = jnp.dot(gate_grad, gate_mat, preferred_element_type=jnp.float32)
    partial_grad = partial_grad + jnp.dot(up_grad, up_mat, preferred_element_type=jnp.float32)
    return (weight_grads, partial_grad)


def routed_local(tokens, cotangent, gate_values, expert_ids, packing, w_gate, w_up, w_down):
    row_count, top_count = expert_ids.shape
    model_width = tokens.shape[1]
    dp_size = lax.axis_size("dp")
    expert_count = lax.axis_size("expert") * w_gate.shape[0]
    capacity = min(row_count, max(2, row_count * top_count // expert_count + 1))
    gate_mat = w_gate[0]
    up_mat = w_up[0]
    down_mat = w_down[0]
    pooled_rows, pooled_upstream, pooled_gates = (
        lax.all_gather(tokens, "dp", axis=0, tiled=True),
        lax.all_gather(cotangent, "dp", axis=0, tiled=True),
        lax.all_gather(gate_values, "dp", axis=0, tiled=True),
    )
    lists_all, pooled_ids = (
        lax.all_gather(packing, "dp", axis=0, tiled=True),
        lax.all_gather(expert_ids, "dp", axis=0, tiled=True),
    )
    member_rows = []
    member_upstream = []
    member_positions = []
    for member in range(dp_size):
        low = member * row_count
        slot_lists = lists_all[low : low + row_count]
        position, occupied, slot_row, slot_gate = slot_table(
            pooled_ids[low : low + row_count],
            pooled_gates[low : low + row_count],
            expert_count,
            capacity,
        )
        send_rows, send_upstream = fill_slots(
            pick_rows(slot_lists, pooled_rows),
            pick_rows(slot_lists, pooled_upstream),
            occupied,
            slot_row,
            slot_gate,
        )
        member_rows.append(send_rows.reshape(expert_count, capacity * model_width))
        member_upstream.append(send_upstream.reshape(expert_count, capacity * model_width))
        member_positions.append(position)
    own_position = jnp.stack(member_positions)[lax.axis_index("dp")]
    send_rows = jnp.concatenate(member_rows, axis=1).reshape(
        expert_count * dp_size * capacity, model_width
    )
    send_upstream = jnp.concatenate(member_upstream, axis=1).reshape(
        expert_count * dp_size * capacity, model_width
    )
    recv_rows, recv_upstream = (
        lax.all_to_all(send_rows, "expert", split_axis=0, concat_axis=0, tiled=True),
        lax.all_to_all(send_upstream, "expert", split_axis=0, concat_axis=0, tiled=True),
    )
    weight_grads, partial_grad = expert_terms(recv_rows, recv_upstream, gate_mat, up_mat, down_mat)
    summed = lax.psum_scatter(
        partial_grad.reshape(expert_count, dp_size * capacity * model_width).astype(jnp.bfloat16),
        "dp",
        scatter_dimension=1,
        tiled=True,
    ).astype(jnp.float32)
    slot_grad = summed.reshape(expert_count * capacity, model_width).astype(jnp.bfloat16)
    returned = lax.all_to_all(slot_grad, "expert", split_axis=0, concat_axis=0, tiled=True)
    rebal_grad = jnp.sum(returned[own_position].astype(jnp.float32), axis=1).astype(jnp.bfloat16)
    pooled_grad = lax.all_gather(rebal_grad, "dp", axis=0, tiled=True)
    home_index = lax.axis_index("dp") * row_count + jnp.arange(row_count, dtype=jnp.int32)
    choose = (lists_all[None, :] == home_index[:, None]).astype(jnp.bfloat16)
    input_grad = jnp.dot(choose, pooled_grad, preferred_element_type=jnp.float32).astype(
        jnp.bfloat16
    )
    return (input_grad, weight_grads[0], weight_grads[1], weight_grads[2])


def swap(value):
    return lax.ppermute(value, "dp", [(0, 1), (1, 0)])


def shift_outer(value, count, inner, step):
    return lax.ppermute(
        value, "expert", [(place, (place + step * inner) % count) for place in range(count)]
    )


def swap_inner(value, count, partner):
    return lax.ppermute(value, "expert", [(place, place ^ partner) for place in range(count)])


VMEM = pl.BlockSpec(memory_space=pltpu.VMEM)
ANY = pl.BlockSpec(memory_space=pl.ANY)
NT = (((1,), (1,)), ((), ()))
TN = (((0,), (0,)), ((), ()))


def on_chip(body, outs, *args, scratch=(), spec=VMEM, limit=True):
    moved = sum(arg.size * arg.dtype.itemsize for arg in args)
    moved += sum(math.prod(shape) * jnp.dtype(dtype).itemsize for shape, dtype in outs)
    granted = {"vmem_limit_bytes": moved + (4 << 20)} if limit else {}
    return pl.pallas_call(
        body,
        out_shape=[jax.ShapeDtypeStruct(shape, dtype) for shape, dtype in outs],
        in_specs=[spec] * len(args),
        out_specs=[VMEM] * len(outs),
        scratch_shapes=list(scratch),
        compiler_params=pltpu.CompilerParams(**granted),
        cost_estimate=pl.CostEstimate(flops=0, bytes_accessed=moved, transcendentals=0),
    )(*args)


def read_kernel(
    ids_hbm, gates_hbm, packing_hbm, tokens_hbm, cotangent_hbm,
    table_ref, tokens_ref, cotangent_ref,
    ids_ref, gates_ref, packing_ref, ready,
):
    pairs = [
        (ids_hbm, ids_ref),
        (gates_hbm, gates_ref),
        (packing_hbm, packing_ref),
        (tokens_hbm, tokens_ref),
        (cotangent_hbm, cotangent_ref),
    ]
    copies = [
        pltpu.make_async_copy(source, target, ready.at[index])
        for index, (source, target) in enumerate(pairs)
    ]
    for copy in copies:
        copy.start()
    for copy in copies:
        copy.wait()
    slots = packing_ref.shape[1]
    count = table_ref.shape[0] - 16
    labels = lax.broadcasted_iota(jnp.int32, (count, slots), 0)
    total = jnp.zeros((count, slots), jnp.float32)
    for k in range(ids_ref.shape[0]):
        named = labels == ids_ref[k : k + 1, :]
        total = total + jnp.where(named, gates_ref[k : k + 1, :].astype(jnp.float32), 0.0)
    table_ref[:count, :] = total.astype(jnp.bfloat16)
    lists = jnp.broadcast_to(packing_ref[...], (16, slots)).astype(jnp.float32)
    table_ref[count:, :] = lists.astype(jnp.bfloat16)


def payload_kernel(table_ref, other_ref, cotangent_ref, payload_ref, here_ref):
    rows, width = cotangent_ref.shape
    count = table_ref.shape[0] - 16
    slots = table_ref.shape[1]
    homes = lax.broadcasted_iota(jnp.int32, (rows, slots), 0) + lax.axis_index("dp") * rows
    gates = jnp.zeros((rows, count), jnp.float32)
    for ref in (table_ref, other_ref):
        lists = ref[count:, :].astype(jnp.float32)[:1, :]
        matched = (lists == homes.astype(jnp.float32)).astype(jnp.float32).astype(jnp.bfloat16)
        gates = gates + lax.dot_general(
            matched, ref[:count, :], NT, preferred_element_type=jnp.float32
        )
    payload_ref[:, :width] = cotangent_ref[...]
    payload_ref[:, width:] = gates.astype(jnp.bfloat16)
    lanes = lax.broadcasted_iota(jnp.int32, here_ref.shape, 1)
    here_ref[...] = (lanes == lax.axis_index("expert")).astype(jnp.float32)


def weight_kernel(own_grads, other_grads, rows, other_rows, upstream, other_upstream, *outs):
    half = outs[0].shape[1]
    for index, out in enumerate(outs):
        own, other = (upstream, other_upstream) if index == 2 else (rows, other_rows)
        span = slice(index * half, (index + 1) * half)
        step = min(out.shape[-1], 1024)
        for left in range(0, out.shape[-1], step):
            columns = slice(left, left + step)
            total = lax.dot_general(
                own_grads[:, span], own[:, columns], TN, preferred_element_type=jnp.float32
            ) + lax.dot_general(
                other_grads[:, span], other[:, columns], TN, preferred_element_type=jnp.float32
            )
            out[0, :, columns] = total.astype(jnp.bfloat16)


def join_kernel(own_ref, other_ref, gate_up_ref, down_ref):
    half = own_ref.shape[0] // 3
    for index, ref in enumerate((own_ref, other_ref)):
        for kind in range(2):
            low = (2 * kind + index) * half
            gate_up_ref[low : low + half, :] = ref[kind * half : (kind + 1) * half, :]
        down_ref[index * half : (index + 1) * half, :] = ref[2 * half :, :]


def pair_kernel(left_ref, right_ref, other_left_ref, other_right_ref, sum_ref, other_sum_ref):
    for one, two, out in (
        (left_ref, right_ref, sum_ref),
        (other_left_ref, other_right_ref, other_sum_ref),
    ):
        total = one[...].astype(jnp.float32) + two[...].astype(jnp.float32)
        out[...] = total.astype(out.dtype)


def along_outer(value, count, inner):
    return [value] + [shift_outer(value, count, inner, step) for step in range(1, count // inner)]


def across_inner(column, count, inner):
    if inner < 4:
        return [column] + [swap_inner(column, count, partner) for partner in range(1, inner)]
    cut = column.shape[0] // 2
    first = swap_inner(column, count, 1)
    second = swap_inner(column, count, 2)
    far_top = swap_inner(first[:cut], count, 2)
    far_bottom = swap_inner(second[cut:], count, 1)
    return [column, first, second, far_top, far_bottom]


def return_inner(near, far, count):
    own, first, second = jnp.split(near, 3, axis=0)
    cut = own.shape[0] // 2
    top = swap_inner(far[:cut], count, 2)
    bottom = swap_inner(far[cut:], count, 1)
    first_bottom = swap_inner(first[cut:], count, 1)
    second_top = swap_inner(second[:cut], count, 2)
    sent_first, sent_second = on_chip(
        pair_kernel, [(top.shape, top.dtype)] * 2, first[:cut], top, second[cut:], bottom
    )
    first_top = swap_inner(sent_first, count, 1)
    second_bottom = swap_inner(sent_second, count, 2)
    total = own.astype(jnp.float32)
    for upper, lower in ((first_top, first_bottom), (second_top, second_bottom)):
        total = total + jnp.concatenate([upper, lower], axis=0).astype(jnp.float32)
    return total


def return_outer(value, count, inner):
    outer = count // inner
    blocks = value.reshape(outer, -1, value.shape[-1])
    rounded = blocks.astype(jnp.bfloat16)
    total = blocks[0]
    for step in range(1, outer):
        total = total + shift_outer(rounded[step], count, inner, -step).astype(jnp.float32)
    return total.astype(jnp.bfloat16)


def dense_local(tokens, cotangent, gate_values, expert_ids, packing, w_gate, w_up, w_down):
    model_width = tokens.shape[1]
    half = w_gate.shape[1]
    count = lax.axis_size("expert")
    inner = 4
    row_count = tokens.shape[0]
    low = jnp.bfloat16
    ids, gates, lists = expert_ids.T, gate_values.T, packing.reshape(1, row_count)
    token_blocks = along_outer(tokens, count, inner)
    table, own_tokens, own_cotangent = on_chip(
        read_kernel,
        [
            ((count + 16, row_count), low),
            (tokens.shape, low),
            (cotangent.shape, low),
        ],
        ids,
        gates,
        lists,
        tokens,
        cotangent,
        spec=ANY,
        limit=False,
        scratch=[
            pltpu.VMEM(ids.shape, ids.dtype),
            pltpu.VMEM(gates.shape, gates.dtype),
            pltpu.VMEM(lists.shape, lists.dtype),
            pltpu.SemaphoreType.DMA((5,)),
        ],
    )
    payload, here = on_chip(
        payload_kernel,
        [((row_count, model_width + count), low), ((8, count), jnp.float32)],
        table,
        swap(table),
        own_cotangent,
    )
    token_column = jnp.concatenate([own_tokens, *token_blocks[1:]], axis=0)
    early = shift_outer(payload, count, inner, 2)
    payload, token_column = lax.optimization_barrier((payload, token_column))
    upstream_blocks = [payload, shift_outer(payload, count, inner, 1), early]
    upstream_blocks.append(shift_outer(payload, count, inner, 3))
    upstream_column = jnp.concatenate(upstream_blocks, axis=0)
    token_columns = across_inner(token_column, count, inner)
    own_weights = jnp.concatenate([w_gate[0], w_up[0], w_down[0]], axis=0)
    sent_weights, token_columns[1] = lax.optimization_barrier((own_weights, token_columns[1]))
    other = swap(sent_weights)
    inputs = jnp.concatenate(token_columns, axis=0)
    other_inputs = swap(inputs)
    upstream = jnp.concatenate(across_inner(upstream_column, count, inner), axis=0)
    gate = jnp.sum(
        upstream[:, model_width:].astype(jnp.float32) * here[:1], axis=1, keepdims=True
    )
    upstream = upstream[:, :model_width]
    gate_up, down = on_chip(
        join_kernel,
        [((4 * half, model_width), low), ((2 * half, model_width), low)],
        own_weights,
        other,
    )
    pre = jnp.dot(inputs, gate_up.T, preferred_element_type=jnp.float32)
    gate_pre, up_pre = pre[:, : 2 * half], pre[:, 2 * half :]
    hidden_grad = gate * jnp.dot(upstream, down.T, preferred_element_type=jnp.float32)
    sigmoid_val = jax.nn.sigmoid(gate_pre)
    activated = gate_pre * sigmoid_val
    hidden = (gate * activated * up_pre).astype(jnp.bfloat16)
    silu_slope = sigmoid_val * (1.0 + gate_pre * (1.0 - sigmoid_val))
    gate_grad = (hidden_grad * up_pre * silu_slope).astype(jnp.bfloat16)
    up_grad = (hidden_grad * activated).astype(jnp.bfloat16)
    both_grad = jnp.concatenate([gate_grad, up_grad], axis=1)
    cut = both_grad.shape[0] // inner * (inner - 1)
    far = jnp.dot(both_grad[cut:], gate_up, preferred_element_type=jnp.float32)
    far = far.astype(jnp.bfloat16)
    near_grad, far = lax.optimization_barrier((both_grad[:cut], far))
    near = jnp.dot(near_grad, gate_up, preferred_element_type=jnp.float32)
    near = near.astype(jnp.bfloat16)
    far, other_inputs = lax.optimization_barrier((far, other_inputs))
    column_sum = return_inner(near, far, count)
    grads = (gate_grad, up_grad, hidden)
    own_grads = jnp.concatenate([grad[:, :half] for grad in grads], axis=1)
    sent_grads = jnp.concatenate([grad[:, half:] for grad in grads], axis=1)
    sent_grads, upstream, _ = lax.optimization_barrier((sent_grads, upstream, near))
    other_grads = swap(sent_grads)
    other_upstream = swap(upstream)
    column_sum, other_grads, other_upstream = lax.optimization_barrier(
        (column_sum, other_grads, other_upstream)
    )
    input_grad = return_outer(column_sum, count, inner)
    weight_grads = on_chip(
        weight_kernel,
        [((1, half, model_width), low)] * 3,
        own_grads,
        other_grads,
        inputs,
        other_inputs,
        upstream,
        other_upstream,
    )
    return (input_grad, *weight_grads)


def local(tokens, cotangent, gate_values, expert_ids, packing, w_gate, w_up, w_down):
    row_count, top = expert_ids.shape
    count = lax.axis_size("expert")
    expert_count = count * w_gate.shape[0]
    capacity = min(row_count, max(2, row_count * top // expert_count + 1))
    few = capacity * 4 <= row_count
    regular = lax.axis_size("dp") == 2 and count % 4 == 0 and w_gate.shape[0] == 1
    chosen = dense_local if regular and not few else routed_local
    return chosen(
        tokens, cotangent, gate_values, expert_ids, packing, w_gate, w_up, w_down
    )


def solution(mesh):
    in_specs = (
        P(("groups", "dp", "expert"), None),
        P(("groups", "dp", "expert"), None),
        P(("groups", "dp", "expert"), None),
        P(("groups", "dp", "expert"), None),
        P(("groups", "dp", "expert")),
        P("expert", "dp", None),
        P("expert", "dp", None),
        P("expert", "dp", None),
    )
    out_specs = (
        P(("groups", "dp", "expert"), None),
        P(("groups", "expert"), "dp", None),
        P(("groups", "expert"), "dp", None),
        P(("groups", "expert"), "dp", None),
    )
    return jax.shard_map(local, mesh=mesh, in_specs=in_specs, out_specs=out_specs, check_vma=False)
```

```python
import math

import jax
import jax.numpy as jnp
from jax import lax
from jax.experimental import pallas as pl
from jax.experimental.pallas import tpu as pltpu
from jax.sharding import PartitionSpec as P


def slot_table(route_ids, route_gates, expert_count, capacity):
    row_count, top_count = route_ids.shape
    flat_ids = route_ids.reshape(-1)
    labels = jnp.arange(expert_count, dtype=jnp.int32)
    onehot = (flat_ids[:, None] == labels[None, :]).astype(jnp.int32)
    earlier = jnp.cumsum(onehot, axis=0) - onehot
    rank_in = jnp.sum(earlier * onehot, axis=1)
    position = flat_ids * capacity + rank_in
    places = jnp.arange(expert_count * capacity, dtype=jnp.int32)
    matched = places[:, None] == position[None, :]
    owner_row = jnp.arange(row_count * top_count, dtype=jnp.int32) // top_count
    occupied = jnp.any(matched, axis=1)
    slot_row = jnp.sum(jnp.where(matched, owner_row[None, :], 0), axis=1)
    flat_gates = route_gates.reshape(-1).astype(jnp.float32)
    slot_gate = jnp.sum(jnp.where(matched, flat_gates[None, :], 0.0), axis=1)
    return (position.reshape(row_count, top_count), occupied, slot_row, slot_gate)


def pick_rows(slot_lists, pooled):
    sources = jnp.arange(pooled.shape[0], dtype=jnp.int32)
    choose = (slot_lists[:, None] == sources[None, :]).astype(jnp.bfloat16)
    return jnp.dot(choose, pooled, preferred_element_type=jnp.float32).astype(jnp.bfloat16)


def fill_slots(rebal_rows, rebal_upstream, occupied, slot_row, slot_gate):
    send_rows = jnp.where(occupied[:, None], rebal_rows[slot_row], jnp.zeros((), jnp.bfloat16))
    scaled = slot_gate[:, None] * rebal_upstream[slot_row].astype(jnp.float32)
    send_upstream = jnp.where(occupied[:, None], scaled, 0.0).astype(jnp.bfloat16)
    return (send_rows, send_upstream)


def expert_terms(inputs, upstream, gate_mat, up_mat, down_mat):
    gate_pre = jnp.dot(inputs, gate_mat.T, preferred_element_type=jnp.float32)
    up_pre = jnp.dot(inputs, up_mat.T, preferred_element_type=jnp.float32)
    sigmoid_val = jax.nn.sigmoid(gate_pre)
    activated = gate_pre * sigmoid_val
    hidden = (activated * up_pre).astype(jnp.bfloat16)
    hidden_grad = jnp.dot(upstream, down_mat.T, preferred_element_type=jnp.float32)
    silu_slope = sigmoid_val * (1.0 + gate_pre * (1.0 - sigmoid_val))
    gate_grad = (hidden_grad * up_pre * silu_slope).astype(jnp.bfloat16)
    up_grad = (hidden_grad * activated).astype(jnp.bfloat16)
    weight_grads = (
        jnp.dot(gate_grad.T, inputs, preferred_element_type=jnp.float32).astype(jnp.bfloat16)[None],
        jnp.dot(up_grad.T, inputs, preferred_element_type=jnp.float32).astype(jnp.bfloat16)[None],
        jnp.dot(hidden.T, upstream, preferred_element_type=jnp.float32).astype(jnp.bfloat16)[None],
    )
    partial_grad = jnp.dot(gate_grad, gate_mat, preferred_element_type=jnp.float32)
    partial_grad = partial_grad + jnp.dot(up_grad, up_mat, preferred_element_type=jnp.float32)
    return (weight_grads, partial_grad)


def routed_local(tokens, cotangent, gate_values, expert_ids, packing, w_gate, w_up, w_down):
    row_count, top_count = expert_ids.shape
    model_width = tokens.shape[1]
    dp_size = lax.axis_size("dp")
    expert_count = lax.axis_size("expert") * w_gate.shape[0]
    capacity = min(row_count, max(2, row_count * top_count // expert_count + 1))
    gate_mat = w_gate[0]
    up_mat = w_up[0]
    down_mat = w_down[0]
    pooled_rows, pooled_upstream, pooled_gates = (
        lax.all_gather(tokens, "dp", axis=0, tiled=True),
        lax.all_gather(cotangent, "dp", axis=0, tiled=True),
        lax.all_gather(gate_values, "dp", axis=0, tiled=True),
    )
    lists_all, pooled_ids = (
        lax.all_gather(packing, "dp", axis=0, tiled=True),
        lax.all_gather(expert_ids, "dp", axis=0, tiled=True),
    )
    member_rows = []
    member_upstream = []
    member_positions = []
    for member in range(dp_size):
        low = member * row_count
        slot_lists = lists_all[low : low + row_count]
        position, occupied, slot_row, slot_gate = slot_table(
            pooled_ids[low : low + row_count],
            pooled_gates[low : low + row_count],
            expert_count,
            capacity,
        )
        send_rows, send_upstream = fill_slots(
            pick_rows(slot_lists, pooled_rows),
            pick_rows(slot_lists, pooled_upstream),
            occupied,
            slot_row,
            slot_gate,
        )
        member_rows.append(send_rows.reshape(expert_count, capacity * model_width))
        member_upstream.append(send_upstream.reshape(expert_count, capacity * model_width))
        member_positions.append(position)
    own_position = jnp.stack(member_positions)[lax.axis_index("dp")]
    send_rows = jnp.concatenate(member_rows, axis=1).reshape(
        expert_count * dp_size * capacity, model_width
    )
    send_upstream = jnp.concatenate(member_upstream, axis=1).reshape(
        expert_count * dp_size * capacity, model_width
    )
    recv_rows, recv_upstream = (
        lax.all_to_all(send_rows, "expert", split_axis=0, concat_axis=0, tiled=True),
        lax.all_to_all(send_upstream, "expert", split_axis=0, concat_axis=0, tiled=True),
    )
    weight_grads, partial_grad = expert_terms(recv_rows, recv_upstream, gate_mat, up_mat, down_mat)
    summed = lax.psum_scatter(
        partial_grad.reshape(expert_count, dp_size * capacity * model_width).astype(jnp.bfloat16),
        "dp",
        scatter_dimension=1,
        tiled=True,
    ).astype(jnp.float32)
    slot_grad = summed.reshape(expert_count * capacity, model_width).astype(jnp.bfloat16)
    returned = lax.all_to_all(slot_grad, "expert", split_axis=0, concat_axis=0, tiled=True)
    rebal_grad = jnp.sum(returned[own_position].astype(jnp.float32), axis=1).astype(jnp.bfloat16)
    pooled_grad = lax.all_gather(rebal_grad, "dp", axis=0, tiled=True)
    home_index = lax.axis_index("dp") * row_count + jnp.arange(row_count, dtype=jnp.int32)
    choose = (lists_all[None, :] == home_index[:, None]).astype(jnp.bfloat16)
    input_grad = jnp.dot(choose, pooled_grad, preferred_element_type=jnp.float32).astype(
        jnp.bfloat16
    )
    return (input_grad, weight_grads[0], weight_grads[1], weight_grads[2])


def swap(value):
    return lax.ppermute(value, "dp", [(0, 1), (1, 0)])


def shift_outer(value, count, inner, step):
    return lax.ppermute(
        value, "expert", [(place, (place + step * inner) % count) for place in range(count)]
    )


def swap_inner(value, count, partner):
    return lax.ppermute(value, "expert", [(place, place ^ partner) for place in range(count)])


VMEM = pl.BlockSpec(memory_space=pltpu.VMEM)
ANY = pl.BlockSpec(memory_space=pl.ANY)
NT = (((1,), (1,)), ((), ()))
TN = (((0,), (0,)), ((), ()))


def on_chip(body, outs, *args, scratch=(), spec=VMEM, limit=True):
    moved = sum(arg.size * arg.dtype.itemsize for arg in args)
    moved += sum(math.prod(shape) * jnp.dtype(dtype).itemsize for shape, dtype in outs)
    granted = {"vmem_limit_bytes": moved + (4 << 20)} if limit else {}
    return pl.pallas_call(
        body,
        out_shape=[jax.ShapeDtypeStruct(shape, dtype) for shape, dtype in outs],
        in_specs=[spec] * len(args),
        out_specs=[VMEM] * len(outs),
        scratch_shapes=list(scratch),
        compiler_params=pltpu.CompilerParams(**granted),
        cost_estimate=pl.CostEstimate(flops=0, bytes_accessed=moved, transcendentals=0),
    )(*args)


def read_kernel(
    ids_hbm, gates_hbm, packing_hbm, tokens_hbm, cotangent_hbm,
    table_ref, tokens_ref, cotangent_ref,
    ids_ref, gates_ref, packing_ref, ready,
):
    pairs = [
        (ids_hbm, ids_ref),
        (gates_hbm, gates_ref),
        (packing_hbm, packing_ref),
        (tokens_hbm, tokens_ref),
        (cotangent_hbm, cotangent_ref),
    ]
    copies = [
        pltpu.make_async_copy(source, target, ready.at[index])
        for index, (source, target) in enumerate(pairs)
    ]
    for copy in copies:
        copy.start()
    for copy in copies:
        copy.wait()
    slots = packing_ref.shape[1]
    count = table_ref.shape[0] - 16
    labels = lax.broadcasted_iota(jnp.int32, (count, slots), 0)
    total = jnp.zeros((count, slots), jnp.float32)
    for k in range(ids_ref.shape[0]):
        named = labels == ids_ref[k : k + 1, :]
        total = total + jnp.where(named, gates_ref[k : k + 1, :].astype(jnp.float32), 0.0)
    table_ref[:count, :] = total.astype(jnp.bfloat16)
    lists = jnp.broadcast_to(packing_ref[...], (16, slots)).astype(jnp.float32)
    table_ref[count:, :] = lists.astype(jnp.bfloat16)


def payload_kernel(table_ref, other_ref, cotangent_ref, payload_ref, here_ref):
    rows, width = cotangent_ref.shape
    count = table_ref.shape[0] - 16
    slots = table_ref.shape[1]
    homes = lax.broadcasted_iota(jnp.int32, (rows, slots), 0) + lax.axis_index("dp") * rows
    gates = jnp.zeros((rows, count), jnp.float32)
    for ref in (table_ref, other_ref):
        lists = ref[count:, :].astype(jnp.float32)[:1, :]
        matched = (lists == homes.astype(jnp.float32)).astype(jnp.float32).astype(jnp.bfloat16)
        gates = gates + lax.dot_general(
            matched, ref[:count, :], NT, preferred_element_type=jnp.float32
        )
    payload_ref[:, :width] = cotangent_ref[...]
    payload_ref[:, width:] = gates.astype(jnp.bfloat16)
    lanes = lax.broadcasted_iota(jnp.int32, here_ref.shape, 1)
    here_ref[...] = (lanes == lax.axis_index("expert")).astype(jnp.float32)


def weight_kernel(own_grads, other_grads, rows, other_rows, upstream, other_upstream, *outs):
    half = outs[0].shape[1]
    for index, out in enumerate(outs):
        own, other = (upstream, other_upstream) if index == 2 else (rows, other_rows)
        span = slice(index * half, (index + 1) * half)
        step = min(out.shape[-1], 1024)
        for left in range(0, out.shape[-1], step):
            columns = slice(left, left + step)
            total = lax.dot_general(
                own_grads[:, span], own[:, columns], TN, preferred_element_type=jnp.float32
            ) + lax.dot_general(
                other_grads[:, span], other[:, columns], TN, preferred_element_type=jnp.float32
            )
            out[0, :, columns] = total.astype(jnp.bfloat16)


def join_kernel(own_ref, other_ref, gate_up_ref, down_ref):
    half = own_ref.shape[0] // 3
    for index, ref in enumerate((own_ref, other_ref)):
        for kind in range(2):
            low = (2 * kind + index) * half
            gate_up_ref[low : low + half, :] = ref[kind * half : (kind + 1) * half, :]
        down_ref[index * half : (index + 1) * half, :] = ref[2 * half :, :]


def pair_kernel(left_ref, right_ref, other_left_ref, other_right_ref, sum_ref, other_sum_ref):
    for one, two, out in (
        (left_ref, right_ref, sum_ref),
        (other_left_ref, other_right_ref, other_sum_ref),
    ):
        total = one[...].astype(jnp.float32) + two[...].astype(jnp.float32)
        out[...] = total.astype(out.dtype)


def along_outer(value, count, inner):
    return [value] + [shift_outer(value, count, inner, step) for step in range(1, count // inner)]


def across_inner(column, count, inner):
    if inner < 4:
        return [column] + [swap_inner(column, count, partner) for partner in range(1, inner)]
    cut = column.shape[0] // 2
    first = swap_inner(column, count, 1)
    second = swap_inner(column, count, 2)
    far_top = swap_inner(first[:cut], count, 2)
    far_bottom = swap_inner(second[cut:], count, 1)
    return [column, first, second, far_top, far_bottom]


def return_inner(near, far, count):
    own, first, second = jnp.split(near, 3, axis=0)
    cut = own.shape[0] // 2
    top = swap_inner(far[:cut], count, 2)
    bottom = swap_inner(far[cut:], count, 1)
    first_bottom = swap_inner(first[cut:], count, 1)
    second_top = swap_inner(second[:cut], count, 2)
    sent_first, sent_second = on_chip(
        pair_kernel, [(top.shape, top.dtype)] * 2, first[:cut], top, second[cut:], bottom
    )
    first_top = swap_inner(sent_first, count, 1)
    second_bottom = swap_inner(sent_second, count, 2)
    total = own.astype(jnp.float32)
    for upper, lower in ((first_top, first_bottom), (second_top, second_bottom)):
        total = total + jnp.concatenate([upper, lower], axis=0).astype(jnp.float32)
    return total


def return_outer(value, count, inner):
    outer = count // inner
    blocks = value.reshape(outer, -1, value.shape[-1])
    rounded = blocks.astype(jnp.bfloat16)
    total = blocks[0]
    for step in sorted(range(1, outer), key=lambda step: step != outer // 2):
        total = total + shift_outer(rounded[step], count, inner, -step).astype(jnp.float32)
    return total.astype(jnp.bfloat16)


def dense_local(tokens, cotangent, gate_values, expert_ids, packing, w_gate, w_up, w_down):
    model_width = tokens.shape[1]
    half = w_gate.shape[1]
    count = lax.axis_size("expert")
    inner = 4
    row_count = tokens.shape[0]
    low = jnp.bfloat16
    ids, gates, lists = expert_ids.T, gate_values.T, packing.reshape(1, row_count)
    token_blocks = along_outer(tokens, count, inner)
    table, own_tokens, own_cotangent = on_chip(
        read_kernel,
        [
            ((count + 16, row_count), low),
            (tokens.shape, low),
            (cotangent.shape, low),
        ],
        ids,
        gates,
        lists,
        tokens,
        cotangent,
        spec=ANY,
        limit=False,
        scratch=[
            pltpu.VMEM(ids.shape, ids.dtype),
            pltpu.VMEM(gates.shape, gates.dtype),
            pltpu.VMEM(lists.shape, lists.dtype),
            pltpu.SemaphoreType.DMA((5,)),
        ],
    )
    payload, here = on_chip(
        payload_kernel,
        [((row_count, model_width + count), low), ((8, count), jnp.float32)],
        table,
        swap(table),
        own_cotangent,
    )
    token_column = jnp.concatenate([own_tokens, *token_blocks[1:]], axis=0)
    early = shift_outer(payload, count, inner, 2)
    payload, token_column = lax.optimization_barrier((payload, token_column))
    upstream_blocks = [payload, shift_outer(payload, count, inner, 1), early]
    upstream_blocks.append(shift_outer(payload, count, inner, 3))
    upstream_column = jnp.concatenate(upstream_blocks, axis=0)
    token_columns = across_inner(token_column, count, inner)
    own_weights = jnp.concatenate([w_gate[0], w_up[0], w_down[0]], axis=0)
    sent_weights, token_columns[1] = lax.optimization_barrier((own_weights, token_columns[1]))
    other = swap(sent_weights)
    inputs = jnp.concatenate(token_columns, axis=0)
    other_inputs = swap(inputs)
    upstream = jnp.concatenate(across_inner(upstream_column, count, inner), axis=0)
    gate = jnp.sum(
        upstream[:, model_width:].astype(jnp.float32) * here[:1], axis=1, keepdims=True
    )
    upstream = upstream[:, :model_width]
    gate_up, down = on_chip(
        join_kernel,
        [((4 * half, model_width), low), ((2 * half, model_width), low)],
        own_weights,
        other,
    )
    pre = jnp.dot(inputs, gate_up.T, preferred_element_type=jnp.float32)
    gate_pre, up_pre = pre[:, : 2 * half], pre[:, 2 * half :]
    hidden_grad = gate * jnp.dot(upstream, down.T, preferred_element_type=jnp.float32)
    sigmoid_val = jax.nn.sigmoid(gate_pre)
    activated = gate_pre * sigmoid_val
    hidden = (gate * activated * up_pre).astype(jnp.bfloat16)
    silu_slope = sigmoid_val * (1.0 + gate_pre * (1.0 - sigmoid_val))
    gate_grad = (hidden_grad * up_pre * silu_slope).astype(jnp.bfloat16)
    up_grad = (hidden_grad * activated).astype(jnp.bfloat16)
    both_grad = jnp.concatenate([gate_grad, up_grad], axis=1)
    cut = both_grad.shape[0] // inner * (inner - 1)
    far = jnp.dot(both_grad[cut:], gate_up, preferred_element_type=jnp.float32)
    far = far.astype(jnp.bfloat16)
    near_grad, far = lax.optimization_barrier((both_grad[:cut], far))
    near = jnp.dot(near_grad, gate_up, preferred_element_type=jnp.float32)
    near = near.astype(jnp.bfloat16)
    far, other_inputs = lax.optimization_barrier((far, other_inputs))
    column_sum = return_inner(near, far, count)
    grads = (gate_grad, up_grad, hidden)
    own_grads = jnp.concatenate([grad[:, :half] for grad in grads], axis=1)
    sent_grads = jnp.concatenate([grad[:, half:] for grad in grads], axis=1)
    sent_grads, upstream, _ = lax.optimization_barrier((sent_grads, upstream, near))
    other_grads = swap(sent_grads)
    other_upstream = swap(upstream)
    column_sum, other_grads, other_upstream = lax.optimization_barrier(
        (column_sum, other_grads, other_upstream)
    )
    input_grad = return_outer(column_sum, count, inner)
    weight_grads = on_chip(
        weight_kernel,
        [((1, half, model_width), low)] * 3,
        own_grads,
        other_grads,
        inputs,
        other_inputs,
        upstream,
        other_upstream,
    )
    return (input_grad, *weight_grads)


def local(tokens, cotangent, gate_values, expert_ids, packing, w_gate, w_up, w_down):
    row_count, top = expert_ids.shape
    count = lax.axis_size("expert")
    expert_count = count * w_gate.shape[0]
    capacity = min(row_count, max(2, row_count * top // expert_count + 1))
    few = capacity * 4 <= row_count
    regular = lax.axis_size("dp") == 2 and count % 4 == 0 and w_gate.shape[0] == 1
    chosen = dense_local if regular and not few else routed_local
    return chosen(
        tokens, cotangent, gate_values, expert_ids, packing, w_gate, w_up, w_down
    )


def solution(mesh):
    in_specs = (
        P(("groups", "dp", "expert"), None),
        P(("groups", "dp", "expert"), None),
        P(("groups", "dp", "expert"), None),
        P(("groups", "dp", "expert"), None),
        P(("groups", "dp", "expert")),
        P("expert", "dp", None),
        P("expert", "dp", None),
        P("expert", "dp", None),
    )
    out_specs = (
        P(("groups", "dp", "expert"), None),
        P(("groups", "expert"), "dp", None),
        P(("groups", "expert"), "dp", None),
        P(("groups", "expert"), "dp", None),
    )
    return jax.shard_map(local, mesh=mesh, in_specs=in_specs, out_specs=out_specs, check_vma=False)
```
